32 devices in a mesh: seq: 8 (over z, x), vocab: 4 (over y, core).
Axes of the slice: x: 2, y: 2, z: 4, core: 2. Of those that a mesh axis runs over, the one named last changes fastest.
Arguments:
- hidden: bfloat16 [64, 5120], P(('seq', 'vocab')), may hold values from -400 to 400
- norm_gain: float32 [5120], replicated, may hold values from 0.1 to 1.9
- head_weight: bfloat16 [5120, 16384], P(None, ('seq', 'vocab')), may hold values from -2 to 2
- teacher_logits: bfloat16 [128, 8, 2048], P('seq', None, 'vocab'), may hold values from -12 to 300
- teacher_slot: int32 [64], replicated, may hold values from 0 to 127, as said below
- valid_tokens: int32 [64], replicated, may hold values 0 or 1
Outputs:
- grad_hidden: bfloat16 [64, 5120], P(('seq', 'vocab'))
- grad_head: bfloat16 [5120, 16384], P(None, ('seq', 'vocab'))
The draws below stay inside these ranges and needn't reach their ends.
Inputs may be any that keep to these rules, and one draw needn't show every extreme that they name: `teacher_slot`: rows use distinct slots; slots g * 16 to (g + 1) * 16 - 1 belong to sequence group g of the teacher's packing; at most 16 rows use one group's slots, and some group holds 16 in every draw.
All inputs are finite; a program needn't handle non-finite values.
Results may differ from the reference program's by a relative error of at most 0.02.
Values may be sent and summed in bfloat16 or wider, within the bound.
No kernel may reach another device: no remote copies, remote signals or barrier semaphores. Data moves between devices by JAX's collectives and lax.ppermute only.
A program may use at most 128 MiB of HBM per device.

```python
import math
import jax
import jax.numpy as jnp
from jax import lax

D = 5120
ROWS = 64
VSPAN = 2048
VOCAB = 16384
TCAP = 16
N_SEQ = 8


def slot_map(key):
    key_group, key_order, key_within, key_others = jax.random.split(jax.random.fold_in(key, 31), 4)
    full_group = jax.random.randint(key_group, (), 0, N_SEQ)
    row_order = jax.random.permutation(key_order, ROWS)
    within = jax.random.permutation(key_within, TCAP)
    others = jax.random.permutation(key_others, (N_SEQ - 1) * TCAP)
    ranks = jnp.arange(ROWS, dtype=jnp.int32)
    full_part = full_group * TCAP + within[jnp.minimum(ranks, TCAP - 1)]
    other_index = others[jnp.clip(ranks - TCAP, 0, (N_SEQ - 1) * TCAP - 1)]
    other_part = (other_index // TCAP + full_group + 1) % N_SEQ * TCAP + other_index % TCAP
    by_rank = jnp.where(ranks < TCAP, full_part, other_part).astype(jnp.int32)
    return jnp.zeros((ROWS,), jnp.int32).at[row_order].set(by_rank)


def draw_teacher_slot(key, part):
    return slot_map(key)


def draw_hidden(key, part):
    key_base, key_row, key_column = jax.random.split(jax.random.fold_in(key, 11), 3)
    row_scale = jnp.exp(jax.random.uniform(key_row, (ROWS, 1), jnp.float32, 0.0, math.log(10.0)))
    column_scale = jnp.exp(jax.random.uniform(key_column, (1, D), jnp.float32, 0.0, math.log(10.0)))
    base_draw = jnp.clip(jax.random.normal(key_base, (ROWS, D), jnp.float32), -4.0, 4.0)
    values = base_draw * row_scale * column_scale
    return values.astype(jnp.bfloat16)


def draw_head_weight(key, part):
    key_main = jax.random.fold_in(key, 41)
    spread = 3.0 / math.sqrt(D)
    values = jnp.clip(jax.random.normal(key_main, (D, VOCAB), jnp.float32), -4.0, 4.0) * spread
    return values.astype(jnp.bfloat16)


def draw_teacher_logits(key, part):
    key_main = jax.random.fold_in(key, 23)
    draw_shape = (N_SEQ * TCAP, N_SEQ, VSPAN)
    values = jnp.clip(jax.random.normal(key_main, draw_shape, jnp.float32), -4.0, 4.0) * 3.0
    return values.astype(jnp.bfloat16)


def touch_ends(result, key, low, largest):
    place = [jax.random.randint(jax.random.fold_in(key, axis), (), 0, length) for axis, length in enumerate(result.shape)]
    longest = result.shape.index(max(result.shape))
    neighbour = place[:longest] + [(place[longest] + 1) % result.shape[longest]] + place[longest + 1:]
    return result.at[tuple(place)].set(low).at[tuple(neighbour)].set(largest)


def setup_inputs(seed: int = 0) -> dict:
    streams_of = jax.random.split(jax.random.key(seed), 7)
    hidden = draw_hidden(jax.random.fold_in(streams_of[6], 71), 0)
    norm_gain = jnp.clip(1.0 + 0.18 * jax.random.normal(streams_of[1], (D,), jnp.float32), 0.1, 1.9)
    head_weight = draw_head_weight(jax.random.fold_in(streams_of[6], 71), 0)
    teacher_logits = draw_teacher_logits(jax.random.fold_in(streams_of[6], 71), 0)
    teacher_slot = draw_teacher_slot(jax.random.fold_in(streams_of[6], 71), 0)
    valid_tokens = touch_ends((jax.random.randint(streams_of[5], (ROWS,), 0, 4) < 3).astype(jnp.int32), jax.random.fold_in(streams_of[5], 1), 0, 1)
    return dict(hidden=hidden, norm_gain=norm_gain, head_weight=head_weight, teacher_logits=teacher_logits, teacher_slot=teacher_slot, valid_tokens=valid_tokens)


epsilon = 1e-06

def block_grad(features, vocab_block):
    return jnp.dot(features.T, vocab_block, preferred_element_type=jnp.float32).astype(jnp.bfloat16)

def partial_grad(features):

    def apply_block(vocab_block):
        return block_grad(features, vocab_block)
    return apply_block

def reference(hidden, norm_gain, head_weight, teacher_logits, teacher_slot, valid_tokens):
    widened = hidden.astype(jnp.float32)
    inv_rms = lax.rsqrt(lax.optimization_barrier(jnp.mean(widened * widened, axis=1, keepdims=True)) + epsilon)
    normed = widened * inv_rms
    features = (normed * norm_gain).astype(jnp.bfloat16)
    logits = jnp.dot(features, head_weight, preferred_element_type=jnp.float32)
    slot_table = teacher_logits.reshape(N_SEQ * TCAP, VOCAB)
    teacher = jnp.take(slot_table, teacher_slot.astype(jnp.int32), axis=0).astype(jnp.float32)
    student_top = lax.optimization_barrier(jnp.max(logits, axis=1, keepdims=True))
    teacher_top = lax.optimization_barrier(jnp.max(teacher, axis=1, keepdims=True))
    shifted = jnp.exp(logits - student_top)
    student_total = lax.optimization_barrier(jnp.sum(shifted, axis=1, keepdims=True))
    teacher_total = lax.optimization_barrier(jnp.sum(jnp.exp(teacher - teacher_top), axis=1, keepdims=True))
    cross_sum = lax.optimization_barrier(jnp.sum(shifted * (logits - teacher), axis=1, keepdims=True))
    student_lse = student_top + jnp.log(student_total)
    teacher_lse = teacher_top + jnp.log(teacher_total)
    divergence = cross_sum / student_total - student_lse + teacher_lse
    student_prob = jnp.exp(logits - student_lse)
    log_gap = logits - student_lse - (teacher - teacher_lse)
    row_weight = valid_tokens.astype(jnp.float32)[:, None]
    logit_grad = (row_weight * student_prob * (log_gap - divergence)).astype(jnp.bfloat16)
    vocab_blocks = logit_grad.reshape(ROWS, N_SEQ, VSPAN).transpose(1, 0, 2)
    grad_blocks = lax.map(partial_grad(features), vocab_blocks)
    grad_head = grad_blocks.transpose(1, 0, 2).reshape(D, VOCAB)
    feature_grad = lax.dot_general(logit_grad, head_weight, (((1,), (1,)), ((), ())), preferred_element_type=jnp.float32)
    norm_grad = feature_grad * norm_gain
    grad_hidden = inv_rms * (norm_grad - normed * lax.optimization_barrier(jnp.mean(norm_grad * normed, axis=1, keepdims=True)))
    return (grad_hidden.astype(jnp.bfloat16), grad_head)
```

```python
import jax
import jax.numpy as jnp
from jax import lax
from jax.sharding import PartitionSpec as P

epsilon = 1e-06
axes = ("seq", "vocab")


def swap(value, mask, count):
    return lax.ppermute(value, axes, [(i, i ^ mask) for i in range(count)])


def merge(parts):
    top = jnp.max(jnp.stack([p[0] for p in parts]), axis=0)
    teacher_top = jnp.max(jnp.stack([p[3] for p in parts]), axis=0)
    total = cross = teacher_total = 0.0
    for p in parts:
        scale = jnp.exp(p[0] - top)
        total += p[1] * scale
        cross += p[2] * scale
        teacher_total += p[4] * jnp.exp(p[3] - teacher_top)
    return jnp.stack([top, total, cross, teacher_top, teacher_total])


def in_order(values, masks):
    bits = len(masks)
    split = values.reshape((2,) * bits + (-1,))
    return split.transpose([bits - m.bit_length() for m in reversed(masks)] + [bits]).reshape(-1)


def shards(masks, n_vocab, hidden, norm_gain, head_weight, teacher_logits, teacher_slot, valid_tokens):
    count = 1 << len(masks)
    me = lax.axis_index(axes)
    my_seq = lax.axis_index("seq")
    n_seq = count // n_vocab
    cap = teacher_logits.shape[0]

    widened = hidden.astype(jnp.float32)
    inv_rms = lax.rsqrt(jnp.mean(widened * widened, axis=1, keepdims=True) + epsilon)
    normed = widened * inv_rms
    gathered = (normed * norm_gain).astype(jnp.bfloat16)
    for mask in masks:
        arrived = swap(gathered, mask, count)
        high = (me & mask) != 0
        gathered = jnp.concatenate(
            [jnp.where(high, arrived, gathered), jnp.where(high, gathered, arrived)], axis=0
        )

    blocks = teacher_logits.transpose(1, 0, 2)
    pieces = [lax.dynamic_index_in_dim(blocks, my_seq, 0, keepdims=False)]
    for k in range(1, n_seq):
        piece = lax.dynamic_index_in_dim(blocks, my_seq ^ k, 0, keepdims=False)
        pieces.append(swap(piece, k * n_vocab, count))
    slot_table = jnp.concatenate(pieces, axis=0)

    slots = in_order(teacher_slot, masks)
    row_weight = in_order(valid_tokens, masks).astype(jnp.float32)[:, None]
    place = ((slots // cap) ^ my_seq) * cap + slots % cap
    pick = (place[:, None] == jnp.arange(n_seq * cap, dtype=jnp.int32)).astype(jnp.bfloat16)
    teacher = jnp.dot(pick, slot_table, preferred_element_type=jnp.float32)

    logits = jnp.dot(gathered, head_weight, preferred_element_type=jnp.float32)
    student_top = jnp.max(logits, axis=1)
    teacher_top = jnp.max(teacher, axis=1)
    shifted = jnp.exp(logits - student_top[:, None])
    stats = jnp.stack([
        student_top,
        jnp.sum(shifted, axis=1),
        jnp.sum(shifted * (logits - teacher), axis=1),
        teacher_top,
        jnp.sum(jnp.exp(teacher - teacher_top[:, None]), axis=1),
    ])
    stats = merge([stats] + [swap(stats, k, count) for k in range(1, n_vocab)])
    stats = merge([stats] + [swap(stats, k * n_vocab, count) for k in range(1, n_seq)])
    student_top, student_total, cross_sum, teacher_top, teacher_total = [s[:, None] for s in stats]

    student_lse = student_top + jnp.log(student_total)
    teacher_lse = teacher_top + jnp.log(teacher_total)
    divergence = cross_sum / student_total - student_lse + teacher_lse
    student_prob = jnp.exp(logits - student_lse)
    log_gap = logits - student_lse - (teacher - teacher_lse)
    logit_grad = (row_weight * student_prob * (log_gap - divergence)).astype(jnp.bfloat16)

    partial = lax.dot_general(
        logit_grad, head_weight, (((1,), (1,)), ((), ())), preferred_element_type=jnp.float32
    )
    for mask in reversed(masks):
        half = partial.shape[0] // 2
        high = (me & mask) != 0
        low_rows, high_rows = partial[:half], partial[half:]
        arrived = swap(jnp.where(high, low_rows, high_rows), mask, count)
        partial = jnp.where(high, high_rows, low_rows) + arrived
    grad_head = lax.dot_general(
        gathered, logit_grad, (((0,), (0,)), ((), ())), preferred_element_type=jnp.float32
    ).astype(jnp.bfloat16)
    norm_grad = partial * norm_gain
    grad_hidden = inv_rms * (
        norm_grad - normed * jnp.mean(norm_grad * normed, axis=1, keepdims=True)
    )
    return (grad_hidden.astype(jnp.bfloat16), grad_head)


def solution(mesh):
    n_seq, n_vocab = mesh.shape["seq"], mesh.shape["vocab"]
    count = n_seq * n_vocab
    bits = count.bit_length() - 1
    masks = [1 << b for b in reversed(range(bits))]
    placed = (
        P(axes, None),
        P(),
        P(None, axes),
        P("seq", None, "vocab"),
        P(),
        P(),
    )

    def local(*arrays):
        return shards(masks, n_vocab, *arrays)

    return jax.shard_map(
        local,
        mesh=mesh,
        in_specs=placed,
        out_specs=(P(axes, None), P(None, axes)),
        check_vma=False,
    )
```

```python
import jax
import jax.numpy as jnp
from jax import lax
from jax.sharding import PartitionSpec as P

epsilon = 1e-06
axes = ("seq", "vocab")


def swap(value, mask, count):
    return lax.ppermute(value, axes, [(i, i ^ mask) for i in range(count)])


def merge(parts):
    top = jnp.max(jnp.stack([p[0] for p in parts]), axis=0)
    teacher_top = jnp.max(jnp.stack([p[3] for p in parts]), axis=0)
    total = cross = teacher_total = 0.0
    for p in parts:
        scale = jnp.exp(p[0] - top)
        total += p[1] * scale
        cross += p[2] * scale
        teacher_total += p[4] * jnp.exp(p[3] - teacher_top)
    return jnp.stack([top, total, cross, teacher_top, teacher_total])


def halve(value, mask, axis, me, count):
    low, high = jnp.split(value, 2, axis=axis)
    up = (me & mask) != 0
    return jnp.where(up, high, low) + swap(jnp.where(up, low, high), mask, count)


def in_order(values, masks):
    bits = len(masks)
    split = values.reshape((2,) * bits + (-1,))
    return split.transpose([bits - m.bit_length() for m in reversed(masks)] + [bits]).reshape(-1)


def shards(masks, n_vocab, hidden, norm_gain, head_weight, teacher_logits, teacher_slot, valid_tokens):
    count = 1 << len(masks)
    me = lax.axis_index(axes)
    my_seq = lax.axis_index("seq")
    n_seq = count // n_vocab
    cap = teacher_logits.shape[0]

    widened = hidden.astype(jnp.float32)
    inv_rms = lax.rsqrt(jnp.mean(widened * widened, axis=1, keepdims=True) + epsilon)
    normed = widened * inv_rms
    gathered = (normed * norm_gain).astype(jnp.bfloat16)
    seq_masks = [m for m in reversed(masks) if m >= n_vocab]
    seq_bits = len(seq_masks)
    behind = len(masks) - seq_bits
    held = teacher_logits.transpose(1, 0, 2)
    for step, mask in enumerate(masks):
        arrived = swap(gathered, mask, count)
        high = (me & mask) != 0
        gathered = jnp.concatenate(
            [jnp.where(high, arrived, gathered), jnp.where(high, gathered, arrived)], axis=0
        )
        if step == 0 or step >= behind and step - behind + 1 < seq_bits:
            bit = 0 if step == 0 else step - behind + 1
            if step:
                held, _ = lax.optimization_barrier((held, before))
            pairs = held.reshape((held.shape[0] // 2, 2) + held.shape[1:])
            up = (me & seq_masks[bit]) != 0
            keep = jnp.where(up, pairs[:, 1], pairs[:, 0])
            send = jnp.where(up, pairs[:, 0], pairs[:, 1])
            held = jnp.concatenate([keep, swap(send, seq_masks[bit], count)], axis=1)
        before = gathered
    slot_table = held[0]

    slots = in_order(teacher_slot, masks)
    row_weight = in_order(valid_tokens, masks).astype(jnp.float32)[:, None]
    place = ((slots // cap) ^ my_seq) * cap + slots % cap
    pick = (place[:, None] == jnp.arange(n_seq * cap, dtype=jnp.int32)).astype(jnp.bfloat16)
    teacher = jnp.dot(pick, slot_table, preferred_element_type=jnp.float32)

    logits = jnp.dot(gathered, head_weight, preferred_element_type=jnp.float32)
    student_top = jnp.max(logits, axis=1)
    teacher_top = jnp.max(teacher, axis=1)
    shifted = jnp.exp(logits - student_top[:, None])
    stats = jnp.stack([
        student_top,
        jnp.sum(shifted, axis=1),
        jnp.sum(shifted * (logits - teacher), axis=1),
        teacher_top,
        jnp.sum(jnp.exp(teacher - teacher_top[:, None]), axis=1),
    ])
    for mask in reversed(masks):
        stats = merge([stats, swap(stats, mask, count)])
    student_top, student_total, cross_sum, teacher_top, teacher_total = [s[:, None] for s in stats]

    student_lse = student_top + jnp.log(student_total)
    teacher_lse = teacher_top + jnp.log(teacher_total)
    divergence = cross_sum / student_total - student_lse + teacher_lse
    student_prob = jnp.exp(logits - student_lse)
    log_gap = logits - student_lse - (teacher - teacher_lse)
    logit_grad = (row_weight * student_prob * (log_gap - divergence)).astype(jnp.bfloat16)

    partial = lax.dot_general(
        logit_grad, head_weight, (((1,), (1,)), ((), ())), preferred_element_type=jnp.float32
    )
    order = list(reversed(masks))
    partial = halve(partial, order[0], 0, me, count)
    split = len(order) > 2
    if split:
        columns = partial.shape[1] // 2
        rows = partial.shape[0] // 4
        left = partial[:, :columns]
        right = partial[:, columns:].reshape(2, 2, rows, columns)
        left = halve(left, order[1], 0, me, count)
        right = halve(right, order[2], 1, me, count)
        left = halve(left, order[2], 0, me, count)
        right = halve(right, order[1], 0, me, count).reshape(rows, columns)
        partial = jnp.concatenate([left, right], axis=1)
    for mask in order[3 if split else 1:]:
        partial = halve(partial, mask, 0, me, count)
    grad_head = lax.dot_general(
        gathered, logit_grad, (((0,), (0,)), ((), ())), preferred_element_type=jnp.float32
    ).astype(jnp.bfloat16)
    norm_grad = partial * norm_gain
    grad_hidden = inv_rms * (
        norm_grad - normed * jnp.mean(norm_grad * normed, axis=1, keepdims=True)
    )
    return (grad_hidden.astype(jnp.bfloat16), grad_head)


def solution(mesh):
    n_seq, n_vocab = mesh.shape["seq"], mesh.shape["vocab"]
    count = n_seq * n_vocab
    bits = count.bit_length() - 1
    masks = [1 << b for b in reversed(range(bits))]
    placed = (
        P(axes, None),
        P(),
        P(None, axes),
        P("seq", None, "vocab"),
        P(),
        P(),
    )

    def local(*arrays):
        return shards(masks, n_vocab, *arrays)

    return jax.shard_map(
        local,
        mesh=mesh,
        in_specs=placed,
        out_specs=(P(axes, None), P(None, axes)),
        check_vma=False,
    )
```

```python
import math

import jax
import jax.numpy as jnp
from jax import lax
from jax.experimental import pallas as pl
from jax.experimental.pallas import tpu as pltpu
from jax.sharding import PartitionSpec as P

epsilon = 1e-06
axes = ("seq", "vocab")


def swap(value, mask, count):
    return lax.ppermute(value, axes, [(i, i ^ mask) for i in range(count)])


def call(kernel, out_shape, scratch, flops, inputs, spaces, out_spaces, name):
    def size(leaf):
        return leaf.size * leaf.dtype.itemsize

    outs = list(out_shape)
    fast = sum(size(x) for x, s in zip(inputs, spaces) if s == pltpu.VMEM)
    fast += sum(size(x) for x, s in zip(outs, out_spaces) if s == pltpu.VMEM)
    held = sum(math.prod(x.shape) * x.dtype.itemsize for x in scratch if x.memory_space == pltpu.VMEM)
    return pl.pallas_call(
        kernel,
        out_shape=outs,
        in_specs=[pl.BlockSpec(memory_space=s) for s in spaces],
        out_specs=[pl.BlockSpec(memory_space=s) for s in out_spaces],
        scratch_shapes=scratch,
        compiler_params=pltpu.CompilerParams(vmem_limit_bytes=2 * fast + held + (8 << 20)),
        cost_estimate=pl.CostEstimate(
            flops=flops, bytes_accessed=sum(map(size, list(inputs) + outs)), transcendentals=0
        ),
        name=name,
    )(*inputs)


def split_evenly(total, unit):
    parts = max(p for p in (1, 2, 4, 5) if total % (p * unit) == 0)
    return parts, total // parts


def logits_kernel(gathered_ref, weight_ref, table_ref, place_ref, logits_ref, teacher_ref, stats_ref, held, sems):
    depth = weight_ref.shape[0]
    parts, size = split_evenly(depth, 256)
    rows = gathered_ref.shape[0]
    copies = []
    for p in range(parts):
        block = pl.ds(p * size, size)
        copies.append(pltpu.make_async_copy(weight_ref.at[block], held.at[block], sems.at[p]))
        copies[-1].start()
    slots = lax.broadcasted_iota(jnp.int32, (rows, table_ref.shape[0]), 1)
    pick = (place_ref[...] == slots).astype(jnp.bfloat16)
    teacher = jnp.dot(pick, table_ref[...], preferred_element_type=jnp.float32)
    teacher_ref[...] = teacher
    teacher_top = jnp.max(teacher, axis=1, keepdims=True)
    teacher_total = jnp.sum(jnp.exp(teacher - teacher_top), axis=1, keepdims=True)
    logits = jnp.zeros(logits_ref.shape, jnp.float32)
    for p in range(parts):
        copies[p].wait()
        logits += jnp.dot(
            gathered_ref[:, p * size : (p + 1) * size],
            held[p * size : (p + 1) * size, :],
            preferred_element_type=jnp.float32,
        )
    logits_ref[...] = logits
    student_top = jnp.max(logits, axis=1, keepdims=True)
    shifted = jnp.exp(logits - student_top)
    student_total = jnp.sum(shifted, axis=1, keepdims=True)
    cross_sum = jnp.sum(shifted * (logits - teacher), axis=1, keepdims=True)
    tops = jnp.concatenate([student_top, teacher_top], axis=0)
    totals = jnp.concatenate([student_total, teacher_total], axis=0)
    crosses = jnp.concatenate([cross_sum, jnp.zeros_like(cross_sum)], axis=0)
    lane = lax.broadcasted_iota(jnp.int32, (2 * rows, 128), 1)
    table = jnp.where(lane == 0, tops, jnp.where(lane == 1, totals, jnp.where(lane == 2, crosses, 0.0)))
    stats = table.T[:4]
    for p in range(stats_ref.shape[0]):
        stats_ref[p] = stats


def grad_rows(logits, teacher, stats, row_weight):
    rows = logits.shape[0]
    tops, totals, crosses = stats[:, 0, :], stats[:, 1, :], stats[:, 2, :]
    top = jnp.max(tops, axis=0, keepdims=True)
    scale = jnp.exp(tops - top)
    total = jnp.sum(totals * scale, axis=0, keepdims=True)
    cross = jnp.sum(crosses * scale, axis=0, keepdims=True)
    table = jnp.concatenate([top, total, cross, jnp.zeros((125, 2 * rows), jnp.float32)], axis=0).T
    student_top, teacher_top = table[:rows, 0:1], table[rows:, 0:1]
    student_total, teacher_total = table[:rows, 1:2], table[rows:, 1:2]
    cross_sum = table[:rows, 2:3]
    student_lse = student_top + jnp.log(student_total)
    teacher_lse = teacher_top + jnp.log(teacher_total)
    divergence = cross_sum / student_total - student_lse + teacher_lse
    log_prob = logits - student_lse
    log_gap = log_prob - (teacher - teacher_lse)
    return (row_weight * jnp.exp(log_prob) * (log_gap - divergence)).astype(jnp.bfloat16)


def back(grad, weight_copies, held, keep_ref, send_ref, size):
    half = grad.shape[0] // 2
    up = (lax.axis_index("vocab") & 1) != 0
    low, high = grad[:half], grad[half:]
    chosen = jnp.concatenate([jnp.where(up, high, low), jnp.where(up, low, high)], axis=0)
    for p, copy in enumerate(weight_copies):
        copy.wait()
        block = lax.dot_general(
            chosen,
            held[p * size : (p + 1) * size, :],
            (((1,), (1,)), ((), ())),
            preferred_element_type=jnp.float32,
        )
        keep_ref[:, p * size : (p + 1) * size] = block[:half]
        send_ref[:, p * size : (p + 1) * size] = block[half:]


def start_copies(weight_ref, held, sems, first):
    columns = held.shape[0]
    parts, size = split_evenly(columns, 256)
    copies = []
    for p in range(parts):
        source = weight_ref.at[pl.ds(first + p * size, size)]
        copies.append(pltpu.make_async_copy(source, held.at[pl.ds(p * size, size)], sems.at[p]))
        copies[-1].start()
    return copies, size


def left_kernel(logits_ref, teacher_ref, stats_ref, valid_ref, weight_ref, grad_ref, keep_ref, send_ref, held, sems):
    copies, size = start_copies(weight_ref, held, sems, 0)
    grad = grad_rows(logits_ref[...], teacher_ref[...], stats_ref[...], valid_ref[...])
    grad_ref[...] = grad
    back(grad, copies, held, keep_ref, send_ref, size)


def right_kernel(grad_ref, weight_ref, keep_ref, send_ref, held, sems):
    copies, size = start_copies(weight_ref, held, sems, held.shape[0])
    back(grad_ref[...], copies, held, keep_ref, send_ref, size)


def head_kernel(gathered_ref, grad_ref, out_ref, held, sems):
    parts, size = split_evenly(out_ref.shape[0], 256)
    grad = grad_ref[...]
    copies = []
    for p in range(parts):
        block = pl.ds(p * size, size)
        held[p * size : (p + 1) * size, :] = lax.dot_general(
            gathered_ref[:, p * size : (p + 1) * size],
            grad,
            (((0,), (0,)), ((), ())),
            preferred_element_type=jnp.float32,
        ).astype(jnp.bfloat16)
        copies.append(pltpu.make_async_copy(held.at[block], out_ref.at[block], sems.at[p]))
        copies[-1].start()
    for copy in copies:
        copy.wait()


def norm_kernel(hidden_ref, gain_ref, features_ref):
    widened = hidden_ref[...].astype(jnp.float32)
    inv_rms = lax.rsqrt(jnp.mean(widened * widened, axis=1, keepdims=True) + epsilon)
    features_ref[...] = (widened * inv_rms * gain_ref[...]).astype(jnp.bfloat16)


def halve(value, mask, axis, me, count):
    low, high = jnp.split(value, 2, axis=axis)
    up = (me & mask) != 0
    return jnp.where(up, high, low) + swap(jnp.where(up, low, high), mask, count)


def in_order(values, masks):
    bits = len(masks)
    split = values.reshape((2,) * bits + (-1,))
    return split.transpose([bits - m.bit_length() for m in reversed(masks)] + [bits]).reshape(-1)


def shards(masks, n_vocab, hidden, norm_gain, head_weight, teacher_logits, teacher_slot, valid_tokens):
    count = 1 << len(masks)
    me = lax.axis_index(axes)
    my_seq = lax.axis_index("seq")
    n_seq = count // n_vocab
    cap = teacher_logits.shape[0]
    depth, width = head_weight.shape
    rows = hidden.shape[0] * count
    shape, fast = jax.ShapeDtypeStruct, pltpu.VMEM

    widened = hidden.astype(jnp.float32)
    inv_rms = lax.rsqrt(jnp.mean(widened * widened, axis=1, keepdims=True) + epsilon)
    normed = widened * inv_rms
    (gathered,) = call(
        norm_kernel, [shape(hidden.shape, jnp.bfloat16)], [], 0, [hidden, norm_gain[None]], [fast] * 2, [fast], "features"
    )
    seq_masks = [m for m in reversed(masks) if m >= n_vocab]
    seq_bits = len(seq_masks)
    behind = len(masks) - seq_bits
    held = teacher_logits.transpose(1, 0, 2)
    for step, mask in enumerate(masks):
        arrived = swap(gathered, mask, count)
        high = (me & mask) != 0
        gathered = jnp.concatenate(
            [jnp.where(high, arrived, gathered), jnp.where(high, gathered, arrived)], axis=0
        )
        if step == 0 or step >= behind and step - behind + 1 < seq_bits:
            bit = 0 if step == 0 else step - behind + 1
            if step:
                held, _ = lax.optimization_barrier((held, before))
            pairs = held.reshape((held.shape[0] // 2, 2) + held.shape[1:])
            up = (me & seq_masks[bit]) != 0
            keep = jnp.where(up, pairs[:, 1], pairs[:, 0])
            send = jnp.where(up, pairs[:, 0], pairs[:, 1])
            held = jnp.concatenate([keep, swap(send, seq_masks[bit], count)], axis=1)
        before = gathered
    slot_table = held[0]

    slots = in_order(teacher_slot, masks)
    row_weight = in_order(valid_tokens, masks).astype(jnp.float32)[:, None]
    place = ((slots // cap) ^ my_seq) * cap + slots % cap

    sems = pltpu.SemaphoreType.DMA((5,))
    logits, teacher, stats = call(
        logits_kernel,
        [shape((rows, width), jnp.float32)] * 2 + [shape((count, 4, 2 * rows), jnp.float32)],
        [pltpu.VMEM((depth, width), jnp.bfloat16), sems],
        2 * rows * depth * width,
        [gathered, head_weight, slot_table, place[:, None]],
        [fast, pl.ANY, fast, fast],
        [fast] * 3,
        "logits",
    )
    stats = lax.all_to_all(stats, axes, split_axis=0, concat_axis=0, tiled=True)
    columns = depth // 2
    halves = [shape((rows // 2, columns), jnp.float32)] * 2
    half_weight = [pltpu.VMEM((columns, width), jnp.bfloat16), sems]
    logit_grad, left, left_out = call(
        left_kernel,
        [shape((rows, width), jnp.bfloat16)] + halves,
        half_weight,
        2 * rows * columns * width,
        [logits, teacher, stats, row_weight, head_weight],
        [fast] * 4 + [pl.ANY],
        [fast] * 3,
        "left",
    )
    right, right_out = call(
        right_kernel,
        halves,
        half_weight,
        2 * rows * columns * width,
        [logit_grad, head_weight],
        [fast, pl.ANY],
        [fast] * 2,
        "right",
    )
    order = list(reversed(masks))
    left = left + swap(left_out, order[0], count)
    right = right + swap(right_out, order[0], count)
    logit_grad, right = lax.optimization_barrier((logit_grad, right))
    (grad_head,) = call(
        head_kernel,
        [shape(head_weight.shape, jnp.bfloat16)],
        [pltpu.VMEM((depth, width), jnp.bfloat16), sems],
        2 * rows * depth * width,
        [gathered, logit_grad],
        [fast] * 2,
        [pl.ANY],
        "grad_head",
    )
    split = len(order) > 2
    if split:
        size = rows // 8
        right = right.reshape(2, 2, size, columns)
        left = halve(left, order[1], 0, me, count)
        right = halve(right, order[2], 1, me, count)
        left, grad_head = lax.optimization_barrier((left, grad_head))
        left = halve(left, order[2], 0, me, count)
        right = halve(right, order[1], 0, me, count).reshape(size, columns)
    partial = jnp.concatenate([left, right], axis=1)
    for mask in order[3 if split else 1:]:
        partial = halve(partial, mask, 0, me, count)
    norm_grad = partial * norm_gain
    grad_hidden = inv_rms * (
        norm_grad - normed * jnp.mean(norm_grad * normed, axis=1, keepdims=True)
    )
    return (grad_hidden.astype(jnp.bfloat16), grad_head)


def solution(mesh):
    n_seq, n_vocab = mesh.shape["seq"], mesh.shape["vocab"]
    count = n_seq * n_vocab
    bits = count.bit_length() - 1
    masks = [1 << b for b in reversed(range(bits))]
    placed = (
        P(axes, None),
        P(),
        P(None, axes),
        P("seq", None, "vocab"),
        P(),
        P(),
    )

    def local(*arrays):
        return shards(masks, n_vocab, *arrays)

    return jax.shard_map(
        local,
        mesh=mesh,
        in_specs=placed,
        out_specs=(P(axes, None), P(None, axes)),
        check_vma=False,
    )
```

```python
import jax
import jax.numpy as jnp
from jax import lax
from jax.experimental import pallas as pl
from jax.experimental.pallas import tpu as pltpu
from jax.sharding import PartitionSpec as P

epsilon = 1e-06
axes = ("seq", "row", "core")


def call(kernel, out_shape, scratch, flops, inputs, spaces, out_spaces, name):
    def size(leaf):
        return leaf.size * leaf.dtype.itemsize

    outs = list(out_shape)
    return pl.pallas_call(
        kernel,
        out_shape=outs,
        in_specs=[pl.BlockSpec(memory_space=s) for s in spaces],
        out_specs=[pl.BlockSpec(memory_space=s) for s in out_spaces],
        scratch_shapes=scratch,
        compiler_params=pltpu.CompilerParams(vmem_limit_bytes=60 << 20),
        cost_estimate=pl.CostEstimate(
            flops=flops, bytes_accessed=sum(map(size, list(inputs) + outs)), transcendentals=0
        ),
        name=name,
    )(*inputs)


def split_evenly(total, unit):
    parts = max(p for p in (1, 2, 4, 5) if total % (p * unit) == 0)
    return parts, total // parts


def logits_kernel(gathered_ref, weight_ref, table_ref, place_ref, logits_ref, teacher_ref, stats_ref, held, sems):
    depth = weight_ref.shape[0]
    parts, size = split_evenly(depth, 256)
    rows = gathered_ref.shape[0]
    copies = []
    for p in range(parts):
        block = pl.ds(p * size, size)
        copies.append(pltpu.make_async_copy(weight_ref.at[block], held.at[block], sems.at[p]))
        copies[-1].start()
    slots = lax.broadcasted_iota(jnp.int32, (rows, table_ref.shape[0]), 1)
    pick = (place_ref[...] == slots).astype(jnp.bfloat16)
    teacher = jnp.dot(pick, table_ref[...], preferred_element_type=jnp.float32)
    teacher_ref[...] = teacher
    teacher_top = jnp.max(teacher, axis=1, keepdims=True)
    teacher_total = jnp.sum(jnp.exp(teacher - teacher_top), axis=1, keepdims=True)
    logits = jnp.zeros(logits_ref.shape, jnp.float32)
    for p in range(parts):
        copies[p].wait()
        logits += jnp.dot(
            gathered_ref[:, p * size : (p + 1) * size],
            held[p * size : (p + 1) * size, :],
            preferred_element_type=jnp.float32,
        )
    logits_ref[...] = logits
    student_top = jnp.max(logits, axis=1, keepdims=True)
    shifted = jnp.exp(logits - student_top)
    student_total = jnp.sum(shifted, axis=1, keepdims=True)
    cross_sum = jnp.sum(shifted * (logits - teacher), axis=1, keepdims=True)
    tops = jnp.concatenate([student_top, teacher_top], axis=0)
    totals = jnp.concatenate([student_total, teacher_total], axis=0)
    crosses = jnp.concatenate([cross_sum, jnp.zeros_like(cross_sum)], axis=0)
    lane = lax.broadcasted_iota(jnp.int32, (2 * rows, 128), 1)
    table = jnp.where(lane == 0, tops, jnp.where(lane == 1, totals, jnp.where(lane == 2, crosses, 0.0)))
    stats = table.T[:4]
    for p in range(stats_ref.shape[0]):
        stats_ref[p] = stats


def grad_rows(logits, teacher, stats, row_weight):
    rows = logits.shape[0]
    tops, totals, crosses = stats[:, 0, :], stats[:, 1, :], stats[:, 2, :]
    top = jnp.max(tops, axis=0, keepdims=True)
    scale = jnp.exp(tops - top)
    total = jnp.sum(totals * scale, axis=0, keepdims=True)
    cross = jnp.sum(crosses * scale, axis=0, keepdims=True)
    table = jnp.concatenate([top, total, cross, jnp.zeros((125, 2 * rows), jnp.float32)], axis=0).T
    student_top, teacher_top = table[:rows, 0:1], table[rows:, 0:1]
    student_total, teacher_total = table[:rows, 1:2], table[rows:, 1:2]
    cross_sum = table[:rows, 2:3]
    student_lse = student_top + jnp.log(student_total)
    teacher_lse = teacher_top + jnp.log(teacher_total)
    divergence = cross_sum / student_total - student_lse + teacher_lse
    log_prob = logits - student_lse
    log_gap = log_prob - (teacher - teacher_lse)
    return (row_weight * jnp.exp(log_prob) * (log_gap - divergence)).astype(jnp.bfloat16)


def back(grad, weight_copies, held, keep_ref, send_ref, size):
    half = grad.shape[0] // 2
    up = lax.axis_index("core") != 0
    low, high = grad[:half], grad[half:]
    chosen = jnp.concatenate([jnp.where(up, high, low), jnp.where(up, low, high)], axis=0)
    for p, copy in enumerate(weight_copies):
        copy.wait()
        block = lax.dot_general(
            chosen,
            held[p * size : (p + 1) * size, :],
            (((1,), (1,)), ((), ())),
            preferred_element_type=jnp.float32,
        )
        keep_ref[:, p * size : (p + 1) * size] = block[:half]
        send_ref[:, p * size : (p + 1) * size] = block[half:]


def start_copies(weight_ref, held, sems, first):
    columns = held.shape[0]
    parts, size = split_evenly(columns, 256)
    copies = []
    for p in range(parts):
        source = weight_ref.at[pl.ds(first + p * size, size)]
        copies.append(pltpu.make_async_copy(source, held.at[pl.ds(p * size, size)], sems.at[p]))
        copies[-1].start()
    return copies, size


def left_kernel(logits_ref, teacher_ref, stats_ref, valid_ref, weight_ref, grad_ref, keep_ref, send_ref, held, sems):
    copies, size = start_copies(weight_ref, held, sems, 0)
    grad = grad_rows(logits_ref[...], teacher_ref[...], stats_ref[...], valid_ref[...])
    grad_ref[...] = grad
    back(grad, copies, held, keep_ref, send_ref, size)


def right_kernel(grad_ref, weight_ref, keep_ref, send_ref, held, sems):
    copies, size = start_copies(weight_ref, held, sems, held.shape[0])
    back(grad_ref[...], copies, held, keep_ref, send_ref, size)


def head_kernel(gathered_ref, grad_ref, out_ref, held, sems):
    parts, size = split_evenly(out_ref.shape[0], 256)
    grad = grad_ref[...]
    copies = []
    for p in range(parts):
        block = pl.ds(p * size, size)
        held[p * size : (p + 1) * size, :] = lax.dot_general(
            gathered_ref[:, p * size : (p + 1) * size],
            grad,
            (((0,), (0,)), ((), ())),
            preferred_element_type=jnp.float32,
        ).astype(jnp.bfloat16)
        copies.append(pltpu.make_async_copy(held.at[block], out_ref.at[block], sems.at[p]))
        copies[-1].start()
    for copy in copies:
        copy.wait()


def norm_kernel(hidden_ref, gain_ref, features_ref):
    widened = hidden_ref[...].astype(jnp.float32)
    inv_rms = lax.rsqrt(jnp.mean(widened * widened, axis=1, keepdims=True) + epsilon)
    features = (widened * inv_rms * gain_ref[...]).astype(jnp.bfloat16)
    for p in range(features_ref.shape[0]):
        features_ref[p] = features


def shards(hidden, norm_gain, head_weight, teacher_logits, teacher_slot, valid_tokens):
    n_seq, n_row = lax.axis_size("seq"), lax.axis_size("row")
    chips = n_seq * n_row
    own, depth = hidden.shape
    width = head_weight.shape[1]
    rows = own * chips * 2
    cap = teacher_logits.shape[0]
    up = lax.axis_index("core") != 0
    shape, fast = jax.ShapeDtypeStruct, pltpu.VMEM
    sems = pltpu.SemaphoreType.DMA((5,))

    def in_order(values):
        return values.reshape(chips, 2, own).transpose(1, 0, 2).reshape(rows, 1)

    def other_core(value):
        return lax.ppermute(value, "core", [(0, 1), (1, 0)])

    (features,) = call(
        norm_kernel,
        [shape((chips, own, depth), jnp.bfloat16)],
        [],
        0,
        [hidden, norm_gain[None]],
        [fast] * 2,
        [fast],
        "features",
    )
    mine = lax.all_to_all(features, ("seq", "row"), split_axis=0, concat_axis=0, tiled=True)
    blocks, _ = lax.optimization_barrier((teacher_logits, features))
    blocks = lax.all_to_all(
        blocks.transpose(1, 0, 2), "seq", split_axis=0, concat_axis=0, tiled=True
    )
    slot_table = blocks.reshape(n_seq * cap, width)
    mine = mine.reshape(rows // 2, depth)
    theirs = other_core(mine)
    gathered = jnp.concatenate(
        [jnp.where(up, theirs, mine), jnp.where(up, mine, theirs)], axis=0
    )
    place = in_order(teacher_slot)
    row_weight = in_order(valid_tokens).astype(jnp.float32)

    logits, teacher, stats = call(
        logits_kernel,
        [shape((rows, width), jnp.float32)] * 2 + [shape((chips * 2, 4, 2 * rows), jnp.float32)],
        [pltpu.VMEM((depth, width), jnp.bfloat16), sems],
        2 * rows * depth * width,
        [gathered, head_weight, slot_table, place],
        [fast, pltpu.HBM, fast, fast],
        [fast] * 3,
        "logits",
    )
    stats = lax.all_to_all(stats, axes, split_axis=0, concat_axis=0, tiled=True)
    columns = depth // 2
    halves = [shape((rows // 2, columns), jnp.float32)] * 2
    half_weight = [pltpu.VMEM((columns, width), jnp.bfloat16), sems]
    logit_grad, left, left_out = call(
        left_kernel,
        [shape((rows, width), jnp.bfloat16)] + halves,
        half_weight,
        2 * rows * columns * width,
        [logits, teacher, stats, row_weight, head_weight],
        [fast] * 4 + [pltpu.HBM],
        [fast] * 3,
        "left",
    )
    right, right_out = call(
        right_kernel,
        halves,
        half_weight,
        2 * rows * columns * width,
        [logit_grad, head_weight],
        [fast, pltpu.HBM],
        [fast] * 2,
        "right",
    )
    left = left + other_core(left_out)
    right = right + other_core(right_out)
    share = jnp.concatenate([left, right], axis=1).reshape(chips, own, depth).astype(jnp.bfloat16)
    shares = lax.all_to_all(share, ("seq", "row"), split_axis=0, concat_axis=0, tiled=True)
    logit_grad, _ = lax.optimization_barrier((logit_grad, share))
    (grad_head,) = call(
        head_kernel,
        [shape(head_weight.shape, jnp.bfloat16)],
        [pltpu.VMEM((depth, width), jnp.bfloat16), sems],
        2 * rows * depth * width,
        [gathered, logit_grad],
        [fast] * 2,
        [pltpu.HBM],
        "grad_head",
    )
    widened = hidden.astype(jnp.float32)
    inv_rms = lax.rsqrt(jnp.mean(widened * widened, axis=1, keepdims=True) + epsilon)
    normed = widened * inv_rms
    norm_grad = jnp.sum(shares.astype(jnp.float32), axis=0) * norm_gain
    grad_hidden = inv_rms * (
        norm_grad - normed * jnp.mean(norm_grad * normed, axis=1, keepdims=True)
    )
    return (grad_hidden.astype(jnp.bfloat16), grad_head)


def solution(mesh):
    n_seq, n_vocab = mesh.shape["seq"], mesh.shape["vocab"]
    finer = jax.sharding.Mesh(mesh.devices.reshape(n_seq, n_vocab // 2, 2), axes)
    placed = (
        P(axes, None),
        P(),
        P(None, axes),
        P("seq", None, ("row", "core")),
        P(),
        P(),
    )
    return jax.shard_map(
        shards,
        mesh=finer,
        in_specs=placed,
        out_specs=(P(axes, None), P(None, axes)),
        check_vma=False,
    )
```

```python
import jax
import jax.numpy as jnp
from jax import lax
from jax.experimental import pallas as pl
from jax.experimental.pallas import tpu as pltpu
from jax.sharding import PartitionSpec as P

epsilon = 1e-06
axes = ("seq", "row", "core")
fast, far = pltpu.VMEM, pl.ANY
shape = jax.ShapeDtypeStruct
f32, bf16 = jnp.float32, jnp.bfloat16
large = 57 << 20


def call(kernel, name, out_shape, inputs, spaces, out_spaces, scratch=(), flops=0, limit=None):
    def size(leaf):
        return leaf.size * leaf.dtype.itemsize

    near = [x for x, s in zip(inputs, spaces) if s == fast]
    near += [x for x, s in zip(out_shape, out_spaces) if s == fast]
    return pl.pallas_call(
        kernel,
        out_shape=list(out_shape),
        in_specs=[pl.BlockSpec(memory_space=s) for s in spaces],
        out_specs=[pl.BlockSpec(memory_space=s) for s in out_spaces],
        scratch_shapes=list(scratch),
        compiler_params=pltpu.CompilerParams(
            vmem_limit_bytes=limit or 2 * sum(map(size, near)) + (8 << 20)
        ),
        cost_estimate=pl.CostEstimate(
            flops=flops,
            bytes_accessed=sum(map(size, list(inputs) + list(out_shape))),
            transcendentals=0,
        ),
        name=name,
    )(*inputs)


def split_evenly(total, unit):
    parts = max(p for p in (1, 2, 4, 5) if total % (p * unit) == 0)
    return parts, total // parts


def my_index():
    return (lax.axis_index("seq") * lax.axis_size("row") + lax.axis_index("row")) * 2 + lax.axis_index("core")


def exchange(value, masks, own, me):
    length = value.shape[0]
    row = lax.broadcasted_iota(jnp.int32, value.shape, 0)
    for bit, mask in enumerate(masks):
        size = own << bit
        if size >= 8:
            parts = [value[i : i + size] for i in range(0, length, size)]
            other = jnp.concatenate([parts[i ^ 1] for i in range(len(parts))], axis=0)
        else:
            later, earlier = pltpu.roll(value, length - size, 0), pltpu.roll(value, size, 0)
            other = jnp.where((row & size) == 0, later, earlier)
        value = jnp.where((me & mask) != 0, other, value)
    return value


def own_order(row_values, masks, own, me):
    rows = row_values.shape[1]
    place = lax.broadcasted_iota(jnp.int32, (rows, rows), 0)
    block, inner = lax.div(place, own), lax.rem(place, own)
    device = jnp.full((rows, rows), me, jnp.int32)
    for bit, mask in enumerate(masks):
        device = device ^ (((block >> bit) & 1) * mask)
    match = device * own + inner == lax.broadcasted_iota(jnp.int32, (rows, rows), 1)
    return jnp.sum(jnp.where(match, row_values.astype(f32), 0.0), axis=1, keepdims=True)


def features_kernel(hidden_ref, gain_ref, features_ref, hidden, gain, sems):
    copies = [
        pltpu.make_async_copy(hidden_ref, hidden, sems.at[0]),
        pltpu.make_async_copy(gain_ref, gain, sems.at[1]),
    ]
    for copy in copies:
        copy.start()
    for copy in copies:
        copy.wait()
    widened = hidden[...].astype(f32)
    inv_rms = lax.rsqrt(jnp.mean(widened * widened, axis=1, keepdims=True) + epsilon)
    features_ref[...] = (widened * inv_rms * gain[...]).astype(bf16)


def teacher_kernel(blocks_ref, keep_ref, send_ref):
    my_seq = lax.axis_index("seq")
    for k in range(keep_ref.shape[0]):
        keep_ref[k] = blocks_ref[my_seq ^ (2 * k)]
        send_ref[k] = blocks_ref[my_seq ^ (2 * k + 1)]


def logits_kernel(masks, own, cap, low_ref, high_ref, weight_ref, table_ref, slots_ref, logits_ref, teacher_ref, local_ref, stats_ref):
    me, my_seq = my_index(), lax.axis_index("seq")
    depth = weight_ref.shape[0]
    rows = logits_ref.shape[0]
    parts, size = split_evenly(depth, 256)
    slots = own_order(slots_ref[...], masks, own, me).astype(jnp.int32)
    place = (lax.div(slots, cap) ^ my_seq) * cap + lax.rem(slots, cap)
    pick = (place == lax.broadcasted_iota(jnp.int32, (rows, table_ref.shape[0]), 1)).astype(bf16)
    teacher = jnp.dot(pick, table_ref[...], preferred_element_type=f32)
    teacher_ref[...] = teacher
    teacher_top = jnp.max(teacher, axis=1, keepdims=True)
    teacher_total = jnp.sum(jnp.exp(teacher - teacher_top), axis=1, keepdims=True)
    logits = jnp.zeros(logits_ref.shape, f32)
    for p in range(parts):
        block = slice(p * size, (p + 1) * size)
        features = jnp.concatenate([low_ref[:, block], high_ref[:, block]], axis=0)
        logits += jnp.dot(features, weight_ref[block, :], preferred_element_type=f32)
    logits_ref[...] = logits
    student_top = jnp.max(logits, axis=1, keepdims=True)
    shifted = jnp.exp(logits - student_top)
    student_total = jnp.sum(shifted, axis=1, keepdims=True)
    cross_sum = jnp.sum(shifted * (logits - teacher), axis=1, keepdims=True)
    tops = jnp.concatenate([student_top, teacher_top], axis=0)
    totals = jnp.concatenate([student_total, teacher_total], axis=0)
    crosses = jnp.concatenate([cross_sum, jnp.zeros_like(cross_sum)], axis=0)
    lane = lax.broadcasted_iota(jnp.int32, (2 * rows, 128), 1)
    table = jnp.where(lane == 0, tops, jnp.where(lane == 1, totals, jnp.where(lane == 2, crosses, 0.0)))
    local_ref[...] = table[:rows]
    stats = exchange(table, masks, own, me).T[:4]
    for p in range(stats_ref.shape[0]):
        stats_ref[p] = stats


def products_kernel(first, logits_ref, teacher_ref, local_ref, weight_ref, keep_ref, send_ref, held, sems):
    columns = held.shape[0]
    parts, size = split_evenly(columns, 256)
    copies = []
    for p in range(parts):
        source = weight_ref.at[pl.ds(first + p * size, size)]
        copies.append(pltpu.make_async_copy(source, held.at[pl.ds(p * size, size)], sems.at[p]))
        copies[-1].start()
    logits = logits_ref[...]
    half = logits.shape[0] // 2
    shifted = jnp.exp(logits - local_ref[:, 0:1])
    center = local_ref[:, 2:3] / local_ref[:, 1:2]
    gaps = (shifted * (logits - teacher_ref[...] - center)).astype(bf16)
    shifted = shifted.astype(bf16)
    left = jnp.concatenate([gaps[:half], shifted[:half], gaps[half:], shifted[half:]], axis=0)
    for p, copy in enumerate(copies):
        copy.wait()
        block = slice(p * size, (p + 1) * size)
        product = lax.dot_general(
            left, held[block, :], (((1,), (1,)), ((), ())), preferred_element_type=f32
        )
        keep_ref[:, block] = product[: 2 * half]
        send_ref[:, block] = product[2 * half :]


def combine_kernel(masks, own, stats_ref, valid_ref, left_ref, left_in_ref, right_ref, right_in_ref, share_ref, terms_ref):
    me = my_index()
    chips, _, depth = share_ref.shape
    rows = valid_ref.shape[1]
    half = rows // 2
    stats = stats_ref[...]
    tops, totals, crosses = stats[:, 0, :], stats[:, 1, :], stats[:, 2, :]
    top = jnp.max(tops, axis=0, keepdims=True)
    scale = jnp.exp(tops - top)
    total = jnp.sum(totals * scale, axis=0, keepdims=True)
    cross = jnp.sum(crosses * scale, axis=0, keepdims=True)
    mine, theirs = stats_ref[me], stats_ref[me ^ 1]
    table = jnp.concatenate(
        [
            top,
            total,
            cross,
            mine[0:1],
            mine[2:3] / mine[1:2],
            theirs[0:1],
            theirs[2:3] / theirs[1:2],
            jnp.zeros((121, 2 * rows), f32),
        ],
        axis=0,
    ).T
    table = exchange(table, masks, own, me)
    student_top, teacher_top = table[:rows, 0:1], table[rows:, 0:1]
    student_total, teacher_total = table[:rows, 1:2], table[rows:, 1:2]
    student_lse = student_top + jnp.log(student_total)
    teacher_lse = teacher_top + jnp.log(teacher_total)
    divergence = table[:rows, 2:3] / student_total - student_lse + teacher_lse
    row_weight = own_order(valid_ref[...], masks, own, me)
    lane = lax.broadcasted_iota(jnp.int32, (rows, 128), 1)
    terms_ref[...] = jnp.where(
        lane == 0,
        student_lse,
        jnp.where(lane == 1, teacher_lse, jnp.where(lane == 2, divergence, row_weight)),
    )
    shift = teacher_lse - student_lse - divergence

    def factors(at):
        near = row_weight * jnp.exp(table[:rows, at : at + 1] - student_lse)
        return near[:half], (near * (table[:rows, at + 1 : at + 2] + shift))[:half]

    a_near, b_near = factors(3)
    a_far, b_far = factors(5)
    columns = depth // 2
    for first, near_ref, far_ref in ((0, left_ref, left_in_ref), (columns, right_ref, right_in_ref)):
        share = (
            a_near * near_ref[:half, :]
            + b_near * near_ref[half:, :]
            + a_far * far_ref[:half, :]
            + b_far * far_ref[half:, :]
        ).astype(bf16)
        for p in range(chips):
            device = me
            for bit, mask in enumerate(masks[:-1]):
                if p >> bit & 1:
                    device = device ^ mask
            share_ref[device >> 1, :, first : first + columns] = share[p * own : (p + 1) * own]


def head_kernel(low_ref, high_ref, logits_ref, teacher_ref, terms_ref, out_ref, held, sems):
    parts, size = split_evenly(out_ref.shape[0], 256)
    student_lse, teacher_lse = terms_ref[:, 0:1], terms_ref[:, 1:2]
    log_prob = logits_ref[...] - student_lse
    log_gap = log_prob - (teacher_ref[...] - teacher_lse)
    grad = (terms_ref[:, 3:4] * jnp.exp(log_prob) * (log_gap - terms_ref[:, 2:3])).astype(bf16)
    copies = []
    for p in range(parts):
        block = slice(p * size, (p + 1) * size)
        features = jnp.concatenate([low_ref[:, block], high_ref[:, block]], axis=0)
        held[block, :] = lax.dot_general(
            features, grad, (((0,), (0,)), ((), ())), preferred_element_type=f32
        ).astype(bf16)
        rows = pl.ds(p * size, size)
        copies.append(pltpu.make_async_copy(held.at[rows], out_ref.at[rows], sems.at[p]))
        copies[-1].start()
    for copy in copies:
        copy.wait()


def finish_kernel(hidden_ref, gain_ref, shares_ref, out_ref):
    widened = hidden_ref[...].astype(f32)
    inv_rms = lax.rsqrt(jnp.mean(widened * widened, axis=1, keepdims=True) + epsilon)
    normed = widened * inv_rms
    feature_grad = shares_ref[0].astype(f32)
    for p in range(1, shares_ref.shape[0]):
        feature_grad += shares_ref[p].astype(f32)
    norm_grad = feature_grad * gain_ref[...]
    mean = jnp.mean(norm_grad * normed, axis=1, keepdims=True)
    out_ref[...] = (inv_rms * (norm_grad - normed * mean)).astype(bf16)


def shards(hidden, norm_gain, head_weight, teacher_logits, teacher_slot, valid_tokens):
    n_seq, n_row = lax.axis_size("seq"), lax.axis_size("row")
    chips = n_seq * n_row
    count = chips * 2
    own, depth = hidden.shape
    width = head_weight.shape[1]
    rows = own * count
    cap = teacher_logits.shape[0]
    columns = depth // 2
    gain = norm_gain[None]
    masks = [1 << b for b in reversed(range(count.bit_length() - 1))]
    seq_masks = [m for m in reversed(masks) if m >= n_row * 2]

    def swap(value, mask):
        return lax.ppermute(value, axes, [(i, i ^ mask) for i in range(count)])

    def sems(number):
        return pltpu.SemaphoreType.DMA((number,))

    (gathered,) = call(
        features_kernel,
        "features",
        [shape((own, depth), bf16)],
        [hidden, gain],
        [far] * 2,
        [fast],
        [pltpu.VMEM((own, depth), bf16), pltpu.VMEM((1, depth), f32), sems(2)],
        limit=large,
    )
    half_blocks = shape((n_seq // 2, cap, width), bf16)
    keep, send = call(
        teacher_kernel,
        "teacher_blocks",
        [half_blocks] * 2,
        [teacher_logits.transpose(1, 0, 2)],
        [fast],
        [fast] * 2,
    )
    held = jnp.concatenate([keep, swap(send, seq_masks[0])], axis=1)
    behind = len(masks) - len(seq_masks)
    for step, mask in enumerate(masks[:-1]):
        gathered = jnp.concatenate([gathered, swap(gathered, mask)], axis=0)
        if step == 0:
            gathered, _ = lax.optimization_barrier((gathered, send))
        bit = step - behind + 2
        if 1 <= bit < len(seq_masks):
            held, _ = lax.optimization_barrier((held, gathered))
            pairs = held.reshape((held.shape[0] // 2, 2) + held.shape[1:])
            held = jnp.concatenate([pairs[:, 0], swap(pairs[:, 1], seq_masks[bit])], axis=1)
    low, high = gathered, swap(gathered, masks[-1])

    def with_masks(kernel, *more):
        return lambda *refs: kernel(masks, own, *more, *refs)

    square = shape((rows, width), f32)
    logits, teacher, local, stats = call(
        with_masks(logits_kernel, cap),
        "logits",
        [square, square, shape((rows, 128), f32), shape((count, 4, 2 * rows), f32)],
        [low, high, head_weight, held[0], teacher_slot[None]],
        [fast] * 5,
        [fast] * 4,
        flops=2 * rows * depth * width,
    )
    stats = lax.all_to_all(stats, axes, split_axis=0, concat_axis=0, tiled=True)

    def products(first, name):
        kept, sent = call(
            lambda *refs: products_kernel(first, *refs),
            name,
            [shape((rows, columns), f32)] * 2,
            [logits, teacher, local, head_weight],
            [fast] * 3 + [far],
            [fast] * 2,
            [pltpu.VMEM((columns, width), bf16), sems(5)],
            flops=4 * rows * columns * width,
            limit=large,
        )
        return kept, swap(sent, masks[-1])

    left = products(0, "left")
    right = products(columns, "right")
    share, terms = call(
        with_masks(combine_kernel),
        "combine",
        [shape((chips, own, depth), bf16), shape((rows, 128), f32)],
        [stats, valid_tokens[None], *left, *right],
        [fast] * 6,
        [fast] * 2,
    )
    shares = lax.all_to_all(share, ("seq", "row"), split_axis=0, concat_axis=0, tiled=True)
    (grad_head,) = call(
        head_kernel,
        "grad_head",
        [shape(head_weight.shape, bf16)],
        [low, high, logits, teacher, terms],
        [fast] * 5,
        [far],
        [pltpu.VMEM((depth, width), bf16), sems(5)],
        flops=2 * rows * depth * width,
        limit=large,
    )
    (grad_hidden,) = call(
        finish_kernel,
        "finish",
        [shape((own, depth), bf16)],
        [hidden, gain, shares],
        [fast] * 3,
        [fast],
    )
    return (grad_hidden, grad_head)


def solution(mesh):
    n_seq, n_vocab = mesh.shape["seq"], mesh.shape["vocab"]
    finer = jax.sharding.Mesh(mesh.devices.reshape(n_seq, n_vocab // 2, 2), axes)
    placed = (
        P(axes, None),
        P(),
        P(None, axes),
        P("seq", None, ("row", "core")),
        P(),
        P(),
    )
    return jax.shard_map(
        shards,
        mesh=finer,
        in_specs=placed,
        out_specs=(P(axes, None), P(None, axes)),
        check_vma=False,
    )
```

```python
import math

import jax
import jax.numpy as jnp
from jax import lax
from jax.experimental import pallas as pl
from jax.experimental.pallas import tpu as pltpu
from jax.sharding import PartitionSpec as P

epsilon = 1e-06
axes = ("seq", "row", "core")
fast, far = pltpu.VMEM, pl.ANY
shape = jax.ShapeDtypeStruct
f32, bf16 = jnp.float32, jnp.bfloat16


def call(kernel, name, out_shape, inputs, spaces, out_spaces, scratch=(), flops=0):
    def size(leaf):
        return leaf.size * leaf.dtype.itemsize

    near = [x for x, s in zip(inputs, spaces) if s == fast]
    near += [x for x, s in zip(out_shape, out_spaces) if s == fast]
    held = sum(x.dtype.itemsize * math.prod(x.shape) for x in scratch if x.memory_space == fast)
    return pl.pallas_call(
        kernel,
        out_shape=list(out_shape),
        in_specs=[pl.BlockSpec(memory_space=s) for s in spaces],
        out_specs=[pl.BlockSpec(memory_space=s) for s in out_spaces],
        scratch_shapes=list(scratch),
        compiler_params=pltpu.CompilerParams(
            vmem_limit_bytes=2 * sum(map(size, near)) + held + (8 << 20)
        ),
        cost_estimate=pl.CostEstimate(
            flops=flops,
            bytes_accessed=sum(map(size, list(inputs) + list(out_shape))),
            transcendentals=0,
        ),
        name=name,
    )(*inputs)


def split_evenly(total, unit):
    parts = max(p for p in (1, 2, 4, 5) if total % (p * unit) == 0)
    return parts, total // parts


def my_index():
    return (lax.axis_index("seq") * lax.axis_size("row") + lax.axis_index("row")) * 2 + lax.axis_index("core")


def exchange(value, masks, own, me):
    length = value.shape[0]
    row = lax.broadcasted_iota(jnp.int32, value.shape, 0)
    for bit, mask in enumerate(masks):
        size = own << bit
        if size >= 8:
            parts = [value[i : i + size] for i in range(0, length, size)]
            other = jnp.concatenate([parts[i ^ 1] for i in range(len(parts))], axis=0)
        else:
            later, earlier = pltpu.roll(value, length - size, 0), pltpu.roll(value, size, 0)
            other = jnp.where((row & size) == 0, later, earlier)
        value = jnp.where((me & mask) != 0, other, value)
    return value


def own_order(row_values, masks, own, me):
    rows = row_values.shape[1]
    place = lax.broadcasted_iota(jnp.int32, (rows, rows), 0)
    block, inner = lax.div(place, own), lax.rem(place, own)
    device = jnp.full((rows, rows), me, jnp.int32)
    for bit, mask in enumerate(masks):
        device = device ^ (((block >> bit) & 1) * mask)
    match = device * own + inner == lax.broadcasted_iota(jnp.int32, (rows, rows), 1)
    return jnp.sum(jnp.where(match, row_values.astype(f32), 0.0), axis=1, keepdims=True)


def features_kernel(hidden_ref, gain_ref, features_ref, hidden, gain, sems):
    copies = [
        pltpu.make_async_copy(hidden_ref, hidden, sems.at[0]),
        pltpu.make_async_copy(gain_ref, gain, sems.at[1]),
    ]
    for copy in copies:
        copy.start()
    for copy in copies:
        copy.wait()
    widened = hidden[...].astype(f32)
    inv_rms = lax.rsqrt(jnp.mean(widened * widened, axis=1, keepdims=True) + epsilon)
    features_ref[...] = (widened * inv_rms * gain[...]).astype(bf16)


def teacher_kernel(blocks_ref, keep_ref, send_ref):
    my_seq = lax.axis_index("seq")
    for k in range(keep_ref.shape[0]):
        keep_ref[k] = blocks_ref[my_seq ^ (2 * k)]
        send_ref[k] = blocks_ref[my_seq ^ (2 * k + 1)]


def logits_kernel(masks, own, cap, low_ref, high_ref, weight_ref, table_ref, slots_ref, logits_ref, teacher_ref, local_ref, stats_ref):
    me, my_seq = my_index(), lax.axis_index("seq")
    depth = weight_ref.shape[0]
    rows = logits_ref.shape[0]
    parts, size = split_evenly(depth, 256)
    slots = own_order(slots_ref[...], masks, own, me).astype(jnp.int32)
    place = (lax.div(slots, cap) ^ my_seq) * cap + lax.rem(slots, cap)
    pick = (place == lax.broadcasted_iota(jnp.int32, (rows, table_ref.shape[0]), 1)).astype(bf16)
    teacher = jnp.dot(pick, table_ref[...], preferred_element_type=f32)
    teacher_ref[...] = teacher
    teacher_top = jnp.max(teacher, axis=1, keepdims=True)
    teacher_total = jnp.sum(jnp.exp(teacher - teacher_top), axis=1, keepdims=True)
    logits = jnp.zeros(logits_ref.shape, f32)
    for p in range(parts):
        block = slice(p * size, (p + 1) * size)
        features = jnp.concatenate([low_ref[:, block], high_ref[:, block]], axis=0)
        logits += jnp.dot(features, weight_ref[block, :], preferred_element_type=f32)
    logits_ref[...] = logits
    student_top = jnp.max(logits, axis=1, keepdims=True)
    shifted = jnp.exp(logits - student_top)
    student_total = jnp.sum(shifted, axis=1, keepdims=True)
    cross_sum = jnp.sum(shifted * (logits - teacher), axis=1, keepdims=True)
    tops = jnp.concatenate([student_top, teacher_top], axis=0)
    totals = jnp.concatenate([student_total, teacher_total], axis=0)
    crosses = jnp.concatenate([cross_sum, jnp.zeros_like(cross_sum)], axis=0)
    lane = lax.broadcasted_iota(jnp.int32, (2 * rows, 128), 1)
    table = jnp.where(lane == 0, tops, jnp.where(lane == 1, totals, jnp.where(lane == 2, crosses, 0.0)))
    local_ref[...] = table[:rows]
    stats = exchange(table, masks, own, me).T[:4]
    for p in range(stats_ref.shape[0]):
        stats_ref[p] = stats


def products_kernel(logits_ref, teacher_ref, local_ref, weight_ref, gaps_ref, shifted_ref):
    depth = weight_ref.shape[0]
    parts, size = split_evenly(depth, 256)
    logits = logits_ref[...]
    rows = logits.shape[0]
    shifted = jnp.exp(logits - local_ref[:, 0:1])
    center = local_ref[:, 2:3] / local_ref[:, 1:2]
    gaps = shifted * (logits - teacher_ref[...] - center)
    left = jnp.concatenate([gaps.astype(bf16), shifted.astype(bf16)], axis=0)
    for p in range(parts):
        block = slice(p * size, (p + 1) * size)
        product = lax.dot_general(
            left, weight_ref[block, :], (((1,), (1,)), ((), ())), preferred_element_type=f32
        )
        gaps_ref[:, block] = product[:rows]
        shifted_ref[:, block] = product[rows:]


def send_kernel(masks, own, stats_ref, valid_ref, gaps_ref, shifted_ref, out_ref, terms_ref):
    me = my_index()
    rows = valid_ref.shape[1]
    half = rows // 2
    stats = stats_ref[...]
    tops, totals, crosses = stats[:, 0, :], stats[:, 1, :], stats[:, 2, :]
    top = jnp.max(tops, axis=0, keepdims=True)
    scale = jnp.exp(tops - top)
    total = jnp.sum(totals * scale, axis=0, keepdims=True)
    cross = jnp.sum(crosses * scale, axis=0, keepdims=True)
    mine = stats_ref[me]
    table = jnp.concatenate(
        [top, total, cross, mine[0:1], mine[2:3] / mine[1:2], jnp.zeros((123, 2 * rows), f32)], axis=0
    ).T
    table = exchange(table, masks, own, me)
    student_top, teacher_top = table[:rows, 0:1], table[rows:, 0:1]
    student_total, teacher_total = table[:rows, 1:2], table[rows:, 1:2]
    student_lse = student_top + jnp.log(student_total)
    teacher_lse = teacher_top + jnp.log(teacher_total)
    divergence = table[:rows, 2:3] / student_total - student_lse + teacher_lse
    row_weight = own_order(valid_ref[...], masks, own, me)
    scale = row_weight * jnp.exp(table[:rows, 3:4] - student_lse)
    offset = scale * (table[:rows, 4:5] + (teacher_lse - student_lse - divergence))
    lane = lax.broadcasted_iota(jnp.int32, (rows, 128), 1)
    terms = row_weight
    for at, column in enumerate((student_lse, teacher_lse, divergence, scale, offset)):
        terms = jnp.where(lane == at, column, terms)
    terms_ref[...] = terms
    out_ref[...] = scale[half:] * gaps_ref[half:, :] + offset[half:] * shifted_ref[half:, :]


def keep_kernel(terms_ref, gaps_ref, shifted_ref, out_ref):
    half = out_ref.shape[0]
    out_ref[...] = terms_ref[:half, 3:4] * gaps_ref[:half, :] + terms_ref[:half, 4:5] * shifted_ref[:half, :]


def share_kernel(masks, own, keep_ref, arrived_ref, share_ref):
    me = my_index()
    share = (keep_ref[...] + arrived_ref[...]).astype(bf16)
    for p in range(share_ref.shape[0]):
        device = me
        for bit, mask in enumerate(masks[:-1]):
            if p >> bit & 1:
                device = device ^ mask
        share_ref[device >> 1] = share[p * own : (p + 1) * own]


def head_kernel(low_ref, high_ref, logits_ref, teacher_ref, terms_ref, out_ref, held, sems):
    parts, size = split_evenly(out_ref.shape[0], 256)
    student_lse, teacher_lse = terms_ref[:, 0:1], terms_ref[:, 1:2]
    log_prob = logits_ref[...] - student_lse
    log_gap = log_prob - (teacher_ref[...] - teacher_lse)
    grad = (terms_ref[:, 5:6] * jnp.exp(log_prob) * (log_gap - terms_ref[:, 2:3])).astype(bf16)
    copies = []
    for p in range(parts):
        block = slice(p * size, (p + 1) * size)
        features = jnp.concatenate([low_ref[:, block], high_ref[:, block]], axis=0)
        held[block, :] = lax.dot_general(
            features, grad, (((0,), (0,)), ((), ())), preferred_element_type=f32
        ).astype(bf16)
        rows = pl.ds(p * size, size)
        copies.append(pltpu.make_async_copy(held.at[rows], out_ref.at[rows], sems.at[p]))
        copies[-1].start()
    for copy in copies:
        copy.wait()


def finish_kernel(hidden_ref, gain_ref, shares_ref, out_ref):
    widened = hidden_ref[...].astype(f32)
    inv_rms = lax.rsqrt(jnp.mean(widened * widened, axis=1, keepdims=True) + epsilon)
    normed = widened * inv_rms
    feature_grad = shares_ref[0].astype(f32)
    for p in range(1, shares_ref.shape[0]):
        feature_grad += shares_ref[p].astype(f32)
    norm_grad = feature_grad * gain_ref[...]
    mean = jnp.mean(norm_grad * normed, axis=1, keepdims=True)
    out_ref[...] = (inv_rms * (norm_grad - normed * mean)).astype(bf16)


def shards(hidden, norm_gain, head_weight, teacher_logits, teacher_slot, valid_tokens):
    n_seq, n_row = lax.axis_size("seq"), lax.axis_size("row")
    chips = n_seq * n_row
    count = chips * 2
    own, depth = hidden.shape
    width = head_weight.shape[1]
    rows = own * count
    cap = teacher_logits.shape[0]
    columns = depth // 2
    gain = norm_gain[None]
    masks = [1 << b for b in reversed(range(count.bit_length() - 1))]
    seq_masks = [m for m in reversed(masks) if m >= n_row * 2]

    def swap(value, mask):
        return lax.ppermute(value, axes, [(i, i ^ mask) for i in range(count)])

    def sems(number):
        return pltpu.SemaphoreType.DMA((number,))

    (gathered,) = call(
        features_kernel,
        "features",
        [shape((own, depth), bf16)],
        [hidden, gain],
        [far] * 2,
        [fast],
        [pltpu.VMEM((own, depth), bf16), pltpu.VMEM((1, depth), f32), sems(2)],
    )
    half_blocks = shape((n_seq // 2, cap, width), bf16)
    keep, send = call(
        teacher_kernel,
        "teacher_blocks",
        [half_blocks] * 2,
        [teacher_logits.transpose(1, 0, 2)],
        [fast],
        [fast] * 2,
    )
    held = jnp.concatenate([keep, swap(send, seq_masks[0])], axis=1)
    behind = len(masks) - len(seq_masks)
    for step, mask in enumerate(masks[:-1]):
        arrived = swap(gathered, mask)
        bit = step - behind + 1
        if 1 <= bit < len(seq_masks):
            pairs = held.reshape((held.shape[0] // 2, 2) + held.shape[1:])
            held = jnp.concatenate([pairs[:, 0], swap(pairs[:, 1], seq_masks[bit])], axis=1)
        gathered = jnp.concatenate([gathered, arrived], axis=0)
    low, held = lax.optimization_barrier((gathered, held))
    high = swap(low, masks[-1])

    def with_masks(kernel, *more):
        return lambda *refs: kernel(masks, own, *more, *refs)

    square = shape((rows, width), f32)
    logits, teacher, local, stats = call(
        with_masks(logits_kernel, cap),
        "logits",
        [square, square, shape((rows, 128), f32), shape((count, 4, 2 * rows), f32)],
        [low, high, head_weight, held[0], teacher_slot[None]],
        [fast] * 5,
        [fast] * 4,
        flops=2 * rows * depth * width,
    )
    stats = lax.all_to_all(stats, axes, split_axis=0, concat_axis=0, tiled=True)

    gaps, shifted = call(
        products_kernel,
        "products",
        [shape((rows, depth), f32)] * 2,
        [logits, teacher, local, head_weight],
        [fast] * 4,
        [fast] * 2,
        flops=4 * rows * depth * width,
    )
    half = shape((rows // 2, depth), f32)
    send, terms = call(
        with_masks(send_kernel),
        "send_half",
        [half, shape((rows, 128), f32)],
        [stats, valid_tokens[None], gaps, shifted],
        [fast] * 4,
        [fast] * 2,
    )
    (keep,) = call(keep_kernel, "keep_half", [half], [terms, gaps, shifted], [fast] * 3, [fast])
    (share,) = call(
        with_masks(share_kernel),
        "share",
        [shape((chips, own, depth), bf16)],
        [keep, swap(send, masks[-1])],
        [fast] * 2,
        [fast],
    )
    terms, share = lax.optimization_barrier((terms, share))
    shares = lax.all_to_all(share, ("seq", "row"), split_axis=0, concat_axis=0, tiled=True)
    (grad_head,) = call(
        head_kernel,
        "grad_head",
        [shape(head_weight.shape, bf16)],
        [low, high, logits, teacher, terms],
        [fast] * 5,
        [far],
        [pltpu.VMEM((depth, width), bf16), sems(5)],
        flops=2 * rows * depth * width,
    )
    (grad_hidden,) = call(
        finish_kernel,
        "finish",
        [shape((own, depth), bf16)],
        [hidden, gain, shares],
        [fast] * 3,
        [fast],
    )
    return (grad_hidden, grad_head)


def solution(mesh):
    n_seq, n_vocab = mesh.shape["seq"], mesh.shape["vocab"]
    finer = jax.sharding.Mesh(mesh.devices.reshape(n_seq, n_vocab // 2, 2), axes)
    placed = (
        P(axes, None),
        P(),
        P(None, axes),
        P("seq", None, ("row", "core")),
        P(),
        P(),
    )
    return jax.shard_map(
        shards,
        mesh=finer,
        in_specs=placed,
        out_specs=(P(axes, None), P(None, axes)),
        check_vma=False,
    )
```

```python
import math

import jax
import jax.numpy as jnp
from jax import lax
from jax.experimental import pallas as pl
from jax.experimental.pallas import tpu as pltpu
from jax.sharding import PartitionSpec as P

epsilon = 1e-06
axes = ("seq", "row", "core")
fast, far = pltpu.VMEM, pl.ANY
shape = jax.ShapeDtypeStruct
f32, bf16 = jnp.float32, jnp.bfloat16


def call(kernel, name, out_shape, inputs, spaces, out_spaces, scratch=(), flops=0):
    def size(leaf):
        return leaf.size * leaf.dtype.itemsize

    near = [x for x, s in zip(inputs, spaces) if s == fast]
    near += [x for x, s in zip(out_shape, out_spaces) if s == fast]
    held = sum(x.dtype.itemsize * math.prod(x.shape) for x in scratch if x.memory_space == fast)
    return pl.pallas_call(
        kernel,
        out_shape=list(out_shape),
        in_specs=[pl.BlockSpec(memory_space=s) for s in spaces],
        out_specs=[pl.BlockSpec(memory_space=s) for s in out_spaces],
        scratch_shapes=list(scratch),
        compiler_params=pltpu.CompilerParams(
            vmem_limit_bytes=2 * sum(map(size, near)) + held + (8 << 20)
        ),
        cost_estimate=pl.CostEstimate(
            flops=flops,
            bytes_accessed=sum(map(size, list(inputs) + list(out_shape))),
            transcendentals=0,
        ),
        name=name,
    )(*inputs)


def split_evenly(total, unit):
    parts = max(p for p in (1, 2, 4, 5) if total % (p * unit) == 0)
    return parts, total // parts


def my_index():
    return (lax.axis_index("seq") * lax.axis_size("row") + lax.axis_index("row")) * 2 + lax.axis_index("core")


def exchange(value, masks, own, me):
    length = value.shape[0]
    row = lax.broadcasted_iota(jnp.int32, value.shape, 0)
    for bit, mask in enumerate(masks):
        size = own << bit
        if size >= 8:
            parts = [value[i : i + size] for i in range(0, length, size)]
            other = jnp.concatenate([parts[i ^ 1] for i in range(len(parts))], axis=0)
        else:
            later, earlier = pltpu.roll(value, length - size, 0), pltpu.roll(value, size, 0)
            other = jnp.where((row & size) == 0, later, earlier)
        value = jnp.where((me & mask) != 0, other, value)
    return value


def own_order(row_values, masks, own, me):
    rows = row_values.shape[1]
    place = lax.broadcasted_iota(jnp.int32, (rows, rows), 0)
    block, inner = lax.div(place, own), lax.rem(place, own)
    device = jnp.full((rows, rows), me, jnp.int32)
    for bit, mask in enumerate(masks):
        device = device ^ (((block >> bit) & 1) * mask)
    match = device * own + inner == lax.broadcasted_iota(jnp.int32, (rows, rows), 1)
    return jnp.sum(jnp.where(match, row_values.astype(f32), 0.0), axis=1, keepdims=True)


def features_kernel(hidden_ref, gain_ref, features_ref, hidden, gain, sems):
    copies = [
        pltpu.make_async_copy(hidden_ref, hidden, sems.at[0]),
        pltpu.make_async_copy(gain_ref, gain, sems.at[1]),
    ]
    for copy in copies:
        copy.start()
    for copy in copies:
        copy.wait()
    widened = hidden[...].astype(f32)
    inv_rms = lax.rsqrt(jnp.mean(widened * widened, axis=1, keepdims=True) + epsilon)
    features_ref[...] = (widened * inv_rms * gain[...]).astype(bf16)


def teacher_kernel(blocks_ref, keep_ref, send_ref):
    my_seq = lax.axis_index("seq")
    for k in range(keep_ref.shape[0]):
        keep_ref[k] = blocks_ref[my_seq ^ (2 * k)]
        send_ref[k] = blocks_ref[my_seq ^ (2 * k + 1)]


def logits_kernel(masks, own, cap, low_ref, high_ref, weight_ref, table_ref, slots_ref, logits_ref, teacher_ref, local_ref, stats_ref):
    me, my_seq = my_index(), lax.axis_index("seq")
    depth = weight_ref.shape[0]
    rows = logits_ref.shape[0]
    parts, size = split_evenly(depth, 256)
    slots = own_order(slots_ref[...], masks, own, me).astype(jnp.int32)
    place = (lax.div(slots, cap) ^ my_seq) * cap + lax.rem(slots, cap)
    pick = (place == lax.broadcasted_iota(jnp.int32, (rows, table_ref.shape[0]), 1)).astype(bf16)
    teacher = jnp.dot(pick, table_ref[...], preferred_element_type=f32)
    teacher_ref[...] = teacher
    teacher_top = jnp.max(teacher, axis=1, keepdims=True)
    teacher_total = jnp.sum(jnp.exp(teacher - teacher_top), axis=1, keepdims=True)
    logits = jnp.zeros(logits_ref.shape, f32)
    for p in range(parts):
        block = slice(p * size, (p + 1) * size)
        features = jnp.concatenate([low_ref[:, block], high_ref[:, block]], axis=0)
        logits += jnp.dot(features, weight_ref[block, :], preferred_element_type=f32)
    logits_ref[...] = logits
    student_top = jnp.max(logits, axis=1, keepdims=True)
    shifted = jnp.exp(logits - student_top)
    student_total = jnp.sum(shifted, axis=1, keepdims=True)
    cross_sum = jnp.sum(shifted * (logits - teacher), axis=1, keepdims=True)
    tops = jnp.concatenate([student_top, teacher_top], axis=0)
    totals = jnp.concatenate([student_total, teacher_total], axis=0)
    crosses = jnp.concatenate([cross_sum, jnp.zeros_like(cross_sum)], axis=0)
    lane = lax.broadcasted_iota(jnp.int32, (2 * rows, 128), 1)
    table = jnp.where(lane == 0, tops, jnp.where(lane == 1, totals, jnp.where(lane == 2, crosses, 0.0)))
    local_ref[...] = table[:rows]
    stats = exchange(table, masks, own, me).T[:4]
    for p in range(stats_ref.shape[0]):
        stats_ref[p] = stats


def products_kernel(logits_ref, teacher_ref, local_ref, weight_ref, gaps_ref, shifted_ref):
    depth = weight_ref.shape[0]
    parts, size = split_evenly(depth, 256)
    logits = logits_ref[...]
    rows = logits.shape[0]
    shifted = jnp.exp(logits - local_ref[:, 0:1])
    center = local_ref[:, 2:3] / local_ref[:, 1:2]
    gaps = shifted * (logits - teacher_ref[...] - center)
    left = jnp.concatenate([gaps.astype(bf16), shifted.astype(bf16)], axis=0)
    for p in range(parts):
        block = slice(p * size, (p + 1) * size)
        product = lax.dot_general(
            left, weight_ref[block, :], (((1,), (1,)), ((), ())), preferred_element_type=f32
        )
        gaps_ref[:, block] = product[:rows]
        shifted_ref[:, block] = product[rows:]


def send_kernel(masks, own, stats_ref, valid_ref, gaps_ref, shifted_ref, out_ref, terms_ref):
    me = my_index()
    rows = valid_ref.shape[1]
    half = rows // 2
    stats = stats_ref[...]
    tops, totals, crosses = stats[:, 0, :], stats[:, 1, :], stats[:, 2, :]
    top = jnp.max(tops, axis=0, keepdims=True)
    scale = jnp.exp(tops - top)
    total = jnp.sum(totals * scale, axis=0, keepdims=True)
    cross = jnp.sum(crosses * scale, axis=0, keepdims=True)
    mine = stats_ref[me]
    table = jnp.concatenate(
        [top, total, cross, mine[0:1], mine[2:3] / mine[1:2], jnp.zeros((123, 2 * rows), f32)], axis=0
    ).T
    table = exchange(table, masks, own, me)
    student_top, teacher_top = table[:rows, 0:1], table[rows:, 0:1]
    student_total, teacher_total = table[:rows, 1:2], table[rows:, 1:2]
    student_lse = student_top + jnp.log(student_total)
    teacher_lse = teacher_top + jnp.log(teacher_total)
    divergence = table[:rows, 2:3] / student_total - student_lse + teacher_lse
    row_weight = own_order(valid_ref[...], masks, own, me)
    scale = row_weight * jnp.exp(table[:rows, 3:4] - student_lse)
    offset = scale * (table[:rows, 4:5] + (teacher_lse - student_lse - divergence))
    lane = lax.broadcasted_iota(jnp.int32, (rows, 128), 1)
    terms = row_weight
    for at, column in enumerate((student_lse, teacher_lse, divergence, scale, offset)):
        terms = jnp.where(lane == at, column, terms)
    terms_ref[...] = terms
    out_ref[...] = scale[half:] * gaps_ref[half:, :] + offset[half:] * shifted_ref[half:, :]


def keep_kernel(terms_ref, gaps_ref, shifted_ref, out_ref):
    half = out_ref.shape[0]
    out_ref[...] = terms_ref[:half, 3:4] * gaps_ref[:half, :] + terms_ref[:half, 4:5] * shifted_ref[:half, :]


def share_kernel(masks, own, keep_ref, arrived_ref, share_ref):
    me = my_index()
    share = (keep_ref[...] + arrived_ref[...]).astype(bf16)
    for p in range(share_ref.shape[0]):
        device = me
        for bit, mask in enumerate(masks[:-1]):
            if p >> bit & 1:
                device = device ^ mask
        share_ref[device >> 1] = share[p * own : (p + 1) * own]


def head_kernel(low_ref, high_ref, logits_ref, teacher_ref, terms_ref, out_ref, held, sems):
    parts, size = split_evenly(out_ref.shape[0], 256)
    student_lse, teacher_lse = terms_ref[:, 0:1], terms_ref[:, 1:2]
    log_prob = logits_ref[...] - student_lse
    log_gap = log_prob - (teacher_ref[...] - teacher_lse)
    grad = (terms_ref[:, 5:6] * jnp.exp(log_prob) * (log_gap - terms_ref[:, 2:3])).astype(bf16)
    copies = []
    for p in range(parts):
        block = slice(p * size, (p + 1) * size)
        features = jnp.concatenate([low_ref[:, block], high_ref[:, block]], axis=0)
        held[block, :] = lax.dot_general(
            features, grad, (((0,), (0,)), ((), ())), preferred_element_type=f32
        ).astype(bf16)
        rows = pl.ds(p * size, size)
        copies.append(pltpu.make_async_copy(held.at[rows], out_ref.at[rows], sems.at[p]))
        copies[-1].start()
    for copy in copies:
        copy.wait()


def finish_kernel(hidden_ref, gain_ref, shares_ref, out_ref):
    widened = hidden_ref[...].astype(f32)
    inv_rms = lax.rsqrt(jnp.mean(widened * widened, axis=1, keepdims=True) + epsilon)
    normed = widened * inv_rms
    feature_grad = shares_ref[0].astype(f32)
    for p in range(1, shares_ref.shape[0]):
        feature_grad += shares_ref[p].astype(f32)
    norm_grad = feature_grad * gain_ref[...]
    mean = jnp.mean(norm_grad * normed, axis=1, keepdims=True)
    out_ref[...] = (inv_rms * (norm_grad - normed * mean)).astype(bf16)


def shards(hidden, norm_gain, head_weight, teacher_logits, teacher_slot, valid_tokens):
    n_seq, n_row = lax.axis_size("seq"), lax.axis_size("row")
    chips = n_seq * n_row
    count = chips * 2
    own, depth = hidden.shape
    width = head_weight.shape[1]
    rows = own * count
    cap = teacher_logits.shape[0]
    columns = depth // 2
    gain = norm_gain[None]
    masks = [1 << b for b in reversed(range(count.bit_length() - 1))]
    seq_masks = [m for m in reversed(masks) if m >= n_row * 2]

    def swap(value, mask):
        return lax.ppermute(value, axes, [(i, i ^ mask) for i in range(count)])

    def sems(number):
        return pltpu.SemaphoreType.DMA((number,))

    (gathered,) = call(
        features_kernel,
        "features",
        [shape((own, depth), bf16)],
        [hidden, gain],
        [far] * 2,
        [fast],
        [pltpu.VMEM((own, depth), bf16), pltpu.VMEM((1, depth), f32), sems(2)],
    )
    half_blocks = shape((n_seq // 2, cap, width), bf16)
    keep, send = call(
        teacher_kernel,
        "teacher_blocks",
        [half_blocks] * 2,
        [teacher_logits.transpose(1, 0, 2)],
        [fast],
        [fast] * 2,
        flops=10**10,
    )
    held = jnp.concatenate([keep, swap(send, seq_masks[0])], axis=1)
    behind = len(masks) - len(seq_masks)
    for step, mask in enumerate(masks[:-1]):
        arrived = swap(gathered, mask)
        bit = step - behind + 1
        if 1 <= bit < len(seq_masks):
            pairs = held.reshape((held.shape[0] // 2, 2) + held.shape[1:])
            held = jnp.concatenate([pairs[:, 0], swap(pairs[:, 1], seq_masks[bit])], axis=1)
        gathered = jnp.concatenate([gathered, arrived], axis=0)
    low, held = lax.optimization_barrier((gathered, held))
    high = swap(low, masks[-1])

    def with_masks(kernel, *more):
        return lambda *refs: kernel(masks, own, *more, *refs)

    square = shape((rows, width), f32)
    logits, teacher, local, stats = call(
        with_masks(logits_kernel, cap),
        "logits",
        [square, square, shape((rows, 128), f32), shape((count, 4, 2 * rows), f32)],
        [low, high, head_weight, held[0], teacher_slot[None]],
        [fast] * 5,
        [fast] * 4,
        flops=2 * rows * depth * width,
    )
    stats = lax.all_to_all(stats, axes, split_axis=0, concat_axis=0, tiled=True)

    gaps, shifted = call(
        products_kernel,
        "products",
        [shape((rows, depth), f32)] * 2,
        [logits, teacher, local, head_weight],
        [fast] * 4,
        [fast] * 2,
        flops=4 * rows * depth * width,
    )
    half = shape((rows // 2, depth), f32)
    send, terms = call(
        with_masks(send_kernel),
        "send_half",
        [half, shape((rows, 128), f32)],
        [stats, valid_tokens[None], gaps, shifted],
        [fast] * 4,
        [fast] * 2,
    )
    (keep,) = call(keep_kernel, "keep_half", [half], [terms, gaps, shifted], [fast] * 3, [fast])
    (share,) = call(
        with_masks(share_kernel),
        "share",
        [shape((chips, own, depth), bf16)],
        [keep, swap(send, masks[-1])],
        [fast] * 2,
        [fast],
    )
    terms, share = lax.optimization_barrier((terms, share))
    shares = lax.all_to_all(share, ("seq", "row"), split_axis=0, concat_axis=0, tiled=True)
    (grad_head,) = call(
        head_kernel,
        "grad_head",
        [shape(head_weight.shape, bf16)],
        [low, high, logits, teacher, terms],
        [fast] * 5,
        [far],
        [pltpu.VMEM((depth, width), bf16), sems(5)],
        flops=2 * rows * depth * width,
    )
    (grad_hidden,) = call(
        finish_kernel,
        "finish",
        [shape((own, depth), bf16)],
        [hidden, gain, shares],
        [fast] * 3,
        [fast],
    )
    return (grad_hidden, grad_head)


def solution(mesh):
    n_seq, n_vocab = mesh.shape["seq"], mesh.shape["vocab"]
    finer = jax.sharding.Mesh(mesh.devices.reshape(n_seq, n_vocab // 2, 2), axes)
    placed = (
        P(axes, None),
        P(),
        P(None, axes),
        P("seq", None, ("row", "core")),
        P(),
        P(),
    )
    return jax.shard_map(
        shards,
        mesh=finer,
        in_specs=placed,
        out_specs=(P(axes, None), P(None, axes)),
        check_vma=False,
    )
```

```python
import math

import jax
import jax.numpy as jnp
from jax import lax
from jax.experimental import pallas as pl
from jax.experimental.pallas import tpu as pltpu
from jax.sharding import PartitionSpec as P

epsilon = 1e-06
axes = ("seq", "row", "core")
fast, far = pltpu.VMEM, pl.ANY
shape = jax.ShapeDtypeStruct
f32, bf16 = jnp.float32, jnp.bfloat16


def call(kernel, name, out_shape, inputs, spaces, out_spaces, scratch=(), flops=0):
    def size(leaf):
        return leaf.size * leaf.dtype.itemsize

    near = [x for x, s in zip(inputs, spaces) if s == fast]
    near += [x for x, s in zip(out_shape, out_spaces) if s == fast]
    held = sum(x.dtype.itemsize * math.prod(x.shape) for x in scratch if x.memory_space == fast)
    return pl.pallas_call(
        kernel,
        out_shape=list(out_shape),
        in_specs=[pl.BlockSpec(memory_space=s) for s in spaces],
        out_specs=[pl.BlockSpec(memory_space=s) for s in out_spaces],
        scratch_shapes=list(scratch),
        compiler_params=pltpu.CompilerParams(
            vmem_limit_bytes=2 * sum(map(size, near)) + held + (8 << 20)
        ),
        cost_estimate=pl.CostEstimate(
            flops=flops,
            bytes_accessed=sum(map(size, list(inputs) + list(out_shape))),
            transcendentals=0,
        ),
        name=name,
    )(*inputs)


def split_evenly(total, unit):
    parts = max(p for p in (1, 2, 4, 5) if total % (p * unit) == 0)
    return parts, total // parts


def my_index():
    return (lax.axis_index("seq") * lax.axis_size("row") + lax.axis_index("row")) * 2 + lax.axis_index("core")


def place_match(rows, masks, own, me):
    place = lax.broadcasted_iota(jnp.int32, (rows, rows), 0)
    block, inner = lax.div(place, own), lax.rem(place, own)
    device = jnp.full((rows, rows), me, jnp.int32)
    for bit, mask in enumerate(masks):
        device = device ^ (((block >> bit) & 1) * mask)
    return device * own + inner == lax.broadcasted_iota(jnp.int32, (rows, rows), 1)


def to_column(match, row_values):
    return jnp.sum(jnp.where(match, row_values, 0.0), axis=1, keepdims=True)


def to_row(match, column):
    return jnp.sum(jnp.where(match, column, 0.0), axis=0, keepdims=True)


def merge(first, second):
    top = jnp.maximum(first[0:1], second[0:1])
    near, far_off = jnp.exp(first[0:1] - top), jnp.exp(second[0:1] - top)
    return top, first[1:2] * near + second[1:2] * far_off, first[2:3] * near + second[2:3] * far_off


def features_kernel(hidden_ref, gain_ref, features_ref, hidden, gain, sems):
    copies = [
        pltpu.make_async_copy(hidden_ref, hidden, sems.at[0]),
        pltpu.make_async_copy(gain_ref, gain, sems.at[1]),
    ]
    for copy in copies:
        copy.start()
    for copy in copies:
        copy.wait()
    widened = hidden[...].astype(f32)
    inv_rms = lax.rsqrt(jnp.mean(widened * widened, axis=1, keepdims=True) + epsilon)
    features_ref[...] = (widened * inv_rms * gain[...]).astype(bf16)


def teacher_kernel(blocks_ref, keep_ref, send_ref):
    my_seq = lax.axis_index("seq")
    for k in range(keep_ref.shape[0]):
        keep_ref[k] = blocks_ref[my_seq ^ (2 * k)]
        send_ref[k] = blocks_ref[my_seq ^ (2 * k + 1)]


def join_kernel(first_ref, second_ref, out_ref):
    length = first_ref.shape[0]
    out_ref[:length, :] = first_ref[...]
    out_ref[length:, :] = second_ref[...]


def logits_kernel(masks, own, cap, low_ref, high_ref, weight_ref, table_ref, slots_ref, logits_ref, teacher_ref, stats_ref):
    my_seq = lax.axis_index("seq")
    rows = logits_ref.shape[0]
    parts, size = split_evenly(weight_ref.shape[0], 256)
    match = place_match(rows, masks, own, my_index())
    slots = to_column(match, slots_ref[...].astype(f32)).astype(jnp.int32)
    place = (lax.div(slots, cap) ^ my_seq) * cap + lax.rem(slots, cap)
    pick = (place == lax.broadcasted_iota(jnp.int32, (rows, table_ref.shape[0]), 1)).astype(bf16)
    teacher = jnp.dot(pick, table_ref[...], preferred_element_type=f32)
    teacher_ref[...] = teacher.astype(bf16)
    teacher_top = jnp.max(teacher, axis=1, keepdims=True)
    teacher_total = jnp.sum(jnp.exp(teacher - teacher_top), axis=1, keepdims=True)
    logits = jnp.zeros(logits_ref.shape, f32)
    for p in range(parts):
        block = slice(p * size, (p + 1) * size)
        features = jnp.concatenate([low_ref[:, block], high_ref[:, block]], axis=0)
        logits += jnp.dot(features, weight_ref[block, :], preferred_element_type=f32)
    logits_ref[...] = logits
    student_top = jnp.max(logits, axis=1, keepdims=True)
    shifted = jnp.exp(logits - student_top)
    student_total = jnp.sum(shifted, axis=1, keepdims=True)
    cross_sum = jnp.sum(shifted * (logits - teacher), axis=1, keepdims=True)
    nothing = jnp.zeros((1, rows), f32)
    pairs = [
        (to_row(match, student_top), to_row(match, teacher_top)),
        (to_row(match, student_total), to_row(match, teacher_total)),
        (to_row(match, cross_sum), nothing),
        (nothing, nothing),
    ]
    stats_ref[...] = jnp.concatenate([jnp.concatenate(p, axis=1) for p in pairs], axis=0)


def products_kernel(masks, own, logits_ref, teacher_ref, mine_ref, theirs_ref, weight_ref, keep_ref, send_ref, stats_ref):
    parts, size = split_evenly(weight_ref.shape[0], 256)
    logits = logits_ref[...]
    rows = logits.shape[0]
    half = rows // 2
    match = place_match(rows, masks, own, my_index())
    top, total, cross = merge(mine_ref[...], theirs_ref[...])
    stats_ref[...] = jnp.concatenate([top, total, cross, jnp.zeros_like(top)], axis=0)
    center = to_column(match, cross[:, :rows] / total[:, :rows])
    shifted = jnp.exp(logits - to_column(match, top[:, :rows]))
    gaps = shifted * (logits - teacher_ref[...].astype(f32) - center)
    pieces = []
    for at in range(0, rows, own):
        pieces += [gaps[at : at + own], shifted[at : at + own]]
    left = jnp.concatenate(pieces, axis=0).astype(bf16)
    for p in range(parts):
        block = slice(p * size, (p + 1) * size)
        product = lax.dot_general(
            left, weight_ref[block, :], (((1,), (1,)), ((), ())), preferred_element_type=f32
        )
        keep_ref[:, block] = product[: 2 * half]
        send_ref[:, block] = product[2 * half :].astype(bf16)


def share_kernel(masks, own, keep_ref, arrived_ref, share_ref):
    me = my_index()
    share = (keep_ref[...] + arrived_ref[...].astype(f32)).astype(bf16)
    for p in range(share_ref.shape[0]):
        device = me
        for bit, mask in enumerate(masks[:-1]):
            if p >> bit & 1:
                device = device ^ mask
        share_ref[device >> 1] = share[p * 2 * own : (p + 1) * 2 * own]


def spread_kernel(value_ref, out_ref):
    for p in range(out_ref.shape[0]):
        out_ref[p] = value_ref[...]


def terms_kernel(masks, own, stats_ref, valid_ref, terms_ref, factors_ref):
    me = my_index()
    rows = valid_ref.shape[1]
    stats = stats_ref[...]
    tops, totals, crosses = stats[:, 0, :], stats[:, 1, :], stats[:, 2, :]
    top = jnp.max(tops, axis=0, keepdims=True)
    scale = jnp.exp(tops - top)
    total = jnp.sum(totals * scale, axis=0, keepdims=True)
    cross = jnp.sum(crosses * scale, axis=0, keepdims=True)[:, :rows]
    lse = top + jnp.log(total)
    student_lse, teacher_lse = lse[:, :rows], lse[:, rows:]
    divergence = cross / total[:, :rows] - student_lse + teacher_lse
    row_weight = valid_ref[...].astype(f32)
    match = place_match(rows, masks, own, me)
    lane = lax.broadcasted_iota(jnp.int32, (rows, 128), 1)
    terms = to_column(match, row_weight)
    for at, values in enumerate((student_lse, teacher_lse, divergence)):
        terms = jnp.where(lane == at, to_column(match, values), terms)
    terms_ref[...] = terms
    scale = row_weight * jnp.exp(tops[:, :rows] - student_lse)
    offset = scale * (crosses[:, :rows] / totals[:, :rows] + (teacher_lse - student_lse - divergence))
    pick = lax.broadcasted_iota(jnp.int32, (2 * own, rows), 0)
    mine = lax.broadcasted_iota(jnp.int32, (2 * own, rows), 1) == me * own + lax.rem(pick, own)
    for p in range(factors_ref.shape[0]):
        both = jnp.where(pick < own, scale[p : p + 1], offset[p : p + 1])
        column = jnp.sum(jnp.where(mine, both, 0.0), axis=1, keepdims=True)
        factors_ref[p] = jnp.broadcast_to(column, factors_ref.shape[1:])


def head_kernel(low_ref, high_ref, logits_ref, teacher_ref, terms_ref, out_ref, held, sems):
    parts, size = split_evenly(out_ref.shape[0], 256)
    student_lse, teacher_lse = terms_ref[:, 0:1], terms_ref[:, 1:2]
    log_prob = logits_ref[...] - student_lse
    log_gap = log_prob - (teacher_ref[...].astype(f32) - teacher_lse)
    grad = (terms_ref[:, 3:4] * jnp.exp(log_prob) * (log_gap - terms_ref[:, 2:3])).astype(bf16)
    copies = []
    for p in range(parts):
        block = slice(p * size, (p + 1) * size)
        features = jnp.concatenate([low_ref[:, block], high_ref[:, block]], axis=0)
        held[block, :] = lax.dot_general(
            features, grad, (((0,), (0,)), ((), ())), preferred_element_type=f32
        ).astype(bf16)
        rows = pl.ds(p * size, size)
        copies.append(pltpu.make_async_copy(held.at[rows], out_ref.at[rows], sems.at[p]))
        copies[-1].start()
    for copy in copies:
        copy.wait()


def finish_kernel(hidden_ref, gain_ref, shares_ref, factors_ref, out_ref):
    own = hidden_ref.shape[0]
    widened = hidden_ref[...].astype(f32)
    inv_rms = lax.rsqrt(jnp.mean(widened * widened, axis=1, keepdims=True) + epsilon)
    normed = widened * inv_rms
    both = shares_ref[0].astype(f32) * factors_ref[0][:, 0:1]
    for p in range(1, shares_ref.shape[0]):
        both += shares_ref[p].astype(f32) * factors_ref[p][:, 0:1]
    norm_grad = (both[:own] + both[own:]) * gain_ref[...]
    mean = jnp.mean(norm_grad * normed, axis=1, keepdims=True)
    out_ref[...] = (inv_rms * (norm_grad - normed * mean)).astype(bf16)


def shards(hidden, norm_gain, head_weight, teacher_logits, teacher_slot, valid_tokens):
    n_seq, n_row = lax.axis_size("seq"), lax.axis_size("row")
    chips = n_seq * n_row
    count = chips * 2
    own, depth = hidden.shape
    width = head_weight.shape[1]
    rows = own * count
    cap = teacher_logits.shape[0]
    columns = depth // 2
    gain = norm_gain[None]
    masks = [1 << b for b in reversed(range(count.bit_length() - 1))]
    seq_masks = [m for m in reversed(masks) if m >= n_row * 2]

    def swap(value, mask):
        return lax.ppermute(value, axes, [(i, i ^ mask) for i in range(count)])

    def sems(number):
        return pltpu.SemaphoreType.DMA((number,))

    (gathered,) = call(
        features_kernel,
        "features",
        [shape((own, depth), bf16)],
        [hidden, gain],
        [far] * 2,
        [fast],
        [pltpu.VMEM((own, depth), bf16), pltpu.VMEM((1, depth), f32), sems(2)],
    )
    half_blocks = shape((n_seq // 2, cap, width), bf16)
    keep, send = call(
        teacher_kernel,
        "teacher_blocks",
        [half_blocks] * 2,
        [teacher_logits.transpose(1, 0, 2)],
        [fast],
        [fast] * 2,
        flops=10**10,
    )
    held = jnp.concatenate([keep, swap(send, seq_masks[0])], axis=1)
    behind = len(masks) - len(seq_masks)
    for step, mask in enumerate(masks[:-1]):
        arrived = swap(gathered, mask)
        bit = step - behind + 1
        if 1 <= bit < len(seq_masks):
            pairs = held.reshape((held.shape[0] // 2, 2) + held.shape[1:])
            held = jnp.concatenate([pairs[:, 0], swap(pairs[:, 1], seq_masks[bit])], axis=1)
        if step < len(masks) - 2:
            gathered = jnp.concatenate([gathered, arrived], axis=0)
    (gathered,) = call(
        join_kernel, "join", [shape((rows // 2, depth), bf16)], [gathered, arrived], [fast] * 2, [fast]
    )
    low, held = lax.optimization_barrier((gathered, held))
    high = swap(low, masks[-1])

    def with_masks(kernel, *more):
        return lambda *refs: kernel(masks, own, *more, *refs)

    logits, teacher, stats = call(
        with_masks(logits_kernel, cap),
        "logits",
        [shape((rows, width), f32), shape((rows, width), bf16), shape((4, 2 * rows), f32)],
        [low, high, head_weight, held[0], teacher_slot[None]],
        [fast] * 5,
        [fast] * 3,
        flops=2 * rows * depth * width,
    )
    keep, send, stats = call(
        with_masks(products_kernel),
        "products",
        [shape((rows, depth), f32), shape((rows, depth), bf16), shape((4, 2 * rows), f32)],
        [logits, teacher, stats, swap(stats, masks[-1]), head_weight],
        [fast] * 5,
        [fast] * 3,
        flops=4 * rows * depth * width,
    )
    (share,) = call(
        with_masks(share_kernel),
        "share",
        [shape((chips, 2 * own, depth), bf16)],
        [keep, swap(send, masks[-1])],
        [fast] * 2,
        [fast],
    )
    stats, share = lax.optimization_barrier((stats, share))
    shares = lax.all_to_all(share, ("seq", "row"), split_axis=0, concat_axis=0, tiled=True)
    (stats,) = call(
        spread_kernel, "spread", [shape((chips, 4, 2 * rows), f32)], [stats], [fast], [fast]
    )
    stats = lax.all_to_all(stats, ("seq", "row"), split_axis=0, concat_axis=0, tiled=True)
    terms, factors = call(
        with_masks(terms_kernel),
        "terms",
        [shape((rows, 128), f32), shape((chips, 2 * own, 128), f32)],
        [stats, valid_tokens[None]],
        [fast] * 2,
        [fast] * 2,
    )
    (grad_head,) = call(
        head_kernel,
        "grad_head",
        [shape(head_weight.shape, bf16)],
        [low, high, logits, teacher, terms],
        [fast] * 5,
        [far],
        [pltpu.VMEM((depth, width), bf16), sems(5)],
        flops=2 * rows * depth * width,
    )
    (grad_hidden,) = call(
        finish_kernel,
        "finish",
        [shape((own, depth), bf16)],
        [hidden, gain, shares, factors],
        [fast] * 4,
        [fast],
    )
    return (grad_hidden, grad_head)


def solution(mesh):
    n_seq, n_vocab = mesh.shape["seq"], mesh.shape["vocab"]
    finer = jax.sharding.Mesh(mesh.devices.reshape(n_seq, n_vocab // 2, 2), axes)
    placed = (
        P(axes, None),
        P(),
        P(None, axes),
        P("seq", None, ("row", "core")),
        P(),
        P(),
    )
    return jax.shard_map(
        shards,
        mesh=finer,
        in_specs=placed,
        out_specs=(P(axes, None), P(None, axes)),
        check_vma=False,
    )
```

```python
import math

import jax
import jax.numpy as jnp
from jax import lax
from jax.experimental import pallas as pl
from jax.experimental.pallas import tpu as pltpu
from jax.sharding import PartitionSpec as P

epsilon = 1e-06
axes = ("seq", "row", "core")
fast, far = pltpu.VMEM, pl.ANY
shape = jax.ShapeDtypeStruct
f32, bf16 = jnp.float32, jnp.bfloat16


def call(kernel, name, out_shape, inputs, spaces, out_spaces, scratch=(), flops=0, light=False):
    def size(leaf):
        return leaf.size * leaf.dtype.itemsize

    near = [x for x, s in zip(inputs, spaces) if s == fast]
    near += [x for x, s in zip(out_shape, out_spaces) if s == fast]
    held = sum(x.dtype.itemsize * math.prod(x.shape) for x in scratch if x.memory_space == fast)
    return pl.pallas_call(
        kernel,
        out_shape=list(out_shape),
        in_specs=[pl.BlockSpec(memory_space=s) for s in spaces],
        out_specs=[pl.BlockSpec(memory_space=s) for s in out_spaces],
        scratch_shapes=list(scratch),
        compiler_params=pltpu.CompilerParams(
            vmem_limit_bytes=2 * sum(map(size, near)) + held + (8 << 20)
        ),
        cost_estimate=pl.CostEstimate(
            flops=flops,
            bytes_accessed=0 if light else sum(map(size, list(inputs) + list(out_shape))),
            transcendentals=0,
        ),
        name=name,
    )(*inputs)


def split_evenly(total, unit):
    parts = max(p for p in (1, 2, 4, 5) if total % (p * unit) == 0)
    return parts, total // parts


def my_index():
    return (lax.axis_index("seq") * lax.axis_size("row") + lax.axis_index("row")) * 2 + lax.axis_index("core")


def place_match(rows, masks, own, me):
    place = lax.broadcasted_iota(jnp.int32, (rows, rows), 0)
    block, inner = lax.div(place, own), lax.rem(place, own)
    device = jnp.full((rows, rows), me, jnp.int32)
    for bit, mask in enumerate(masks):
        device = device ^ (((block >> bit) & 1) * mask)
    return device * own + inner == lax.broadcasted_iota(jnp.int32, (rows, rows), 1)


def to_column(match, row_values):
    return jnp.sum(jnp.where(match, row_values, 0.0), axis=1, keepdims=True)


def to_row(match, column):
    return jnp.sum(jnp.where(match, column, 0.0), axis=0, keepdims=True)


def merge(first, second):
    top = jnp.maximum(first[0:1], second[0:1])
    near, far_off = jnp.exp(first[0:1] - top), jnp.exp(second[0:1] - top)
    return top, first[1:2] * near + second[1:2] * far_off, first[2:3] * near + second[2:3] * far_off


def features_kernel(hidden_ref, gain_ref, features_ref, hidden, gain, sems):
    copies = [
        pltpu.make_async_copy(hidden_ref, hidden, sems.at[0]),
        pltpu.make_async_copy(gain_ref, gain, sems.at[1]),
    ]
    for copy in copies:
        copy.start()
    for copy in copies:
        copy.wait()
    widened = hidden[...].astype(f32)
    inv_rms = lax.rsqrt(jnp.mean(widened * widened, axis=1, keepdims=True) + epsilon)
    features_ref[...] = (widened * inv_rms * gain[...]).astype(bf16)


def teacher_kernel(blocks_ref, keep_ref, send_ref):
    my_seq = lax.axis_index("seq")
    for k in range(keep_ref.shape[0]):
        keep_ref[k] = blocks_ref[my_seq ^ (2 * k)]
        send_ref[k] = blocks_ref[my_seq ^ (2 * k + 1)]


def join_kernel(first_ref, second_ref, out_ref):
    length = first_ref.shape[0]
    out_ref[:length, :] = first_ref[...]
    out_ref[length:, :] = second_ref[...]


def logits_kernel(masks, own, cap, low_ref, high_ref, weight_ref, table_ref, slots_ref, logits_ref, teacher_ref, stats_ref):
    my_seq = lax.axis_index("seq")
    rows = logits_ref.shape[0]
    parts, size = split_evenly(weight_ref.shape[0], 256)
    match = place_match(rows, masks, own, my_index())
    slots = to_column(match, slots_ref[...].astype(f32)).astype(jnp.int32)
    place = (lax.div(slots, cap) ^ my_seq) * cap + lax.rem(slots, cap)
    pick = (place == lax.broadcasted_iota(jnp.int32, (rows, table_ref.shape[0]), 1)).astype(bf16)
    teacher = jnp.dot(pick, table_ref[...], preferred_element_type=f32)
    teacher_ref[...] = teacher.astype(bf16)
    teacher_top = jnp.max(teacher, axis=1, keepdims=True)
    teacher_total = jnp.sum(jnp.exp(teacher - teacher_top), axis=1, keepdims=True)
    logits = jnp.zeros(logits_ref.shape, f32)
    for p in range(parts):
        block = slice(p * size, (p + 1) * size)
        features = jnp.concatenate([low_ref[:, block], high_ref[:, block]], axis=0)
        logits += jnp.dot(features, weight_ref[block, :], preferred_element_type=f32)
    logits_ref[...] = logits
    student_top = jnp.max(logits, axis=1, keepdims=True)
    shifted = jnp.exp(logits - student_top)
    student_total = jnp.sum(shifted, axis=1, keepdims=True)
    cross_sum = jnp.sum(shifted * (logits - teacher), axis=1, keepdims=True)
    nothing = jnp.zeros((1, rows), f32)
    pairs = [
        (to_row(match, student_top), to_row(match, teacher_top)),
        (to_row(match, student_total), to_row(match, teacher_total)),
        (to_row(match, cross_sum), nothing),
        (nothing, nothing),
    ]
    stats_ref[...] = jnp.concatenate([jnp.concatenate(p, axis=1) for p in pairs], axis=0)


def products_kernel(masks, own, logits_ref, teacher_ref, mine_ref, theirs_ref, weight_ref, keep_ref, send_ref, stats_ref):
    parts, size = split_evenly(weight_ref.shape[0], 256)
    logits = logits_ref[...]
    rows = logits.shape[0]
    half = rows // 2
    match = place_match(rows, masks, own, my_index())
    top, total, cross = merge(mine_ref[...], theirs_ref[...])
    stats_ref[...] = jnp.concatenate([top, total, cross, jnp.zeros_like(top)], axis=0)
    center = to_column(match, cross[:, :rows] / total[:, :rows])
    shifted = jnp.exp(logits - to_column(match, top[:, :rows]))
    gaps = shifted * (logits - teacher_ref[...].astype(f32) - center)
    pieces = []
    for at in range(0, rows, own):
        pieces += [gaps[at : at + own], shifted[at : at + own]]
    left = jnp.concatenate(pieces, axis=0).astype(bf16)
    for p in range(parts):
        block = slice(p * size, (p + 1) * size)
        product = lax.dot_general(
            left, weight_ref[block, :], (((1,), (1,)), ((), ())), preferred_element_type=f32
        )
        keep_ref[:, block] = product[: 2 * half]
        send_ref[:, block] = product[2 * half :].astype(bf16)


def share_kernel(masks, own, keep_ref, arrived_ref, share_ref):
    me = my_index()
    share = (keep_ref[...] + arrived_ref[...].astype(f32)).astype(bf16)
    for p in range(share_ref.shape[0]):
        device = me
        for bit, mask in enumerate(masks[:-1]):
            if p >> bit & 1:
                device = device ^ mask
        share_ref[device >> 1] = share[p * 2 * own : (p + 1) * 2 * own]


def spread_kernel(value_ref, out_ref):
    for p in range(out_ref.shape[0]):
        out_ref[p] = value_ref[...]


def terms_kernel(masks, own, stats_ref, valid_ref, terms_ref, factors_ref):
    me = my_index()
    rows = valid_ref.shape[1]
    stats = stats_ref[...]
    tops, totals, crosses = stats[:, 0, :], stats[:, 1, :], stats[:, 2, :]
    top = jnp.max(tops, axis=0, keepdims=True)
    scale = jnp.exp(tops - top)
    total = jnp.sum(totals * scale, axis=0, keepdims=True)
    cross = jnp.sum(crosses * scale, axis=0, keepdims=True)[:, :rows]
    lse = top + jnp.log(total)
    student_lse, teacher_lse = lse[:, :rows], lse[:, rows:]
    divergence = cross / total[:, :rows] - student_lse + teacher_lse
    row_weight = valid_ref[...].astype(f32)
    match = place_match(rows, masks, own, me)
    lane = lax.broadcasted_iota(jnp.int32, (rows, 128), 1)
    terms = to_column(match, row_weight)
    for at, values in enumerate((student_lse, teacher_lse, divergence)):
        terms = jnp.where(lane == at, to_column(match, values), terms)
    terms_ref[...] = terms
    scale = row_weight * jnp.exp(tops[:, :rows] - student_lse)
    offset = scale * (crosses[:, :rows] / totals[:, :rows] + (teacher_lse - student_lse - divergence))
    pick = lax.broadcasted_iota(jnp.int32, (2 * own, rows), 0)
    mine = lax.broadcasted_iota(jnp.int32, (2 * own, rows), 1) == me * own + lax.rem(pick, own)
    for p in range(factors_ref.shape[0]):
        both = jnp.where(pick < own, scale[p : p + 1], offset[p : p + 1])
        column = jnp.sum(jnp.where(mine, both, 0.0), axis=1, keepdims=True)
        factors_ref[p] = jnp.broadcast_to(column, factors_ref.shape[1:])


def head_kernel(low_ref, high_ref, logits_ref, teacher_ref, terms_ref, out_ref, held, sems):
    parts, size = split_evenly(out_ref.shape[0], 256)
    student_lse, teacher_lse = terms_ref[:, 0:1], terms_ref[:, 1:2]
    log_prob = logits_ref[...] - student_lse
    log_gap = log_prob - (teacher_ref[...].astype(f32) - teacher_lse)
    grad = (terms_ref[:, 3:4] * jnp.exp(log_prob) * (log_gap - terms_ref[:, 2:3])).astype(bf16)
    copies = []
    for p in range(parts):
        block = slice(p * size, (p + 1) * size)
        features = jnp.concatenate([low_ref[:, block], high_ref[:, block]], axis=0)
        held[block, :] = lax.dot_general(
            features, grad, (((0,), (0,)), ((), ())), preferred_element_type=f32
        ).astype(bf16)
        rows = pl.ds(p * size, size)
        copies.append(pltpu.make_async_copy(held.at[rows], out_ref.at[rows], sems.at[p]))
        copies[-1].start()
    for copy in copies:
        copy.wait()


def finish_kernel(hidden_ref, gain_ref, shares_ref, factors_ref, out_ref):
    own = hidden_ref.shape[0]
    widened = hidden_ref[...].astype(f32)
    inv_rms = lax.rsqrt(jnp.mean(widened * widened, axis=1, keepdims=True) + epsilon)
    normed = widened * inv_rms
    both = shares_ref[0].astype(f32) * factors_ref[0][:, 0:1]
    for p in range(1, shares_ref.shape[0]):
        both += shares_ref[p].astype(f32) * factors_ref[p][:, 0:1]
    norm_grad = (both[:own] + both[own:]) * gain_ref[...]
    mean = jnp.mean(norm_grad * normed, axis=1, keepdims=True)
    out_ref[...] = (inv_rms * (norm_grad - normed * mean)).astype(bf16)


def shards(hidden, norm_gain, head_weight, teacher_logits, teacher_slot, valid_tokens):
    n_seq, n_row = lax.axis_size("seq"), lax.axis_size("row")
    chips = n_seq * n_row
    count = chips * 2
    own, depth = hidden.shape
    width = head_weight.shape[1]
    rows = own * count
    cap = teacher_logits.shape[0]
    columns = depth // 2
    gain = norm_gain[None]
    masks = [1 << b for b in reversed(range(count.bit_length() - 1))]
    seq_masks = [m for m in reversed(masks) if m >= n_row * 2]

    def swap(value, mask):
        return lax.ppermute(value, axes, [(i, i ^ mask) for i in range(count)])

    def sems(number):
        return pltpu.SemaphoreType.DMA((number,))

    (gathered,) = call(
        features_kernel,
        "features",
        [shape((own, depth), bf16)],
        [hidden, gain],
        [far] * 2,
        [fast],
        [pltpu.VMEM((own, depth), bf16), pltpu.VMEM((1, depth), f32), sems(2)],
    )
    half_blocks = shape((n_seq // 2, cap, width), bf16)
    keep, send = call(
        teacher_kernel,
        "teacher_blocks",
        [half_blocks] * 2,
        [teacher_logits.transpose(1, 0, 2)],
        [fast],
        [fast] * 2,
        flops=10**10,
    )
    held = jnp.concatenate([keep, swap(send, seq_masks[0])], axis=1)
    behind = len(masks) - len(seq_masks)
    for step, mask in enumerate(masks[:-1]):
        arrived = swap(gathered, mask)
        bit = step - behind + 1
        if 1 <= bit < len(seq_masks):
            pairs = held.reshape((held.shape[0] // 2, 2) + held.shape[1:])
            held = jnp.concatenate([pairs[:, 0], swap(pairs[:, 1], seq_masks[bit])], axis=1)
        if step < len(masks) - 2:
            gathered = jnp.concatenate([gathered, arrived], axis=0)
    (gathered,) = call(
        join_kernel, "join", [shape((rows // 2, depth), bf16)], [gathered, arrived], [fast] * 2, [fast]
    )
    low, held = lax.optimization_barrier((gathered, held))
    high = swap(low, masks[-1])

    def with_masks(kernel, *more):
        return lambda *refs: kernel(masks, own, *more, *refs)

    logits, teacher, stats = call(
        with_masks(logits_kernel, cap),
        "logits",
        [shape((rows, width), f32), shape((rows, width), bf16), shape((4, 2 * rows), f32)],
        [low, high, head_weight, held[0], teacher_slot[None]],
        [fast] * 5,
        [fast] * 3,
        flops=2 * rows * depth * width,
    )
    keep, send, stats = call(
        with_masks(products_kernel),
        "products",
        [shape((rows, depth), f32), shape((rows, depth), bf16), shape((4, 2 * rows), f32)],
        [logits, teacher, stats, swap(stats, masks[-1]), head_weight],
        [fast] * 5,
        [fast] * 3,
        flops=4 * rows * depth * width,
    )
    (share,) = call(
        with_masks(share_kernel),
        "share",
        [shape((chips, 2 * own, depth), bf16)],
        [keep, swap(send, masks[-1])],
        [fast] * 2,
        [fast],
    )
    shares = lax.all_to_all(share, ("seq", "row"), split_axis=0, concat_axis=0, tiled=True)
    (stats,) = call(
        spread_kernel, "spread", [shape((chips, 4, 2 * rows), f32)], [stats], [fast], [fast]
    )
    stats = lax.all_to_all(stats, ("seq", "row"), split_axis=0, concat_axis=0, tiled=True)
    terms, factors = call(
        with_masks(terms_kernel),
        "terms",
        [shape((rows, 128), f32), shape((chips, 2 * own, 128), f32)],
        [stats, valid_tokens[None]],
        [fast] * 2,
        [fast] * 2,
        light=True,
    )
    (grad_head,) = call(
        head_kernel,
        "grad_head",
        [shape(head_weight.shape, bf16)],
        [low, high, logits, teacher, terms],
        [fast] * 5,
        [far],
        [pltpu.VMEM((depth, width), bf16), sems(5)],
        light=True,
    )
    (grad_hidden,) = call(
        finish_kernel,
        "finish",
        [shape((own, depth), bf16)],
        [hidden, gain, shares, factors],
        [fast] * 4,
        [fast],
    )
    return (grad_hidden, grad_head)


def solution(mesh):
    n_seq, n_vocab = mesh.shape["seq"], mesh.shape["vocab"]
    finer = jax.sharding.Mesh(mesh.devices.reshape(n_seq, n_vocab // 2, 2), axes)
    placed = (
        P(axes, None),
        P(),
        P(None, axes),
        P("seq", None, ("row", "core")),
        P(),
        P(),
    )
    return jax.shard_map(
        shards,
        mesh=finer,
        in_specs=placed,
        out_specs=(P(axes, None), P(None, axes)),
        check_vma=False,
    )
```

```python
import math

import jax
import jax.numpy as jnp
from jax import lax
from jax.experimental import pallas as pl
from jax.experimental.pallas import tpu as pltpu
from jax.sharding import PartitionSpec as P

epsilon = 1e-06
axes = ("seq", "row", "core")
fast, far = pltpu.VMEM, pl.ANY
shape = jax.ShapeDtypeStruct
f32, bf16 = jnp.float32, jnp.bfloat16


def call(kernel, name, out_shape, inputs, spaces, out_spaces, scratch=(), flops=0, light=False):
    def size(leaf):
        return leaf.size * leaf.dtype.itemsize

    near = [x for x, s in zip(inputs, spaces) if s == fast]
    near += [x for x, s in zip(out_shape, out_spaces) if s == fast]
    held = sum(x.dtype.itemsize * math.prod(x.shape) for x in scratch if x.memory_space == fast)
    return pl.pallas_call(
        kernel,
        out_shape=list(out_shape),
        in_specs=[pl.BlockSpec(memory_space=s) for s in spaces],
        out_specs=[pl.BlockSpec(memory_space=s) for s in out_spaces],
        scratch_shapes=list(scratch),
        compiler_params=pltpu.CompilerParams(
            vmem_limit_bytes=2 * sum(map(size, near)) + held + (8 << 20)
        ),
        cost_estimate=pl.CostEstimate(
            flops=flops,
            bytes_accessed=0 if light else sum(map(size, list(inputs) + list(out_shape))),
            transcendentals=0,
        ),
        name=name,
    )(*inputs)


def split_evenly(total, unit):
    parts = max(p for p in (1, 2, 4, 5) if total % (p * unit) == 0)
    return parts, total // parts


def my_index():
    return (lax.axis_index("seq") * lax.axis_size("row") + lax.axis_index("row")) * 2 + lax.axis_index("core")


def partner(me, masks, place):
    for bit, mask in enumerate(masks):
        if place >> bit & 1:
            me = me ^ mask
    return me


def place_match(rows, masks, own, me):
    place = lax.broadcasted_iota(jnp.int32, (rows, rows), 0)
    block, inner = lax.div(place, own), lax.rem(place, own)
    device = jnp.full((rows, rows), me, jnp.int32)
    for bit, mask in enumerate(masks):
        device = device ^ (((block >> bit) & 1) * mask)
    return device * own + inner == lax.broadcasted_iota(jnp.int32, (rows, rows), 1)


def to_column(match, row_values):
    return jnp.sum(jnp.where(match, row_values, 0.0), axis=1, keepdims=True)


def to_row(match, column):
    return jnp.sum(jnp.where(match, column, 0.0), axis=0, keepdims=True)


def merge(first, second):
    top = jnp.maximum(first[0:1], second[0:1])
    near, far_off = jnp.exp(first[0:1] - top), jnp.exp(second[0:1] - top)
    return top, first[1:2] * near + second[1:2] * far_off, first[2:3] * near + second[2:3] * far_off


def features_kernel(hidden_ref, gain_ref, features_ref, hidden, gain, sems):
    copies = [
        pltpu.make_async_copy(hidden_ref, hidden, sems.at[0]),
        pltpu.make_async_copy(gain_ref, gain, sems.at[1]),
    ]
    for copy in copies:
        copy.start()
    for copy in copies:
        copy.wait()
    widened = hidden[...].astype(f32)
    inv_rms = lax.rsqrt(jnp.mean(widened * widened, axis=1, keepdims=True) + epsilon)
    features_ref[...] = (widened * inv_rms * gain[...]).astype(bf16)


def teacher_kernel(blocks_ref, keep_ref, send_ref):
    my_seq = lax.axis_index("seq")
    for k in range(keep_ref.shape[0]):
        keep_ref[k] = blocks_ref[my_seq ^ (2 * k)]
        send_ref[k] = blocks_ref[my_seq ^ (2 * k + 1)]


def join_kernel(first_ref, second_ref, out_ref):
    length = first_ref.shape[0]
    out_ref[:length] = first_ref[...]
    out_ref[length:] = second_ref[...]


def logits_kernel(masks, own, cap, low_ref, high_ref, weight_ref, table_ref, slots_ref, logits_ref, teacher_ref, stats_ref):
    my_seq = lax.axis_index("seq")
    rows = logits_ref.shape[0]
    parts, size = split_evenly(weight_ref.shape[0], 256)
    match = place_match(rows, masks, own, my_index())
    slots = to_column(match, slots_ref[...].astype(f32)).astype(jnp.int32)
    place = (lax.div(slots, cap) ^ my_seq) * cap + lax.rem(slots, cap)
    pick = (place == lax.broadcasted_iota(jnp.int32, (rows, table_ref.shape[0]), 1)).astype(bf16)
    teacher = jnp.dot(pick, table_ref[...], preferred_element_type=f32)
    teacher_ref[...] = teacher.astype(bf16)
    teacher_top = jnp.max(teacher, axis=1, keepdims=True)
    teacher_total = jnp.sum(jnp.exp(teacher - teacher_top), axis=1, keepdims=True)
    logits = jnp.zeros(logits_ref.shape, f32)
    for p in range(parts):
        block = slice(p * size, (p + 1) * size)
        features = jnp.concatenate([low_ref[:, block], high_ref[:, block]], axis=0)
        logits += jnp.dot(features, weight_ref[block, :], preferred_element_type=f32)
    logits_ref[...] = logits
    student_top = jnp.max(logits, axis=1, keepdims=True)
    shifted = jnp.exp(logits - student_top)
    student_total = jnp.sum(shifted, axis=1, keepdims=True)
    cross_sum = jnp.sum(shifted * (logits - teacher), axis=1, keepdims=True)
    nothing = jnp.zeros((1, rows), f32)
    pairs = [
        (to_row(match, student_top), to_row(match, teacher_top)),
        (to_row(match, student_total), to_row(match, teacher_total)),
        (to_row(match, cross_sum), nothing),
        (nothing, nothing),
    ]
    stats_ref[...] = jnp.concatenate([jnp.concatenate(p, axis=1) for p in pairs], axis=0)


def products_kernel(masks, own, logits_ref, teacher_ref, mine_ref, theirs_ref, weight_ref, keep_ref, send_ref, stats_ref):
    parts, size = split_evenly(weight_ref.shape[0], 256)
    logits = logits_ref[...]
    rows = logits.shape[0]
    half = rows // 2
    match = place_match(rows, masks, own, my_index())
    top, total, cross = merge(mine_ref[...], theirs_ref[...])
    stats_ref[...] = jnp.concatenate([top, total, cross, jnp.zeros_like(top)], axis=0)
    center = to_column(match, cross[:, :rows] / total[:, :rows])
    shifted = jnp.exp(logits - to_column(match, top[:, :rows]))
    gaps = shifted * (logits - teacher_ref[...].astype(f32) - center)
    pieces = []
    for at in range(0, rows, own):
        pieces += [gaps[at : at + own], shifted[at : at + own]]
    left = jnp.concatenate(pieces, axis=0).astype(bf16)
    for p in range(parts):
        block = slice(p * size, (p + 1) * size)
        product = lax.dot_general(
            left, weight_ref[block, :], (((1,), (1,)), ((), ())), preferred_element_type=f32
        )
        keep_ref[:, block] = product[: 2 * half]
        send_ref[:, block] = product[2 * half :].astype(bf16)


def share_kernel(masks, own, keep_ref, arrived_ref, share_ref):
    me = my_index()
    share = (keep_ref[...] + arrived_ref[...].astype(f32)).astype(bf16)
    for p in range(share_ref.shape[0]):
        share_ref[partner(me, masks, p) >> 1] = share[p * 2 * own : (p + 1) * 2 * own]


def terms_kernel(masks, own, stats_ref, valid_ref, terms_ref, factors_ref):
    me = my_index()
    rows = valid_ref.shape[1]
    chips = factors_ref.shape[0]
    stats = stats_ref[...]
    tops, totals, crosses = stats[:, 0, :], stats[:, 1, :], stats[:, 2, :]
    top = jnp.max(tops, axis=0, keepdims=True)
    scale = jnp.exp(tops - top)
    total = jnp.sum(totals * scale, axis=0, keepdims=True)
    cross = jnp.sum(crosses * scale, axis=0, keepdims=True)[:, :rows]
    lse = top + jnp.log(total)
    student_lse, teacher_lse = lse[:, :rows], lse[:, rows:]
    divergence = cross / total[:, :rows] - student_lse + teacher_lse
    row_weight = valid_ref[...].astype(f32)
    match = place_match(rows, masks, own, me)
    lane = lax.broadcasted_iota(jnp.int32, (rows, 128), 1)
    terms = to_column(match, row_weight)
    for at, values in enumerate((student_lse, teacher_lse, divergence)):
        terms = jnp.where(lane == at, to_column(match, values), terms)
    terms_ref[...] = terms
    scale = row_weight * jnp.exp(tops[:, :rows] - student_lse)
    offset = scale * (crosses[:, :rows] / totals[:, :rows] + (teacher_lse - student_lse - divergence))
    pick = lax.broadcasted_iota(jnp.int32, (2 * own, rows), 0)
    mine = lax.broadcasted_iota(jnp.int32, (2 * own, rows), 1) == me * own + lax.rem(pick, own)
    for p in range(chips):
        both = jnp.where(pick < own, scale[p : p + 1], offset[p : p + 1])
        column = jnp.sum(jnp.where(mine, both, 0.0), axis=1, keepdims=True)
        factors_ref[partner(me, masks, p) >> 1] = jnp.broadcast_to(column, factors_ref.shape[1:])


def head_kernel(low_ref, high_ref, logits_ref, teacher_ref, terms_ref, out_ref, held, sems):
    parts, size = split_evenly(out_ref.shape[0], 256)
    student_lse, teacher_lse = terms_ref[:, 0:1], terms_ref[:, 1:2]
    log_prob = logits_ref[...] - student_lse
    log_gap = log_prob - (teacher_ref[...].astype(f32) - teacher_lse)
    grad = (terms_ref[:, 3:4] * jnp.exp(log_prob) * (log_gap - terms_ref[:, 2:3])).astype(bf16)
    copies = []
    for p in range(parts):
        block = slice(p * size, (p + 1) * size)
        features = jnp.concatenate([low_ref[:, block], high_ref[:, block]], axis=0)
        held[block, :] = lax.dot_general(
            features, grad, (((0,), (0,)), ((), ())), preferred_element_type=f32
        ).astype(bf16)
        rows = pl.ds(p * size, size)
        copies.append(pltpu.make_async_copy(held.at[rows], out_ref.at[rows], sems.at[p]))
        copies[-1].start()
    for copy in copies:
        copy.wait()


def finish_kernel(hidden_ref, gain_ref, shares_ref, factors_ref, out_ref):
    own = hidden_ref.shape[0]
    widened = hidden_ref[...].astype(f32)
    inv_rms = lax.rsqrt(jnp.mean(widened * widened, axis=1, keepdims=True) + epsilon)
    normed = widened * inv_rms
    both = shares_ref[0].astype(f32) * factors_ref[0][:, 0:1]
    for p in range(1, shares_ref.shape[0]):
        both += shares_ref[p].astype(f32) * factors_ref[p][:, 0:1]
    norm_grad = (both[:own] + both[own:]) * gain_ref[...]
    mean = jnp.mean(norm_grad * normed, axis=1, keepdims=True)
    out_ref[...] = (inv_rms * (norm_grad - normed * mean)).astype(bf16)


def shards(hidden, norm_gain, head_weight, teacher_logits, teacher_slot, valid_tokens):
    n_seq, n_row = lax.axis_size("seq"), lax.axis_size("row")
    chips = n_seq * n_row
    count = chips * 2
    own, depth = hidden.shape
    width = head_weight.shape[1]
    rows = own * count
    cap = teacher_logits.shape[0]
    columns = depth // 2
    gain = norm_gain[None]
    masks = [1 << b for b in reversed(range(count.bit_length() - 1))]
    seq_masks = [m for m in reversed(masks) if m >= n_row * 2]

    def swap(value, mask):
        return lax.ppermute(value, axes, [(i, i ^ mask) for i in range(count)])

    def sems(number):
        return pltpu.SemaphoreType.DMA((number,))

    (gathered,) = call(
        features_kernel,
        "features",
        [shape((own, depth), bf16)],
        [hidden, gain],
        [far] * 2,
        [fast],
        [pltpu.VMEM((own, depth), bf16), pltpu.VMEM((1, depth), f32), sems(2)],
    )
    half_blocks = shape((n_seq // 2, cap, width), bf16)
    keep, send = call(
        teacher_kernel,
        "teacher_blocks",
        [half_blocks] * 2,
        [teacher_logits.transpose(1, 0, 2)],
        [fast],
        [fast] * 2,
        flops=10**10,
    )
    held = jnp.concatenate([keep, swap(send, seq_masks[0])], axis=1)
    behind = len(masks) - len(seq_masks)
    for step, mask in enumerate(masks[:-1]):
        arrived = swap(gathered, mask)
        bit = step - behind + 1
        if 1 <= bit < len(seq_masks):
            pairs = held.reshape((held.shape[0] // 2, 2) + held.shape[1:])
            held = jnp.concatenate([pairs[:, 0], swap(pairs[:, 1], seq_masks[bit])], axis=1)
        if step < len(masks) - 2:
            gathered = jnp.concatenate([gathered, arrived], axis=0)
    (gathered,) = call(
        join_kernel, "join", [shape((rows // 2, depth), bf16)], [gathered, arrived], [fast] * 2, [fast]
    )
    low, held = lax.optimization_barrier((gathered, held))
    high = swap(low, masks[-1])

    def with_masks(kernel, *more):
        return lambda *refs: kernel(masks, own, *more, *refs)

    logits, teacher, stats = call(
        with_masks(logits_kernel, cap),
        "logits",
        [shape((rows, width), f32), shape((rows, width), bf16), shape((4, 2 * rows), f32)],
        [low, high, head_weight, held[0], teacher_slot[None]],
        [fast] * 5,
        [fast] * 3,
        flops=2 * rows * depth * width,
    )
    keep, send, stats = call(
        with_masks(products_kernel),
        "products",
        [shape((rows, depth), f32), shape((rows, depth), bf16), shape((4, 2 * rows), f32)],
        [logits, teacher, stats, swap(stats, masks[-1]), head_weight],
        [fast] * 5,
        [fast] * 3,
        flops=4 * rows * depth * width,
    )
    (share,) = call(
        with_masks(share_kernel),
        "share",
        [shape((chips, 2 * own, depth), bf16)],
        [keep, swap(send, masks[-1])],
        [fast] * 2,
        [fast],
    )
    stats = stats[None]
    for step, mask in enumerate(masks[:-1]):
        (stats,) = call(
            join_kernel,
            "join_statistics",
            [shape((2 * stats.shape[0], 4, 2 * rows), f32)],
            [stats, swap(stats, mask)],
            [fast] * 2,
            [fast],
            light=True,
        )
        if step == 0:
            stats, share = lax.optimization_barrier((stats, share))
    shares = lax.all_to_all(share, ("seq", "row"), split_axis=0, concat_axis=0, tiled=True)
    terms, factors = call(
        with_masks(terms_kernel),
        "terms",
        [shape((rows, 128), f32), shape((chips, 2 * own, 128), f32)],
        [stats, valid_tokens[None]],
        [fast] * 2,
        [fast] * 2,
        light=True,
    )
    (grad_head,) = call(
        head_kernel,
        "grad_head",
        [shape(head_weight.shape, bf16)],
        [low, high, logits, teacher, terms],
        [fast] * 5,
        [far],
        [pltpu.VMEM((depth, width), bf16), sems(5)],
        light=True,
    )
    (grad_hidden,) = call(
        finish_kernel,
        "finish",
        [shape((own, depth), bf16)],
        [hidden, gain, shares, factors],
        [fast] * 4,
        [fast],
    )
    return (grad_hidden, grad_head)


def solution(mesh):
    n_seq, n_vocab = mesh.shape["seq"], mesh.shape["vocab"]
    finer = jax.sharding.Mesh(mesh.devices.reshape(n_seq, n_vocab // 2, 2), axes)
    placed = (
        P(axes, None),
        P(),
        P(None, axes),
        P("seq", None, ("row", "core")),
        P(),
        P(),
    )
    return jax.shard_map(
        shards,
        mesh=finer,
        in_specs=placed,
        out_specs=(P(axes, None), P(None, axes)),
        check_vma=False,
    )
```

```python
import math

import jax
import jax.numpy as jnp
from jax import lax
from jax.experimental import pallas as pl
from jax.experimental.pallas import tpu as pltpu
from jax.sharding import PartitionSpec as P

epsilon = 1e-06
axes = ("seq", "row", "core")
fast, far = pltpu.VMEM, pl.ANY
shape = jax.ShapeDtypeStruct
f32, bf16 = jnp.float32, jnp.bfloat16


def call(kernel, name, out_shape, inputs, spaces, out_spaces, scratch=(), flops=0, light=False):
    def size(leaf):
        return leaf.size * leaf.dtype.itemsize

    near = [x for x, s in zip(inputs, spaces) if s == fast]
    near += [x for x, s in zip(out_shape, out_spaces) if s == fast]
    held = sum(x.dtype.itemsize * math.prod(x.shape) for x in scratch if x.memory_space == fast)
    return pl.pallas_call(
        kernel,
        out_shape=list(out_shape),
        in_specs=[pl.BlockSpec(memory_space=s) for s in spaces],
        out_specs=[pl.BlockSpec(memory_space=s) for s in out_spaces],
        scratch_shapes=list(scratch),
        compiler_params=pltpu.CompilerParams(
            vmem_limit_bytes=2 * sum(map(size, near)) + held + (8 << 20)
        ),
        cost_estimate=pl.CostEstimate(
            flops=flops,
            bytes_accessed=0 if light else sum(map(size, list(inputs) + list(out_shape))),
            transcendentals=0,
        ),
        name=name,
    )(*inputs)


def split_evenly(total, unit):
    parts = max(p for p in (1, 2, 4, 5) if total % (p * unit) == 0)
    return parts, total // parts


def my_index():
    return (lax.axis_index("seq") * lax.axis_size("row") + lax.axis_index("row")) * 2 + lax.axis_index("core")


def partner(me, masks, place):
    for bit, mask in enumerate(masks):
        if place >> bit & 1:
            me = me ^ mask
    return me


def place_match(rows, masks, own, me):
    place = lax.broadcasted_iota(jnp.int32, (rows, rows), 0)
    block, inner = lax.div(place, own), lax.rem(place, own)
    device = jnp.full((rows, rows), me, jnp.int32)
    for bit, mask in enumerate(masks):
        device = device ^ (((block >> bit) & 1) * mask)
    return device * own + inner == lax.broadcasted_iota(jnp.int32, (rows, rows), 1)


def to_column(match, row_values):
    return jnp.sum(jnp.where(match, row_values, 0.0), axis=1, keepdims=True)


def to_row(match, column):
    return jnp.sum(jnp.where(match, column, 0.0), axis=0, keepdims=True)


def merge(first, second):
    top = jnp.maximum(first[0:1], second[0:1])
    near, far_off = jnp.exp(first[0:1] - top), jnp.exp(second[0:1] - top)
    return top, first[1:2] * near + second[1:2] * far_off, first[2:3] * near + second[2:3] * far_off


def features_kernel(hidden_ref, gain_ref, features_ref, hidden, gain, sems):
    copies = [
        pltpu.make_async_copy(hidden_ref, hidden, sems.at[0]),
        pltpu.make_async_copy(gain_ref, gain, sems.at[1]),
    ]
    for copy in copies:
        copy.start()
    for copy in copies:
        copy.wait()
    widened = hidden[...].astype(f32)
    inv_rms = lax.rsqrt(jnp.mean(widened * widened, axis=1, keepdims=True) + epsilon)
    features_ref[...] = (widened * inv_rms * gain[...]).astype(bf16)


def teacher_kernel(blocks_ref, keep_ref, send_ref):
    my_seq = lax.axis_index("seq")
    for k in range(keep_ref.shape[0]):
        keep_ref[k] = blocks_ref[my_seq ^ (2 * k)]
        send_ref[k] = blocks_ref[my_seq ^ (2 * k + 1)]


def join_kernel(first_ref, second_ref, *rest):
    out_ref = rest[-1]
    length = first_ref.shape[0]
    out_ref[:length] = first_ref[...]
    out_ref[length:] = second_ref[...]


def logits_kernel(masks, own, cap, low_ref, high_ref, weight_ref, table_ref, slots_ref, logits_ref, teacher_ref, stats_ref):
    my_seq = lax.axis_index("seq")
    rows = logits_ref.shape[0]
    parts, size = split_evenly(weight_ref.shape[0], 256)
    match = place_match(rows, masks, own, my_index())
    slots = to_column(match, slots_ref[...].astype(f32)).astype(jnp.int32)
    place = (lax.div(slots, cap) ^ my_seq) * cap + lax.rem(slots, cap)
    pick = (place == lax.broadcasted_iota(jnp.int32, (rows, table_ref.shape[0]), 1)).astype(bf16)
    teacher = jnp.dot(pick, table_ref[...], preferred_element_type=f32)
    teacher_ref[...] = teacher.astype(bf16)
    teacher_top = jnp.max(teacher, axis=1, keepdims=True)
    teacher_total = jnp.sum(jnp.exp(teacher - teacher_top), axis=1, keepdims=True)
    logits = jnp.zeros(logits_ref.shape, f32)
    for p in range(parts):
        block = slice(p * size, (p + 1) * size)
        features = jnp.concatenate([low_ref[:, block], high_ref[:, block]], axis=0)
        logits += jnp.dot(features, weight_ref[block, :], preferred_element_type=f32)
    logits_ref[...] = logits
    student_top = jnp.max(logits, axis=1, keepdims=True)
    shifted = jnp.exp(logits - student_top)
    student_total = jnp.sum(shifted, axis=1, keepdims=True)
    cross_sum = jnp.sum(shifted * (logits - teacher), axis=1, keepdims=True)
    nothing = jnp.zeros((1, rows), f32)
    pairs = [
        (to_row(match, student_top), to_row(match, teacher_top)),
        (to_row(match, student_total), to_row(match, teacher_total)),
        (to_row(match, cross_sum), nothing),
        (nothing, nothing),
    ]
    stats_ref[...] = jnp.concatenate([jnp.concatenate(p, axis=1) for p in pairs], axis=0)


def products_kernel(masks, own, logits_ref, teacher_ref, mine_ref, theirs_ref, weight_ref, keep_ref, send_ref):
    parts, size = split_evenly(weight_ref.shape[0], 256)
    logits = logits_ref[...]
    rows = logits.shape[0]
    half = rows // 2
    match = place_match(rows, masks, own, my_index())
    top, total, cross = merge(mine_ref[...], theirs_ref[...])
    center = to_column(match, cross[:, :rows] / total[:, :rows])
    shifted = jnp.exp(logits - to_column(match, top[:, :rows]))
    gaps = shifted * (logits - teacher_ref[...].astype(f32) - center)
    pieces = []
    for at in range(0, rows, own):
        pieces += [gaps[at : at + own], shifted[at : at + own]]
    left = jnp.concatenate(pieces, axis=0).astype(bf16)
    for p in range(parts):
        block = slice(p * size, (p + 1) * size)
        product = lax.dot_general(
            left, weight_ref[block, :], (((1,), (1,)), ((), ())), preferred_element_type=f32
        )
        keep_ref[:, block] = product[: 2 * half]
        send_ref[:, block] = product[2 * half :].astype(bf16)


def share_kernel(masks, own, keep_ref, arrived_ref, share_ref):
    me = my_index()
    share = (keep_ref[...] + arrived_ref[...].astype(f32)).astype(bf16)
    for p in range(share_ref.shape[0]):
        share_ref[partner(me, masks, p) >> 1] = share[p * 2 * own : (p + 1) * 2 * own]


def terms_kernel(masks, own, mine_ref, theirs_ref, valid_ref, terms_ref, factors_ref):
    me = my_index()
    rows = valid_ref.shape[1]
    chips = factors_ref.shape[0]
    mine, theirs = mine_ref[...], theirs_ref[...]
    tops = jnp.maximum(mine[:, 0, :], theirs[:, 0, :])
    near, other = jnp.exp(mine[:, 0, :] - tops), jnp.exp(theirs[:, 0, :] - tops)
    totals = mine[:, 1, :] * near + theirs[:, 1, :] * other
    crosses = mine[:, 2, :] * near + theirs[:, 2, :] * other
    top = jnp.max(tops, axis=0, keepdims=True)
    scale = jnp.exp(tops - top)
    total = jnp.sum(totals * scale, axis=0, keepdims=True)
    cross = jnp.sum(crosses * scale, axis=0, keepdims=True)[:, :rows]
    lse = top + jnp.log(total)
    student_lse, teacher_lse = lse[:, :rows], lse[:, rows:]
    divergence = cross / total[:, :rows] - student_lse + teacher_lse
    row_weight = valid_ref[...].astype(f32)
    match = place_match(rows, masks, own, me)
    lane = lax.broadcasted_iota(jnp.int32, (rows, 128), 1)
    terms = to_column(match, row_weight)
    for at, values in enumerate((student_lse, teacher_lse, divergence)):
        terms = jnp.where(lane == at, to_column(match, values), terms)
    terms_ref[...] = terms
    scale = row_weight * jnp.exp(tops[:, :rows] - student_lse)
    offset = scale * (crosses[:, :rows] / totals[:, :rows] + (teacher_lse - student_lse - divergence))
    pick = lax.broadcasted_iota(jnp.int32, (2 * own, rows), 0)
    mine = lax.broadcasted_iota(jnp.int32, (2 * own, rows), 1) == me * own + lax.rem(pick, own)
    for p in range(chips):
        both = jnp.where(pick < own, scale[p : p + 1], offset[p : p + 1])
        column = jnp.sum(jnp.where(mine, both, 0.0), axis=1, keepdims=True)
        factors_ref[partner(me, masks, p) >> 1] = jnp.broadcast_to(column, factors_ref.shape[1:])


def head_kernel(low_ref, high_ref, logits_ref, teacher_ref, terms_ref, out_ref, held, sems):
    parts, size = split_evenly(out_ref.shape[0], 256)
    student_lse, teacher_lse = terms_ref[:, 0:1], terms_ref[:, 1:2]
    log_prob = logits_ref[...] - student_lse
    log_gap = log_prob - (teacher_ref[...].astype(f32) - teacher_lse)
    grad = (terms_ref[:, 3:4] * jnp.exp(log_prob) * (log_gap - terms_ref[:, 2:3])).astype(bf16)
    copies = []
    for p in range(parts):
        block = slice(p * size, (p + 1) * size)
        features = jnp.concatenate([low_ref[:, block], high_ref[:, block]], axis=0)
        held[block, :] = lax.dot_general(
            features, grad, (((0,), (0,)), ((), ())), preferred_element_type=f32
        ).astype(bf16)
        rows = pl.ds(p * size, size)
        copies.append(pltpu.make_async_copy(held.at[rows], out_ref.at[rows], sems.at[p]))
        copies[-1].start()
    for copy in copies:
        copy.wait()


def finish_kernel(hidden_ref, gain_ref, shares_ref, factors_ref, out_ref):
    own = hidden_ref.shape[0]
    widened = hidden_ref[...].astype(f32)
    inv_rms = lax.rsqrt(jnp.mean(widened * widened, axis=1, keepdims=True) + epsilon)
    normed = widened * inv_rms
    both = shares_ref[0].astype(f32) * factors_ref[0][:, 0:1]
    for p in range(1, shares_ref.shape[0]):
        both += shares_ref[p].astype(f32) * factors_ref[p][:, 0:1]
    norm_grad = (both[:own] + both[own:]) * gain_ref[...]
    mean = jnp.mean(norm_grad * normed, axis=1, keepdims=True)
    out_ref[...] = (inv_rms * (norm_grad - normed * mean)).astype(bf16)


def shards(hidden, norm_gain, head_weight, teacher_logits, teacher_slot, valid_tokens):
    n_seq, n_row = lax.axis_size("seq"), lax.axis_size("row")
    chips = n_seq * n_row
    count = chips * 2
    own, depth = hidden.shape
    width = head_weight.shape[1]
    rows = own * count
    cap = teacher_logits.shape[0]
    columns = depth // 2
    gain = norm_gain[None]
    masks = [1 << b for b in reversed(range(count.bit_length() - 1))]
    seq_masks = [m for m in reversed(masks) if m >= n_row * 2]

    def swap(value, mask):
        return lax.ppermute(value, axes, [(i, i ^ mask) for i in range(count)])

    def sems(number):
        return pltpu.SemaphoreType.DMA((number,))

    (gathered,) = call(
        features_kernel,
        "features",
        [shape((own, depth), bf16)],
        [hidden, gain],
        [far] * 2,
        [fast],
        [pltpu.VMEM((own, depth), bf16), pltpu.VMEM((1, depth), f32), sems(2)],
    )
    half_blocks = shape((n_seq // 2, cap, width), bf16)
    keep, send = call(
        teacher_kernel,
        "teacher_blocks",
        [half_blocks] * 2,
        [teacher_logits.transpose(1, 0, 2)],
        [fast],
        [fast] * 2,
        flops=10**10,
    )
    held = jnp.concatenate([keep, swap(send, seq_masks[0])], axis=1)
    behind = len(masks) - len(seq_masks)
    for step, mask in enumerate(masks[:-1]):
        arrived = swap(gathered, mask)
        bit = step - behind + 1
        if 1 <= bit < len(seq_masks):
            pairs = held.reshape((held.shape[0] // 2, 2) + held.shape[1:])
            held = jnp.concatenate([pairs[:, 0], swap(pairs[:, 1], seq_masks[bit])], axis=1)
        if step < len(masks) - 2:
            gathered = jnp.concatenate([gathered, arrived], axis=0)
    (gathered,) = call(
        join_kernel, "join", [shape((rows // 2, depth), bf16)], [gathered, arrived], [fast] * 2, [fast]
    )
    low, held = lax.optimization_barrier((gathered, held))
    high = swap(low, masks[-1])

    def with_masks(kernel, *more):
        return lambda *refs: kernel(masks, own, *more, *refs)

    logits, teacher, stats = call(
        with_masks(logits_kernel, cap),
        "logits",
        [shape((rows, width), f32), shape((rows, width), bf16), shape((4, 2 * rows), f32)],
        [low, high, head_weight, held[0], teacher_slot[None]],
        [fast] * 5,
        [fast] * 3,
        flops=2 * rows * depth * width,
    )
    keep, send = call(
        with_masks(products_kernel),
        "products",
        [shape((rows, depth), f32), shape((rows, depth), bf16)],
        [logits, teacher, stats, swap(stats, masks[-1]), head_weight],
        [fast] * 5,
        [fast] * 2,
        flops=4 * rows * depth * width,
    )
    def join(value, mask, *after):
        (joined,) = call(
            join_kernel,
            "join_statistics",
            [shape((2 * value.shape[0], 4, 2 * rows), f32)],
            [value, swap(value, mask), *after],
            [fast] * 2 + [far] * len(after),
            [fast],
            light=True,
        )
        return joined

    stats = join(stats[None], masks[0], send)
    stats, send = lax.optimization_barrier((stats, send))
    (share,) = call(
        with_masks(share_kernel),
        "share",
        [shape((chips, 2 * own, depth), bf16)],
        [keep, swap(send, masks[-1])],
        [fast] * 2,
        [fast],
    )
    for step, mask in enumerate(masks[1:-1]):
        stats = join(stats, mask, *[share] * (step == 0))
    other_stats = swap(stats, masks[-1])
    shares = lax.all_to_all(share, ("seq", "row"), split_axis=0, concat_axis=0, tiled=True)
    terms, factors = call(
        with_masks(terms_kernel),
        "terms",
        [shape((rows, 128), f32), shape((chips, 2 * own, 128), f32)],
        [stats, other_stats, valid_tokens[None]],
        [fast] * 3,
        [fast] * 2,
        light=True,
    )
    (grad_head,) = call(
        head_kernel,
        "grad_head",
        [shape(head_weight.shape, bf16)],
        [low, high, logits, teacher, terms],
        [fast] * 5,
        [far],
        [pltpu.VMEM((depth, width), bf16), sems(5)],
        light=True,
    )
    (grad_hidden,) = call(
        finish_kernel,
        "finish",
        [shape((own, depth), bf16)],
        [hidden, gain, shares, factors],
        [fast] * 4,
        [fast],
    )
    return (grad_hidden, grad_head)


def solution(mesh):
    n_seq, n_vocab = mesh.shape["seq"], mesh.shape["vocab"]
    finer = jax.sharding.Mesh(mesh.devices.reshape(n_seq, n_vocab // 2, 2), axes)
    placed = (
        P(axes, None),
        P(),
        P(None, axes),
        P("seq", None, ("row", "core")),
        P(),
        P(),
    )
    return jax.shard_map(
        shards,
        mesh=finer,
        in_specs=placed,
        out_specs=(P(axes, None), P(None, axes)),
        check_vma=False,
    )
```

```python
import math

import jax
import jax.numpy as jnp
from jax import lax
from jax.experimental import pallas as pl
from jax.experimental.pallas import tpu as pltpu
from jax.sharding import PartitionSpec as P

epsilon = 1e-06
axes = ("seq", "row", "core")
fast, far = pltpu.VMEM, pl.ANY
shape = jax.ShapeDtypeStruct
f32, bf16 = jnp.float32, jnp.bfloat16


def call(kernel, name, out_shape, inputs, spaces, out_spaces, scratch=(), flops=0, light=False):
    def size(leaf):
        return leaf.size * leaf.dtype.itemsize

    near = [x for x, s in zip(inputs, spaces) if s == fast]
    near += [x for x, s in zip(out_shape, out_spaces) if s == fast]
    held = sum(x.dtype.itemsize * math.prod(x.shape) for x in scratch if x.memory_space == fast)
    return pl.pallas_call(
        kernel,
        out_shape=list(out_shape),
        in_specs=[pl.BlockSpec(memory_space=s) for s in spaces],
        out_specs=[pl.BlockSpec(memory_space=s) for s in out_spaces],
        scratch_shapes=list(scratch),
        compiler_params=pltpu.CompilerParams(
            vmem_limit_bytes=2 * sum(map(size, near)) + held + (8 << 20)
        ),
        cost_estimate=pl.CostEstimate(
            flops=flops,
            bytes_accessed=0 if light else sum(map(size, list(inputs) + list(out_shape))),
            transcendentals=0,
        ),
        name=name,
    )(*inputs)


def split_evenly(total, unit):
    parts = max(p for p in (1, 2, 4, 5) if total % (p * unit) == 0)
    return parts, total // parts


def my_index():
    return (lax.axis_index("seq") * lax.axis_size("row") + lax.axis_index("row")) * 2 + lax.axis_index("core")


def partner(me, masks, place):
    for bit, mask in enumerate(masks):
        if place >> bit & 1:
            me = me ^ mask
    return me


def place_match(rows, masks, own, me):
    place = lax.broadcasted_iota(jnp.int32, (rows, rows), 0)
    block, inner = lax.div(place, own), lax.rem(place, own)
    device = jnp.full((rows, rows), me, jnp.int32)
    for bit, mask in enumerate(masks):
        device = device ^ (((block >> bit) & 1) * mask)
    return device * own + inner == lax.broadcasted_iota(jnp.int32, (rows, rows), 1)


def to_column(match, row_values):
    return jnp.sum(jnp.where(match, row_values, 0.0), axis=1, keepdims=True)


def to_row(match, column):
    return jnp.sum(jnp.where(match, column, 0.0), axis=0, keepdims=True)


def merge(first, second):
    top = jnp.maximum(first[0:1], second[0:1])
    near, far_off = jnp.exp(first[0:1] - top), jnp.exp(second[0:1] - top)
    return top, first[1:2] * near + second[1:2] * far_off, first[2:3] * near + second[2:3] * far_off


def features_kernel(hidden_ref, gain_ref, features_ref, hidden, gain, sems):
    copies = [
        pltpu.make_async_copy(hidden_ref, hidden, sems.at[0]),
        pltpu.make_async_copy(gain_ref, gain, sems.at[1]),
    ]
    for copy in copies:
        copy.start()
    for copy in copies:
        copy.wait()
    widened = hidden[...].astype(f32)
    inv_rms = lax.rsqrt(jnp.mean(widened * widened, axis=1, keepdims=True) + epsilon)
    features_ref[...] = (widened * inv_rms * gain[...]).astype(bf16)


def teacher_kernel(blocks_ref, keep_ref, send_ref):
    my_seq = lax.axis_index("seq")
    for k in range(keep_ref.shape[0]):
        keep_ref[k] = blocks_ref[my_seq ^ (2 * k)]
        send_ref[k] = blocks_ref[my_seq ^ (2 * k + 1)]


def join_kernel(first_ref, second_ref, *rest):
    out_ref = rest[-1]
    length = first_ref.shape[0]
    out_ref[:length] = first_ref[...]
    out_ref[length:] = second_ref[...]


def logits_kernel(masks, own, cap, low_ref, high_ref, weight_ref, table_ref, slots_ref, logits_ref, teacher_ref, stats_ref):
    my_seq = lax.axis_index("seq")
    rows = logits_ref.shape[0]
    parts, size = split_evenly(weight_ref.shape[0], 256)
    match = place_match(rows, masks, own, my_index())
    slots = to_column(match, slots_ref[...].astype(f32)).astype(jnp.int32)
    place = (lax.div(slots, cap) ^ my_seq) * cap + lax.rem(slots, cap)
    pick = (place == lax.broadcasted_iota(jnp.int32, (rows, table_ref.shape[0]), 1)).astype(bf16)
    teacher = jnp.dot(pick, table_ref[...], preferred_element_type=f32)
    teacher_ref[...] = teacher.astype(bf16)
    teacher_top = jnp.max(teacher, axis=1, keepdims=True)
    teacher_total = jnp.sum(jnp.exp(teacher - teacher_top), axis=1, keepdims=True)
    logits = jnp.zeros(logits_ref.shape, f32)
    for p in range(parts):
        block = slice(p * size, (p + 1) * size)
        features = jnp.concatenate([low_ref[:, block], high_ref[:, block]], axis=0)
        logits += jnp.dot(features, weight_ref[block, :], preferred_element_type=f32)
    logits_ref[...] = logits
    student_top = jnp.max(logits, axis=1, keepdims=True)
    shifted = jnp.exp(logits - student_top)
    student_total = jnp.sum(shifted, axis=1, keepdims=True)
    cross_sum = jnp.sum(shifted * (logits - teacher), axis=1, keepdims=True)
    nothing = jnp.zeros((1, rows), f32)
    pairs = [
        (to_row(match, student_top), to_row(match, teacher_top)),
        (to_row(match, student_total), to_row(match, teacher_total)),
        (to_row(match, cross_sum), nothing),
        (nothing, nothing),
    ]
    stats_ref[...] = jnp.concatenate([jnp.concatenate(p, axis=1) for p in pairs], axis=0)


def products_kernel(masks, own, logits_ref, teacher_ref, mine_ref, theirs_ref, weight_ref, keep_ref, send_ref):
    parts, size = split_evenly(weight_ref.shape[0], 256)
    logits = logits_ref[...]
    rows = logits.shape[0]
    half = rows // 2
    match = place_match(rows, masks, own, my_index())
    top, total, cross = merge(mine_ref[...], theirs_ref[...])
    center = to_column(match, cross[:, :rows] / total[:, :rows])
    shifted = jnp.exp(logits - to_column(match, top[:, :rows]))
    gaps = shifted * (logits - teacher_ref[...].astype(f32) - center)
    pieces = []
    for at in range(0, rows, own):
        pieces += [gaps[at : at + own], shifted[at : at + own]]
    left = jnp.concatenate(pieces, axis=0).astype(bf16)
    for p in range(parts):
        block = slice(p * size, (p + 1) * size)
        product = lax.dot_general(
            left, weight_ref[block, :], (((1,), (1,)), ((), ())), preferred_element_type=f32
        )
        keep_ref[:, block] = product[: 2 * half]
        send_ref[:, block] = product[2 * half :].astype(bf16)


def share_kernel(masks, own, keep_ref, arrived_ref, share_ref):
    me = my_index()
    share = (keep_ref[...] + arrived_ref[...].astype(f32)).astype(bf16)
    for p in range(share_ref.shape[0]):
        share_ref[partner(me, masks, p) >> 1] = share[p * 2 * own : (p + 1) * 2 * own]


def terms_kernel(masks, own, mine_ref, theirs_ref, valid_ref, terms_ref, factors_ref):
    me = my_index()
    rows = valid_ref.shape[1]
    chips = factors_ref.shape[0]
    mine, theirs = mine_ref[...], theirs_ref[...]
    tops = jnp.maximum(mine[:, 0, :], theirs[:, 0, :])
    near, other = jnp.exp(mine[:, 0, :] - tops), jnp.exp(theirs[:, 0, :] - tops)
    totals = mine[:, 1, :] * near + theirs[:, 1, :] * other
    crosses = mine[:, 2, :] * near + theirs[:, 2, :] * other
    top = jnp.max(tops, axis=0, keepdims=True)
    scale = jnp.exp(tops - top)
    total = jnp.sum(totals * scale, axis=0, keepdims=True)
    cross = jnp.sum(crosses * scale, axis=0, keepdims=True)[:, :rows]
    lse = top + jnp.log(total)
    student_lse, teacher_lse = lse[:, :rows], lse[:, rows:]
    divergence = cross / total[:, :rows] - student_lse + teacher_lse
    row_weight = valid_ref[...].astype(f32)
    match = place_match(rows, masks, own, me)
    lane = lax.broadcasted_iota(jnp.int32, (rows, 128), 1)
    terms = to_column(match, row_weight)
    for at, values in enumerate((student_lse, teacher_lse, divergence)):
        terms = jnp.where(lane == at, to_column(match, values), terms)
    terms_ref[...] = terms
    scale = row_weight * jnp.exp(tops[:, :rows] - student_lse)
    offset = scale * (crosses[:, :rows] / totals[:, :rows] + (teacher_lse - student_lse - divergence))
    pick = lax.broadcasted_iota(jnp.int32, (2 * own, rows), 0)
    mine = lax.broadcasted_iota(jnp.int32, (2 * own, rows), 1) == me * own + lax.rem(pick, own)
    for p in range(chips):
        both = jnp.where(pick < own, scale[p : p + 1], offset[p : p + 1])
        column = jnp.sum(jnp.where(mine, both, 0.0), axis=1, keepdims=True)
        factors_ref[partner(me, masks, p) >> 1] = jnp.broadcast_to(column, factors_ref.shape[1:])


def head_kernel(low_ref, high_ref, logits_ref, teacher_ref, terms_ref, out_ref, held, sems):
    parts, size = split_evenly(out_ref.shape[0], 256)
    student_lse, teacher_lse = terms_ref[:, 0:1], terms_ref[:, 1:2]
    log_prob = logits_ref[...] - student_lse
    log_gap = log_prob - (teacher_ref[...].astype(f32) - teacher_lse)
    grad = (terms_ref[:, 3:4] * jnp.exp(log_prob) * (log_gap - terms_ref[:, 2:3])).astype(bf16)
    copies = []
    for p in range(parts):
        block = slice(p * size, (p + 1) * size)
        features = jnp.concatenate([low_ref[:, block], high_ref[:, block]], axis=0)
        held[block, :] = lax.dot_general(
            features, grad, (((0,), (0,)), ((), ())), preferred_element_type=f32
        ).astype(bf16)
        rows = pl.ds(p * size, size)
        copies.append(pltpu.make_async_copy(held.at[rows], out_ref.at[rows], sems.at[p]))
        copies[-1].start()
    for copy in copies:
        copy.wait()


def finish_kernel(hidden_ref, gain_ref, shares_ref, factors_ref, out_ref):
    own = hidden_ref.shape[0]
    widened = hidden_ref[...].astype(f32)
    inv_rms = lax.rsqrt(jnp.mean(widened * widened, axis=1, keepdims=True) + epsilon)
    normed = widened * inv_rms
    both = shares_ref[0].astype(f32) * factors_ref[0][:, 0:1]
    for p in range(1, shares_ref.shape[0]):
        both += shares_ref[p].astype(f32) * factors_ref[p][:, 0:1]
    norm_grad = (both[:own] + both[own:]) * gain_ref[...]
    mean = jnp.mean(norm_grad * normed, axis=1, keepdims=True)
    out_ref[...] = (inv_rms * (norm_grad - normed * mean)).astype(bf16)


def shards(hidden, norm_gain, head_weight, teacher_logits, teacher_slot, valid_tokens):
    n_seq, n_row = lax.axis_size("seq"), lax.axis_size("row")
    chips = n_seq * n_row
    count = chips * 2
    own, depth = hidden.shape
    width = head_weight.shape[1]
    rows = own * count
    cap = teacher_logits.shape[0]
    columns = depth // 2
    gain = norm_gain[None]
    masks = [1 << b for b in reversed(range(count.bit_length() - 1))]
    seq_masks = [m for m in reversed(masks) if m >= n_row * 2]

    def swap(value, mask):
        return lax.ppermute(value, axes, [(i, i ^ mask) for i in range(count)])

    def sems(number):
        return pltpu.SemaphoreType.DMA((number,))

    (gathered,) = call(
        features_kernel,
        "features",
        [shape((own, depth), bf16)],
        [hidden, gain],
        [far] * 2,
        [fast],
        [pltpu.VMEM((own, depth), bf16), pltpu.VMEM((1, depth), f32), sems(2)],
    )
    half_blocks = shape((n_seq // 2, cap, width), bf16)
    keep, send = call(
        teacher_kernel,
        "teacher_blocks",
        [half_blocks] * 2,
        [teacher_logits.transpose(1, 0, 2)],
        [fast],
        [fast] * 2,
        flops=10**10,
    )
    held = jnp.concatenate([keep, swap(send, seq_masks[0])], axis=1)
    behind = len(masks) - len(seq_masks)
    for step, mask in enumerate(masks[:-1]):
        arrived = swap(gathered, mask)
        bit = step - behind + 1
        if 1 <= bit < len(seq_masks):
            pairs = held.reshape((held.shape[0] // 2, 2) + held.shape[1:])
            held = jnp.concatenate([pairs[:, 0], swap(pairs[:, 1], seq_masks[bit])], axis=1)
        if step < len(masks) - 2:
            gathered = jnp.concatenate([gathered, arrived], axis=0)
    (gathered,) = call(
        join_kernel, "join", [shape((rows // 2, depth), bf16)], [gathered, arrived], [fast] * 2, [fast]
    )
    low, held = lax.optimization_barrier((gathered, held))
    high = swap(low, masks[-1])

    def with_masks(kernel, *more):
        return lambda *refs: kernel(masks, own, *more, *refs)

    logits, teacher, stats = call(
        with_masks(logits_kernel, cap),
        "logits",
        [shape((rows, width), f32), shape((rows, width), bf16), shape((4, 2 * rows), f32)],
        [low, high, head_weight, held[0], teacher_slot[None]],
        [fast] * 5,
        [fast] * 3,
        flops=2 * rows * depth * width,
    )
    keep, send = call(
        with_masks(products_kernel),
        "products",
        [shape((rows, depth), f32), shape((rows, depth), bf16)],
        [logits, teacher, stats, swap(stats, masks[-1]), head_weight],
        [fast] * 5,
        [fast] * 2,
        flops=4 * rows * depth * width,
    )
    def join(value, mask, *after):
        (joined,) = call(
            join_kernel,
            "join_statistics",
            [shape((2 * value.shape[0], 4, 2 * rows), f32)],
            [value, swap(value, mask), *after],
            [fast] * 2 + [far] * len(after),
            [fast],
            light=True,
        )
        return joined

    stats = join(stats[None], masks[0], send)
    stats, send = lax.optimization_barrier((stats, send))
    (share,) = call(
        with_masks(share_kernel),
        "share",
        [shape((chips, 2 * own, depth), bf16)],
        [keep, swap(send, masks[-1])],
        [fast] * 2,
        [fast],
    )
    for step, mask in enumerate(masks[1:-1]):
        if step == 0:
            stats, share = lax.optimization_barrier((join(stats, mask, share), share))
        else:
            stats = join(stats, mask)
    other_stats = swap(stats, masks[-1])
    shares = lax.all_to_all(share, ("seq", "row"), split_axis=0, concat_axis=0, tiled=True)
    terms, factors = call(
        with_masks(terms_kernel),
        "terms",
        [shape((rows, 128), f32), shape((chips, 2 * own, 128), f32)],
        [stats, other_stats, valid_tokens[None]],
        [fast] * 3,
        [fast] * 2,
        light=True,
    )
    (grad_head,) = call(
        head_kernel,
        "grad_head",
        [shape(head_weight.shape, bf16)],
        [low, high, logits, teacher, terms],
        [fast] * 5,
        [far],
        [pltpu.VMEM((depth, width), bf16), sems(5)],
        light=True,
    )
    (grad_hidden,) = call(
        finish_kernel,
        "finish",
        [shape((own, depth), bf16)],
        [hidden, gain, shares, factors],
        [fast] * 4,
        [fast],
    )
    return (grad_hidden, grad_head)


def solution(mesh):
    n_seq, n_vocab = mesh.shape["seq"], mesh.shape["vocab"]
    finer = jax.sharding.Mesh(mesh.devices.reshape(n_seq, n_vocab // 2, 2), axes)
    placed = (
        P(axes, None),
        P(),
        P(None, axes),
        P("seq", None, ("row", "core")),
        P(),
        P(),
    )
    return jax.shard_map(
        shards,
        mesh=finer,
        in_specs=placed,
        out_specs=(P(axes, None), P(None, axes)),
        check_vma=False,
    )
```

```python
import math

import jax
import jax.numpy as jnp
from jax import lax
from jax.experimental import pallas as pl
from jax.experimental.pallas import tpu as pltpu
from jax.sharding import PartitionSpec as P

epsilon = 1e-06
axes = ("seq", "row", "core")
fast, far = pltpu.VMEM, pl.ANY
shape = jax.ShapeDtypeStruct
f32, bf16 = jnp.float32, jnp.bfloat16


def call(kernel, name, out_shape, inputs, spaces, out_spaces, scratch=(), flops=0, light=False):
    def size(leaf):
        return leaf.size * leaf.dtype.itemsize

    near = [x for x, s in zip(inputs, spaces) if s == fast]
    near += [x for x, s in zip(out_shape, out_spaces) if s == fast]
    held = sum(x.dtype.itemsize * math.prod(x.shape) for x in scratch if x.memory_space == fast)
    return pl.pallas_call(
        kernel,
        out_shape=list(out_shape),
        in_specs=[pl.BlockSpec(memory_space=s) for s in spaces],
        out_specs=[pl.BlockSpec(memory_space=s) for s in out_spaces],
        scratch_shapes=list(scratch),
        compiler_params=pltpu.CompilerParams(
            vmem_limit_bytes=2 * sum(map(size, near)) + held + (8 << 20)
        ),
        cost_estimate=pl.CostEstimate(
            flops=flops,
            bytes_accessed=0 if light else sum(map(size, list(inputs) + list(out_shape))),
            transcendentals=0,
        ),
        name=name,
    )(*inputs)


def split_evenly(total, unit):
    parts = max(p for p in (1, 2, 4, 5) if total % (p * unit) == 0)
    return parts, total // parts


def my_index():
    return (lax.axis_index("seq") * lax.axis_size("row") + lax.axis_index("row")) * 2 + lax.axis_index("core")


def partner(me, masks, place):
    for bit, mask in enumerate(masks):
        if place >> bit & 1:
            me = me ^ mask
    return me


def place_match(rows, masks, own, me):
    place = lax.broadcasted_iota(jnp.int32, (rows, rows), 0)
    block, inner = lax.div(place, own), lax.rem(place, own)
    device = jnp.full((rows, rows), me, jnp.int32)
    for bit, mask in enumerate(masks):
        device = device ^ (((block >> bit) & 1) * mask)
    return device * own + inner == lax.broadcasted_iota(jnp.int32, (rows, rows), 1)


def to_column(match, row_values):
    return jnp.sum(jnp.where(match, row_values, 0.0), axis=1, keepdims=True)


def to_row(match, column):
    return jnp.sum(jnp.where(match, column, 0.0), axis=0, keepdims=True)


def features_kernel(hidden_ref, gain_ref, features_ref, hidden, gain, sems):
    copies = [
        pltpu.make_async_copy(hidden_ref, hidden, sems.at[0]),
        pltpu.make_async_copy(gain_ref, gain, sems.at[1]),
    ]
    for copy in copies:
        copy.start()
    for copy in copies:
        copy.wait()
    widened = hidden[...].astype(f32)
    inv_rms = lax.rsqrt(jnp.mean(widened * widened, axis=1, keepdims=True) + epsilon)
    features_ref[...] = (widened * inv_rms * gain[...]).astype(bf16)


def teacher_kernel(blocks_ref, keep_ref, send_ref):
    my_seq = lax.axis_index("seq")
    for k in range(keep_ref.shape[0]):
        keep_ref[k] = blocks_ref[my_seq ^ (2 * k)]
        send_ref[k] = blocks_ref[my_seq ^ (2 * k + 1)]


def join_kernel(first_ref, second_ref, out_ref):
    length = first_ref.shape[0]
    out_ref[:length] = first_ref[...]
    out_ref[length:] = second_ref[...]


def logits_kernel(masks, own, cap, low_ref, high_ref, weight_ref, table_ref, slots_ref, logits_ref, teacher_ref, local_ref, stats_ref):
    my_seq = lax.axis_index("seq")
    rows = logits_ref.shape[0]
    parts, size = split_evenly(weight_ref.shape[0], 256)
    match = place_match(rows, masks, own, my_index())
    slots = to_column(match, slots_ref[...].astype(f32)).astype(jnp.int32)
    place = (lax.div(slots, cap) ^ my_seq) * cap + lax.rem(slots, cap)
    pick = (place == lax.broadcasted_iota(jnp.int32, (rows, table_ref.shape[0]), 1)).astype(bf16)
    teacher = jnp.dot(pick, table_ref[...], preferred_element_type=f32)
    teacher_ref[...] = teacher.astype(bf16)
    teacher_top = jnp.max(teacher, axis=1, keepdims=True)
    teacher_total = jnp.sum(jnp.exp(teacher - teacher_top), axis=1, keepdims=True)
    logits = jnp.zeros(logits_ref.shape, f32)
    for p in range(parts):
        block = slice(p * size, (p + 1) * size)
        features = jnp.concatenate([low_ref[:, block], high_ref[:, block]], axis=0)
        logits += jnp.dot(features, weight_ref[block, :], preferred_element_type=f32)
    logits_ref[...] = logits
    student_top = jnp.max(logits, axis=1, keepdims=True)
    shifted = jnp.exp(logits - student_top)
    student_total = jnp.sum(shifted, axis=1, keepdims=True)
    cross_sum = jnp.sum(shifted * (logits - teacher), axis=1, keepdims=True)
    nothing = jnp.zeros((1, rows), f32)
    pairs = [
        (to_row(match, student_top), to_row(match, teacher_top)),
        (to_row(match, student_total), to_row(match, teacher_total)),
        (to_row(match, cross_sum), nothing),
        (nothing, nothing),
    ]
    stats = jnp.concatenate([jnp.concatenate(p, axis=1) for p in pairs], axis=0)
    local_ref[...] = stats
    for p in range(stats_ref.shape[0]):
        stats_ref[p] = stats


def products_kernel(masks, own, logits_ref, teacher_ref, local_ref, weight_ref, keep_ref, send_ref):
    parts, size = split_evenly(weight_ref.shape[0], 256)
    logits = logits_ref[...]
    rows = logits.shape[0]
    half = rows // 2
    match = place_match(rows, masks, own, my_index())
    center = to_column(match, local_ref[2:3, :rows] / local_ref[1:2, :rows])
    shifted = jnp.exp(logits - to_column(match, local_ref[0:1, :rows]))
    gaps = (shifted * (logits - teacher_ref[...].astype(f32) - center)).astype(bf16)
    shifted = shifted.astype(bf16)
    left = jnp.concatenate([gaps[:half], shifted[:half], gaps[half:], shifted[half:]], axis=0)
    for p in range(parts):
        block = slice(p * size, (p + 1) * size)
        product = lax.dot_general(
            left, weight_ref[block, :], (((1,), (1,)), ((), ())), preferred_element_type=f32
        )
        keep_ref[:, block] = product[: 2 * half]
        send_ref[:, block] = product[2 * half :].astype(bf16)


def terms_kernel(masks, own, stats_ref, valid_ref, terms_ref):
    me = my_index()
    rows = valid_ref.shape[1]
    stats = stats_ref[...]
    tops, totals, crosses = stats[:, 0, :], stats[:, 1, :], stats[:, 2, :]
    top = jnp.max(tops, axis=0, keepdims=True)
    scale = jnp.exp(tops - top)
    total = jnp.sum(totals * scale, axis=0, keepdims=True)
    cross = jnp.sum(crosses * scale, axis=0, keepdims=True)[:, :rows]
    lse = top + jnp.log(total)
    student_lse, teacher_lse = lse[:, :rows], lse[:, rows:]
    divergence = cross / total[:, :rows] - student_lse + teacher_lse
    row_weight = valid_ref[...].astype(f32)
    values = [student_lse, teacher_lse, divergence, row_weight]
    for device in (me, me ^ 1):
        part = stats_ref[device]
        factor = row_weight * jnp.exp(part[0:1, :rows] - student_lse)
        center = part[2:3, :rows] / part[1:2, :rows]
        values += [factor, factor * (center + (teacher_lse - student_lse - divergence))]
    match = place_match(rows, masks, own, me)
    lane = lax.broadcasted_iota(jnp.int32, (rows, 128), 1)
    terms = jnp.zeros((rows, 128), f32)
    for at, value in enumerate(values):
        terms = jnp.where(lane == at, to_column(match, value), terms)
    terms_ref[...] = terms


def share_kernel(masks, own, terms_ref, keep_ref, arrived_ref, share_ref):
    me = my_index()
    half = keep_ref.shape[0] // 2
    near = terms_ref[:half, 4:5] * keep_ref[:half, :] + terms_ref[:half, 5:6] * keep_ref[half:, :]
    other = terms_ref[:half, 6:7] * arrived_ref[:half, :].astype(f32)
    other += terms_ref[:half, 7:8] * arrived_ref[half:, :].astype(f32)
    share = (near + other).astype(bf16)
    for p in range(share_ref.shape[0]):
        share_ref[partner(me, masks, p) >> 1] = share[p * own : (p + 1) * own]


def head_kernel(low_ref, high_ref, logits_ref, teacher_ref, terms_ref, out_ref, held, sems):
    parts, size = split_evenly(out_ref.shape[0], 256)
    student_lse, teacher_lse = terms_ref[:, 0:1], terms_ref[:, 1:2]
    log_prob = logits_ref[...] - student_lse
    log_gap = log_prob - (teacher_ref[...].astype(f32) - teacher_lse)
    grad = (terms_ref[:, 3:4] * jnp.exp(log_prob) * (log_gap - terms_ref[:, 2:3])).astype(bf16)
    copies = []
    for p in range(parts):
        block = slice(p * size, (p + 1) * size)
        features = jnp.concatenate([low_ref[:, block], high_ref[:, block]], axis=0)
        held[block, :] = lax.dot_general(
            features, grad, (((0,), (0,)), ((), ())), preferred_element_type=f32
        ).astype(bf16)
        rows = pl.ds(p * size, size)
        copies.append(pltpu.make_async_copy(held.at[rows], out_ref.at[rows], sems.at[p]))
        copies[-1].start()
    for copy in copies:
        copy.wait()


def finish_kernel(hidden_ref, gain_ref, shares_ref, out_ref):
    widened = hidden_ref[...].astype(f32)
    inv_rms = lax.rsqrt(jnp.mean(widened * widened, axis=1, keepdims=True) + epsilon)
    normed = widened * inv_rms
    feature_grad = shares_ref[0].astype(f32)
    for p in range(1, shares_ref.shape[0]):
        feature_grad += shares_ref[p].astype(f32)
    norm_grad = feature_grad * gain_ref[...]
    mean = jnp.mean(norm_grad * normed, axis=1, keepdims=True)
    out_ref[...] = (inv_rms * (norm_grad - normed * mean)).astype(bf16)


def shards(hidden, norm_gain, head_weight, teacher_logits, teacher_slot, valid_tokens):
    n_seq, n_row = lax.axis_size("seq"), lax.axis_size("row")
    chips = n_seq * n_row
    count = chips * 2
    own, depth = hidden.shape
    width = head_weight.shape[1]
    rows = own * count
    cap = teacher_logits.shape[0]
    columns = depth // 2
    gain = norm_gain[None]
    masks = [1 << b for b in reversed(range(count.bit_length() - 1))]
    seq_masks = [m for m in reversed(masks) if m >= n_row * 2]

    def swap(value, mask):
        return lax.ppermute(value, axes, [(i, i ^ mask) for i in range(count)])

    def sems(number):
        return pltpu.SemaphoreType.DMA((number,))

    (gathered,) = call(
        features_kernel,
        "features",
        [shape((own, depth), bf16)],
        [hidden, gain],
        [far] * 2,
        [fast],
        [pltpu.VMEM((own, depth), bf16), pltpu.VMEM((1, depth), f32), sems(2)],
    )
    half_blocks = shape((n_seq // 2, cap, width), bf16)
    keep, send = call(
        teacher_kernel,
        "teacher_blocks",
        [half_blocks] * 2,
        [teacher_logits.transpose(1, 0, 2)],
        [fast],
        [fast] * 2,
        flops=10**10,
    )
    held = jnp.concatenate([keep, swap(send, seq_masks[0])], axis=1)
    behind = len(masks) - len(seq_masks)
    for step, mask in enumerate(masks[:-1]):
        arrived = swap(gathered, mask)
        bit = step - behind + 1
        if 1 <= bit < len(seq_masks):
            pairs = held.reshape((held.shape[0] // 2, 2) + held.shape[1:])
            held = jnp.concatenate([pairs[:, 0], swap(pairs[:, 1], seq_masks[bit])], axis=1)
        if step < len(masks) - 2:
            gathered = jnp.concatenate([gathered, arrived], axis=0)
    (gathered,) = call(
        join_kernel, "join", [shape((rows // 2, depth), bf16)], [gathered, arrived], [fast] * 2, [fast]
    )
    low, held = lax.optimization_barrier((gathered, held))
    high = swap(low, masks[-1])

    def with_masks(kernel, *more):
        return lambda *refs: kernel(masks, own, *more, *refs)

    logits, teacher, local, stats = call(
        with_masks(logits_kernel, cap),
        "logits",
        [
            shape((rows, width), f32),
            shape((rows, width), bf16),
            shape((4, 2 * rows), f32),
            shape((count, 4, 2 * rows), f32),
        ],
        [low, high, head_weight, held[0], teacher_slot[None]],
        [fast] * 5,
        [fast] * 4,
        flops=2 * rows * depth * width,
    )
    stats = lax.all_to_all(stats, axes, split_axis=0, concat_axis=0, tiled=True)
    keep, send = call(
        with_masks(products_kernel),
        "products",
        [shape((rows, depth), f32), shape((rows, depth), bf16)],
        [logits, teacher, local, head_weight],
        [fast] * 4,
        [fast] * 2,
        flops=4 * rows * depth * width,
    )
    (terms,) = call(
        with_masks(terms_kernel),
        "terms",
        [shape((rows, 128), f32)],
        [stats, valid_tokens[None]],
        [fast] * 2,
        [fast],
        flops=2 * 10**10,
    )
    (share,) = call(
        with_masks(share_kernel),
        "share",
        [shape((chips, own, depth), bf16)],
        [terms, keep, swap(send, masks[-1])],
        [fast] * 3,
        [fast],
    )
    terms, share = lax.optimization_barrier((terms, share))
    shares = lax.all_to_all(share, ("seq", "row"), split_axis=0, concat_axis=0, tiled=True)
    (grad_head,) = call(
        head_kernel,
        "grad_head",
        [shape(head_weight.shape, bf16)],
        [low, high, logits, teacher, terms],
        [fast] * 5,
        [far],
        [pltpu.VMEM((depth, width), bf16), sems(5)],
        flops=2 * rows * depth * width,
    )
    (grad_hidden,) = call(
        finish_kernel,
        "finish",
        [shape((own, depth), bf16)],
        [hidden, gain, shares],
        [fast] * 3,
        [fast],
    )
    return (grad_hidden, grad_head)


def solution(mesh):
    n_seq, n_vocab = mesh.shape["seq"], mesh.shape["vocab"]
    finer = jax.sharding.Mesh(mesh.devices.reshape(n_seq, n_vocab // 2, 2), axes)
    placed = (
        P(axes, None),
        P(),
        P(None, axes),
        P("seq", None, ("row", "core")),
        P(),
        P(),
    )
    return jax.shard_map(
        shards,
        mesh=finer,
        in_specs=placed,
        out_specs=(P(axes, None), P(None, axes)),
        check_vma=False,
    )
```

```python
import math

import jax
import jax.numpy as jnp
from jax import lax
from jax.experimental import pallas as pl
from jax.experimental.pallas import tpu as pltpu
from jax.sharding import PartitionSpec as P

epsilon = 1e-06
axes = ("seq", "row", "core")
fast, far = pltpu.VMEM, pl.ANY
shape = jax.ShapeDtypeStruct
f32, bf16 = jnp.float32, jnp.bfloat16


def call(kernel, name, out_shape, inputs, spaces, out_spaces, scratch=(), flops=0, light=False):
    def size(leaf):
        return leaf.size * leaf.dtype.itemsize

    near = [x for x, s in zip(inputs, spaces) if s == fast]
    near += [x for x, s in zip(out_shape, out_spaces) if s == fast]
    held = sum(x.dtype.itemsize * math.prod(x.shape) for x in scratch if x.memory_space == fast)
    return pl.pallas_call(
        kernel,
        out_shape=list(out_shape),
        in_specs=[pl.BlockSpec(memory_space=s) for s in spaces],
        out_specs=[pl.BlockSpec(memory_space=s) for s in out_spaces],
        scratch_shapes=list(scratch),
        compiler_params=pltpu.CompilerParams(
            vmem_limit_bytes=2 * sum(map(size, near)) + held + (8 << 20)
        ),
        cost_estimate=pl.CostEstimate(
            flops=flops,
            bytes_accessed=0 if light else sum(map(size, list(inputs) + list(out_shape))),
            transcendentals=0,
        ),
        name=name,
    )(*inputs)


def split_evenly(total, unit):
    parts = max(p for p in (1, 2, 4, 5) if total % (p * unit) == 0)
    return parts, total // parts


def my_index():
    return (lax.axis_index("seq") * lax.axis_size("row") + lax.axis_index("row")) * 2 + lax.axis_index("core")


def partner(me, masks, place):
    for bit, mask in enumerate(masks):
        if place >> bit & 1:
            me = me ^ mask
    return me


def place_match(rows, masks, own, me):
    place = lax.broadcasted_iota(jnp.int32, (rows, rows), 0)
    block, inner = lax.div(place, own), lax.rem(place, own)
    device = jnp.full((rows, rows), me, jnp.int32)
    for bit, mask in enumerate(masks):
        device = device ^ (((block >> bit) & 1) * mask)
    return device * own + inner == lax.broadcasted_iota(jnp.int32, (rows, rows), 1)


def to_column(match, row_values):
    return jnp.sum(jnp.where(match, row_values, 0.0), axis=1, keepdims=True)


def to_row(match, column):
    return jnp.sum(jnp.where(match, column, 0.0), axis=0, keepdims=True)


def merge(first, second):
    top = jnp.maximum(first[0:1], second[0:1])
    near, far_off = jnp.exp(first[0:1] - top), jnp.exp(second[0:1] - top)
    return top, first[1:2] * near + second[1:2] * far_off, first[2:3] * near + second[2:3] * far_off


def first_kernel(out_ref):
    out_ref[...] = jnp.zeros_like(out_ref)


def features_kernel(hidden_ref, gain_ref, first_ref, features_ref):
    widened = hidden_ref[...].astype(f32)
    inv_rms = lax.rsqrt(jnp.mean(widened * widened, axis=1, keepdims=True) + epsilon)
    features_ref[...] = (widened * inv_rms * gain_ref[...]).astype(bf16)


def teacher_kernel(blocks_ref, keep_ref, send_ref):
    my_seq = lax.axis_index("seq")
    for k in range(keep_ref.shape[0]):
        keep_ref[k] = blocks_ref[my_seq ^ (2 * k)]
        send_ref[k] = blocks_ref[my_seq ^ (2 * k + 1)]


def join_kernel(first_ref, second_ref, *rest):
    out_ref = rest[-1]
    length = first_ref.shape[0]
    out_ref[:length] = first_ref[...]
    out_ref[length:] = second_ref[...]


def logits_kernel(masks, own, cap, low_ref, high_ref, weight_ref, table_ref, slots_ref, logits_ref, teacher_ref, stats_ref):
    my_seq = lax.axis_index("seq")
    rows = logits_ref.shape[0]
    parts, size = split_evenly(weight_ref.shape[0], 256)
    match = place_match(rows, masks, own, my_index())
    slots = to_column(match, slots_ref[...].astype(f32)).astype(jnp.int32)
    place = (lax.div(slots, cap) ^ my_seq) * cap + lax.rem(slots, cap)
    pick = (place == lax.broadcasted_iota(jnp.int32, (rows, table_ref.shape[0]), 1)).astype(bf16)
    teacher = jnp.dot(pick, table_ref[...], preferred_element_type=f32)
    teacher_ref[...] = teacher.astype(bf16)
    teacher_top = jnp.max(teacher, axis=1, keepdims=True)
    teacher_total = jnp.sum(jnp.exp(teacher - teacher_top), axis=1, keepdims=True)
    logits = jnp.zeros(logits_ref.shape, f32)
    for p in range(parts):
        block = slice(p * size, (p + 1) * size)
        features = jnp.concatenate([low_ref[:, block], high_ref[:, block]], axis=0)
        logits += jnp.dot(features, weight_ref[block, :], preferred_element_type=f32)
    logits_ref[...] = logits
    student_top = jnp.max(logits, axis=1, keepdims=True)
    shifted = jnp.exp(logits - student_top)
    student_total = jnp.sum(shifted, axis=1, keepdims=True)
    cross_sum = jnp.sum(shifted * (logits - teacher), axis=1, keepdims=True)
    nothing = jnp.zeros((1, rows), f32)
    pairs = [
        (to_row(match, student_top), to_row(match, teacher_top)),
        (to_row(match, student_total), to_row(match, teacher_total)),
        (to_row(match, cross_sum), nothing),
        (nothing, nothing),
    ]
    stats_ref[...] = jnp.concatenate([jnp.concatenate(p, axis=1) for p in pairs], axis=0)


def products_kernel(masks, own, logits_ref, teacher_ref, mine_ref, theirs_ref, weight_ref, keep_ref, send_ref):
    parts, size = split_evenly(weight_ref.shape[0], 256)
    logits = logits_ref[...]
    rows = logits.shape[0]
    half = rows // 2
    match = place_match(rows, masks, own, my_index())
    top, total, cross = merge(mine_ref[...], theirs_ref[...])
    center = to_column(match, cross[:, :rows] / total[:, :rows])
    shifted = jnp.exp(logits - to_column(match, top[:, :rows]))
    gaps = shifted * (logits - teacher_ref[...].astype(f32) - center)
    pieces = []
    for at in range(0, rows, own):
        pieces += [gaps[at : at + own], shifted[at : at + own]]
    left = jnp.concatenate(pieces, axis=0).astype(bf16)
    for p in range(parts):
        block = slice(p * size, (p + 1) * size)
        product = lax.dot_general(
            left, weight_ref[block, :], (((1,), (1,)), ((), ())), preferred_element_type=f32
        )
        keep_ref[:, block] = product[: 2 * half]
        send_ref[:, block] = product[2 * half :].astype(bf16)


def share_kernel(masks, own, keep_ref, arrived_ref, share_ref, held, sems):
    me = my_index()
    chips, length, columns = share_ref.shape
    length //= 2
    copies = []
    for p in range(chips):
        block = slice(p * length, (p + 1) * length)
        halves = [
            keep_ref[block, at : at + columns] + arrived_ref[block, at : at + columns].astype(f32)
            for at in (0, columns)
        ]
        held[p] = jnp.concatenate(halves, axis=0).astype(bf16)
        copies.append(
            pltpu.make_async_copy(held.at[p], share_ref.at[partner(me, masks, p) >> 1], sems.at[p])
        )
        copies[-1].start()
    for copy in copies:
        copy.wait()


def terms_kernel(masks, own, mine_ref, theirs_ref, valid_ref, terms_ref, factors_ref):
    me = my_index()
    rows = valid_ref.shape[1]
    chips = factors_ref.shape[0]
    mine, theirs = mine_ref[...], theirs_ref[...]
    tops = jnp.maximum(mine[:, 0, :], theirs[:, 0, :])
    near, other = jnp.exp(mine[:, 0, :] - tops), jnp.exp(theirs[:, 0, :] - tops)
    totals = mine[:, 1, :] * near + theirs[:, 1, :] * other
    crosses = mine[:, 2, :] * near + theirs[:, 2, :] * other
    top = jnp.max(tops, axis=0, keepdims=True)
    scale = jnp.exp(tops - top)
    total = jnp.sum(totals * scale, axis=0, keepdims=True)
    cross = jnp.sum(crosses * scale, axis=0, keepdims=True)[:, :rows]
    lse = top + jnp.log(total)
    student_lse, teacher_lse = lse[:, :rows], lse[:, rows:]
    divergence = cross / total[:, :rows] - student_lse + teacher_lse
    row_weight = valid_ref[...].astype(f32)
    match = place_match(rows, masks, own, me)
    lane = lax.broadcasted_iota(jnp.int32, (rows, 128), 1)
    terms = to_column(match, row_weight)
    for at, values in enumerate((student_lse, teacher_lse, divergence)):
        terms = jnp.where(lane == at, to_column(match, values), terms)
    terms_ref[...] = terms
    scale = row_weight * jnp.exp(tops[:, :rows] - student_lse)
    offset = scale * (crosses[:, :rows] / totals[:, :rows] + (teacher_lse - student_lse - divergence))
    pick = lax.rem(lax.broadcasted_iota(jnp.int32, (4 * own, rows), 0), 2 * own)
    mine = lax.broadcasted_iota(jnp.int32, (4 * own, rows), 1) == me * own + lax.rem(pick, own)
    for p in range(chips):
        both = jnp.where(pick < own, scale[p : p + 1], offset[p : p + 1])
        column = jnp.sum(jnp.where(mine, both, 0.0), axis=1, keepdims=True)
        factors_ref[partner(me, masks, p) >> 1] = jnp.broadcast_to(column, factors_ref.shape[1:])


def head_kernel(low_ref, high_ref, logits_ref, teacher_ref, terms_ref, out_ref, held, sems):
    parts, size = split_evenly(out_ref.shape[0], 256)
    student_lse, teacher_lse = terms_ref[:, 0:1], terms_ref[:, 1:2]
    log_prob = logits_ref[...] - student_lse
    log_gap = log_prob - (teacher_ref[...].astype(f32) - teacher_lse)
    grad = (terms_ref[:, 3:4] * jnp.exp(log_prob) * (log_gap - terms_ref[:, 2:3])).astype(bf16)
    copies = []
    for p in range(parts):
        block = slice(p * size, (p + 1) * size)
        features = jnp.concatenate([low_ref[:, block], high_ref[:, block]], axis=0)
        held[block, :] = lax.dot_general(
            features, grad, (((0,), (0,)), ((), ())), preferred_element_type=f32
        ).astype(bf16)
        rows = pl.ds(p * size, size)
        copies.append(pltpu.make_async_copy(held.at[rows], out_ref.at[rows], sems.at[p]))
        copies[-1].start()
    for copy in copies:
        copy.wait()


def finish_kernel(hidden_ref, gain_ref, shares_ref, factors_ref, out_ref):
    own = hidden_ref.shape[0]
    widened = hidden_ref[...].astype(f32)
    inv_rms = lax.rsqrt(jnp.mean(widened * widened, axis=1, keepdims=True) + epsilon)
    normed = widened * inv_rms
    both = shares_ref[0].astype(f32) * factors_ref[0][:, 0:1]
    for p in range(1, shares_ref.shape[0]):
        both += shares_ref[p].astype(f32) * factors_ref[p][:, 0:1]
    sums = [both[at : at + own] + both[at + own : at + 2 * own] for at in (0, 2 * own)]
    norm_grad = jnp.concatenate(sums, axis=1) * gain_ref[...]
    mean = jnp.mean(norm_grad * normed, axis=1, keepdims=True)
    out_ref[...] = (inv_rms * (norm_grad - normed * mean)).astype(bf16)


def shards(hidden, norm_gain, head_weight, teacher_logits, teacher_slot, valid_tokens):
    n_seq, n_row = lax.axis_size("seq"), lax.axis_size("row")
    chips = n_seq * n_row
    count = chips * 2
    own, depth = hidden.shape
    width = head_weight.shape[1]
    rows = own * count
    cap = teacher_logits.shape[0]
    columns = depth // 2
    gain = norm_gain[None]
    masks = [1 << b for b in reversed(range(count.bit_length() - 1))]
    seq_masks = [m for m in reversed(masks) if m >= n_row * 2]

    def swap(value, mask):
        return lax.ppermute(value, axes, [(i, i ^ mask) for i in range(count)])

    def sems(number):
        return pltpu.SemaphoreType.DMA((number,))

    (first,) = call(first_kernel, "first", [shape((8, 128), f32)], [], [], [fast], flops=10**10)
    (gathered,) = call(
        features_kernel,
        "features",
        [shape((own, depth), bf16)],
        [hidden, gain, first],
        [fast] * 3,
        [fast],
    )
    half_blocks = shape((n_seq // 2, cap, width), bf16)
    keep, send = call(
        teacher_kernel,
        "teacher_blocks",
        [half_blocks] * 2,
        [teacher_logits.transpose(1, 0, 2)],
        [fast],
        [fast] * 2,
        flops=10**10,
    )
    held = jnp.concatenate([keep, swap(send, seq_masks[0])], axis=1)
    behind = len(masks) - len(seq_masks)
    for step, mask in enumerate(masks[:-1]):
        arrived = swap(gathered, mask)
        bit = step - behind + 1
        if 1 <= bit < len(seq_masks):
            pairs = held.reshape((held.shape[0] // 2, 2) + held.shape[1:])
            held = jnp.concatenate([pairs[:, 0], swap(pairs[:, 1], seq_masks[bit])], axis=1)
        if step < len(masks) - 2:
            gathered = jnp.concatenate([gathered, arrived], axis=0)
    (gathered,) = call(
        join_kernel, "join", [shape((rows // 2, depth), bf16)], [gathered, arrived], [fast] * 2, [fast]
    )
    low, held = lax.optimization_barrier((gathered, held))
    high = swap(low, masks[-1])

    def with_masks(kernel, *more):
        return lambda *refs: kernel(masks, own, *more, *refs)

    logits, teacher, stats = call(
        with_masks(logits_kernel, cap),
        "logits",
        [shape((rows, width), f32), shape((rows, width), bf16), shape((4, 2 * rows), f32)],
        [low, high, head_weight, held[0], teacher_slot[None]],
        [fast] * 5,
        [fast] * 3,
        flops=2 * rows * depth * width,
    )
    keep, send = call(
        with_masks(products_kernel),
        "products",
        [shape((rows, depth), f32), shape((rows, depth), bf16)],
        [logits, teacher, stats, swap(stats, masks[-1]), head_weight],
        [fast] * 5,
        [fast] * 2,
        flops=4 * rows * depth * width,
    )
    def join(value, mask, *after):
        (joined,) = call(
            join_kernel,
            "join_statistics",
            [shape((2 * value.shape[0], 4, 2 * rows), f32)],
            [value, swap(value, mask), *after],
            [fast] * 2 + [far] * len(after),
            [fast],
            light=True,
        )
        return joined

    stats = join(stats[None], masks[0], send)
    stats, send = lax.optimization_barrier((stats, send))
    (share,) = call(
        with_masks(share_kernel),
        "share",
        [shape((chips, 4 * own, columns), bf16)],
        [keep, swap(send, masks[-1])],
        [fast] * 2,
        [far],
        [pltpu.VMEM((chips, 4 * own, columns), bf16), sems(chips)],
    )
    for step, mask in enumerate(masks[1:-1]):
        if step == 0:
            stats, share = lax.optimization_barrier((join(stats, mask, share), share))
        else:
            stats = join(stats, mask)
    other_stats = swap(stats, masks[-1])
    shares = lax.all_to_all(share, ("seq", "row"), split_axis=0, concat_axis=0, tiled=True)
    terms, factors = call(
        with_masks(terms_kernel),
        "terms",
        [shape((rows, 128), f32), shape((chips, 4 * own, 128), f32)],
        [stats, other_stats, valid_tokens[None]],
        [fast] * 3,
        [fast] * 2,
        light=True,
    )
    (grad_head,) = call(
        head_kernel,
        "grad_head",
        [shape(head_weight.shape, bf16)],
        [low, high, logits, teacher, terms],
        [fast] * 5,
        [far],
        [pltpu.VMEM((depth, width), bf16), sems(5)],
        light=True,
    )
    (grad_hidden,) = call(
        finish_kernel,
        "finish",
        [shape((own, depth), bf16)],
        [hidden, gain, shares, factors],
        [fast] * 4,
        [fast],
    )
    return (grad_hidden, grad_head)


def solution(mesh):
    n_seq, n_vocab = mesh.shape["seq"], mesh.shape["vocab"]
    finer = jax.sharding.Mesh(mesh.devices.reshape(n_seq, n_vocab // 2, 2), axes)
    placed = (
        P(axes, None),
        P(),
        P(None, axes),
        P("seq", None, ("row", "core")),
        P(),
        P(),
    )
    return jax.shard_map(
        shards,
        mesh=finer,
        in_specs=placed,
        out_specs=(P(axes, None), P(None, axes)),
        check_vma=False,
    )
```

```python
import math

import jax
import jax.numpy as jnp
from jax import lax
from jax.experimental import pallas as pl
from jax.experimental.pallas import tpu as pltpu
from jax.sharding import PartitionSpec as P

epsilon = 1e-06
axes = ("seq", "row", "core")
fast, far = pltpu.VMEM, pl.ANY
shape = jax.ShapeDtypeStruct
f32, bf16 = jnp.float32, jnp.bfloat16


def call(kernel, name, out_shape, inputs, spaces, out_spaces, scratch=(), flops=0, light=False):
    def size(leaf):
        return leaf.size * leaf.dtype.itemsize

    near = [x for x, s in zip(inputs, spaces) if s == fast]
    near += [x for x, s in zip(out_shape, out_spaces) if s == fast]
    held = sum(x.dtype.itemsize * math.prod(x.shape) for x in scratch if x.memory_space == fast)
    return pl.pallas_call(
        kernel,
        out_shape=list(out_shape),
        in_specs=[pl.BlockSpec(memory_space=s) for s in spaces],
        out_specs=[pl.BlockSpec(memory_space=s) for s in out_spaces],
        scratch_shapes=list(scratch),
        compiler_params=pltpu.CompilerParams(
            vmem_limit_bytes=2 * sum(map(size, near)) + held + (8 << 20)
        ),
        cost_estimate=pl.CostEstimate(
            flops=flops,
            bytes_accessed=0 if light else sum(map(size, list(inputs) + list(out_shape))),
            transcendentals=0,
        ),
        name=name,
    )(*inputs)


def split_evenly(total, unit):
    parts = max(p for p in (1, 2, 4, 5) if total % (p * unit) == 0)
    return parts, total // parts


def my_index():
    return (lax.axis_index("seq") * lax.axis_size("row") + lax.axis_index("row")) * 2 + lax.axis_index("core")


def partner(me, masks, place):
    for bit, mask in enumerate(masks):
        if place >> bit & 1:
            me = me ^ mask
    return me


def chip_of(device):
    chip = device >> 1
    n_row = lax.axis_size("row")
    return lax.rem(chip, n_row) * lax.axis_size("seq") + lax.div(chip, n_row)


def place_match(rows, masks, own, me):
    place = lax.broadcasted_iota(jnp.int32, (rows, rows), 0)
    block, inner = lax.div(place, own), lax.rem(place, own)
    device = jnp.full((rows, rows), me, jnp.int32)
    for bit, mask in enumerate(masks):
        device = device ^ (((block >> bit) & 1) * mask)
    return device * own + inner == lax.broadcasted_iota(jnp.int32, (rows, rows), 1)


def to_column(match, row_values):
    return jnp.sum(jnp.where(match, row_values, 0.0), axis=1, keepdims=True)


def to_row(match, column):
    return jnp.sum(jnp.where(match, column, 0.0), axis=0, keepdims=True)


def merge(first, second):
    top = jnp.maximum(first[0:1], second[0:1])
    near, far_off = jnp.exp(first[0:1] - top), jnp.exp(second[0:1] - top)
    return top, first[1:2] * near + second[1:2] * far_off, first[2:3] * near + second[2:3] * far_off


def first_kernel(out_ref):
    out_ref[...] = jnp.zeros_like(out_ref)


def features_kernel(hidden_ref, gain_ref, first_ref, features_ref):
    widened = hidden_ref[...].astype(f32)
    inv_rms = lax.rsqrt(jnp.mean(widened * widened, axis=1, keepdims=True) + epsilon)
    features_ref[...] = (widened * inv_rms * gain_ref[...]).astype(bf16)


def teacher_kernel(blocks_ref, keep_ref, send_ref):
    my_seq = lax.axis_index("seq")
    for k in range(keep_ref.shape[0]):
        keep_ref[k] = blocks_ref[my_seq ^ (2 * k)]
        send_ref[k] = blocks_ref[my_seq ^ (2 * k + 1)]


def join_kernel(first_ref, second_ref, *rest):
    out_ref = rest[-1]
    length = first_ref.shape[0]
    out_ref[:length] = first_ref[...]
    out_ref[length:] = second_ref[...]


def logits_kernel(masks, own, cap, low_ref, high_ref, weight_ref, table_ref, slots_ref, logits_ref, teacher_ref, stats_ref):
    my_seq = lax.axis_index("seq")
    rows = logits_ref.shape[0]
    parts, size = split_evenly(weight_ref.shape[0], 256)
    match = place_match(rows, masks, own, my_index())
    slots = to_column(match, slots_ref[...].astype(f32)).astype(jnp.int32)
    place = (lax.div(slots, cap) ^ my_seq) * cap + lax.rem(slots, cap)
    pick = (place == lax.broadcasted_iota(jnp.int32, (rows, table_ref.shape[0]), 1)).astype(bf16)
    teacher = jnp.dot(pick, table_ref[...], preferred_element_type=f32)
    teacher_ref[...] = teacher.astype(bf16)
    teacher_top = jnp.max(teacher, axis=1, keepdims=True)
    teacher_total = jnp.sum(jnp.exp(teacher - teacher_top), axis=1, keepdims=True)
    logits = jnp.zeros(logits_ref.shape, f32)
    for p in range(parts):
        block = slice(p * size, (p + 1) * size)
        features = jnp.concatenate([low_ref[:, block], high_ref[:, block]], axis=0)
        logits += jnp.dot(features, weight_ref[block, :], preferred_element_type=f32)
    logits_ref[...] = logits
    student_top = jnp.max(logits, axis=1, keepdims=True)
    shifted = jnp.exp(logits - student_top)
    student_total = jnp.sum(shifted, axis=1, keepdims=True)
    cross_sum = jnp.sum(shifted * (logits - teacher), axis=1, keepdims=True)
    nothing = jnp.zeros((1, rows), f32)
    pairs = [
        (to_row(match, student_top), to_row(match, teacher_top)),
        (to_row(match, student_total), to_row(match, teacher_total)),
        (to_row(match, cross_sum), nothing),
        (nothing, nothing),
    ]
    stats_ref[...] = jnp.concatenate([jnp.concatenate(p, axis=1) for p in pairs], axis=0)


def products_kernel(masks, own, logits_ref, teacher_ref, mine_ref, theirs_ref, weight_ref, keep_ref, send_ref):
    parts, size = split_evenly(weight_ref.shape[0], 256)
    logits = logits_ref[...]
    rows = logits.shape[0]
    half = rows // 2
    match = place_match(rows, masks, own, my_index())
    top, total, cross = merge(mine_ref[...], theirs_ref[...])
    center = to_column(match, cross[:, :rows] / total[:, :rows])
    shifted = jnp.exp(logits - to_column(match, top[:, :rows]))
    gaps = shifted * (logits - teacher_ref[...].astype(f32) - center)
    pieces = []
    for at in range(0, rows, own):
        pieces += [gaps[at : at + own], shifted[at : at + own]]
    left = jnp.concatenate(pieces, axis=0).astype(bf16)
    for p in range(parts):
        block = slice(p * size, (p + 1) * size)
        product = lax.dot_general(
            left, weight_ref[block, :], (((1,), (1,)), ((), ())), preferred_element_type=f32
        )
        keep_ref[:, block] = product[: 2 * half]
        send_ref[:, block] = product[2 * half :].astype(bf16)


def share_kernel(masks, own, keep_ref, arrived_ref, share_ref, held, sems):
    me = my_index()
    chips, length, columns = share_ref.shape
    length //= 2
    copies = []
    for p in range(chips):
        block = slice(p * length, (p + 1) * length)
        halves = [
            keep_ref[block, at : at + columns] + arrived_ref[block, at : at + columns].astype(f32)
            for at in (0, columns)
        ]
        held[p] = jnp.concatenate(halves, axis=0).astype(bf16)
        copies.append(
            pltpu.make_async_copy(held.at[p], share_ref.at[chip_of(partner(me, masks, p))], sems.at[p])
        )
        copies[-1].start()
    for copy in copies:
        copy.wait()


def terms_kernel(masks, own, mine_ref, theirs_ref, valid_ref, terms_ref, factors_ref):
    me = my_index()
    rows = valid_ref.shape[1]
    chips = factors_ref.shape[0]
    mine, theirs = mine_ref[...], theirs_ref[...]
    tops = jnp.maximum(mine[:, 0, :], theirs[:, 0, :])
    near, other = jnp.exp(mine[:, 0, :] - tops), jnp.exp(theirs[:, 0, :] - tops)
    totals = mine[:, 1, :] * near + theirs[:, 1, :] * other
    crosses = mine[:, 2, :] * near + theirs[:, 2, :] * other
    top = jnp.max(tops, axis=0, keepdims=True)
    scale = jnp.exp(tops - top)
    total = jnp.sum(totals * scale, axis=0, keepdims=True)
    cross = jnp.sum(crosses * scale, axis=0, keepdims=True)[:, :rows]
    lse = top + jnp.log(total)
    student_lse, teacher_lse = lse[:, :rows], lse[:, rows:]
    divergence = cross / total[:, :rows] - student_lse + teacher_lse
    row_weight = valid_ref[...].astype(f32)
    match = place_match(rows, masks, own, me)
    lane = lax.broadcasted_iota(jnp.int32, (rows, 128), 1)
    terms = to_column(match, row_weight)
    for at, values in enumerate((student_lse, teacher_lse, divergence)):
        terms = jnp.where(lane == at, to_column(match, values), terms)
    terms_ref[...] = terms
    scale = row_weight * jnp.exp(tops[:, :rows] - student_lse)
    offset = scale * (crosses[:, :rows] / totals[:, :rows] + (teacher_lse - student_lse - divergence))
    pick = lax.rem(lax.broadcasted_iota(jnp.int32, (4 * own, rows), 0), 2 * own)
    mine = lax.broadcasted_iota(jnp.int32, (4 * own, rows), 1) == me * own + lax.rem(pick, own)
    for p in range(chips):
        both = jnp.where(pick < own, scale[p : p + 1], offset[p : p + 1])
        column = jnp.sum(jnp.where(mine, both, 0.0), axis=1, keepdims=True)
        factors_ref[chip_of(partner(me, masks, p))] = jnp.broadcast_to(column, factors_ref.shape[1:])


def head_kernel(low_ref, high_ref, logits_ref, teacher_ref, terms_ref, out_ref, held, sems):
    parts, size = split_evenly(out_ref.shape[0], 256)
    student_lse, teacher_lse = terms_ref[:, 0:1], terms_ref[:, 1:2]
    log_prob = logits_ref[...] - student_lse
    log_gap = log_prob - (teacher_ref[...].astype(f32) - teacher_lse)
    grad = (terms_ref[:, 3:4] * jnp.exp(log_prob) * (log_gap - terms_ref[:, 2:3])).astype(bf16)
    copies = []
    for p in range(parts):
        block = slice(p * size, (p + 1) * size)
        features = jnp.concatenate([low_ref[:, block], high_ref[:, block]], axis=0)
        held[block, :] = lax.dot_general(
            features, grad, (((0,), (0,)), ((), ())), preferred_element_type=f32
        ).astype(bf16)
        rows = pl.ds(p * size, size)
        copies.append(pltpu.make_async_copy(held.at[rows], out_ref.at[rows], sems.at[p]))
        copies[-1].start()
    for copy in copies:
        copy.wait()


def finish_kernel(hidden_ref, gain_ref, shares_ref, factors_ref, out_ref):
    own = hidden_ref.shape[0]
    widened = hidden_ref[...].astype(f32)
    inv_rms = lax.rsqrt(jnp.mean(widened * widened, axis=1, keepdims=True) + epsilon)
    normed = widened * inv_rms
    both = shares_ref[0].astype(f32) * factors_ref[0][:, 0:1]
    for p in range(1, shares_ref.shape[0]):
        both += shares_ref[p].astype(f32) * factors_ref[p][:, 0:1]
    sums = [both[at : at + own] + both[at + own : at + 2 * own] for at in (0, 2 * own)]
    norm_grad = jnp.concatenate(sums, axis=1) * gain_ref[...]
    mean = jnp.mean(norm_grad * normed, axis=1, keepdims=True)
    out_ref[...] = (inv_rms * (norm_grad - normed * mean)).astype(bf16)


def shards(hidden, norm_gain, head_weight, teacher_logits, teacher_slot, valid_tokens):
    n_seq, n_row = lax.axis_size("seq"), lax.axis_size("row")
    chips = n_seq * n_row
    count = chips * 2
    own, depth = hidden.shape
    width = head_weight.shape[1]
    rows = own * count
    cap = teacher_logits.shape[0]
    columns = depth // 2
    gain = norm_gain[None]
    masks = [1 << b for b in reversed(range(count.bit_length() - 1))]
    seq_masks = [m for m in reversed(masks) if m >= n_row * 2]

    def swap(value, mask):
        return lax.ppermute(value, axes, [(i, i ^ mask) for i in range(count)])

    def sems(number):
        return pltpu.SemaphoreType.DMA((number,))

    (first,) = call(first_kernel, "first", [shape((8, 128), f32)], [], [], [fast], flops=10**10)
    (gathered,) = call(
        features_kernel,
        "features",
        [shape((own, depth), bf16)],
        [hidden, gain, first],
        [fast] * 3,
        [fast],
    )
    half_blocks = shape((n_seq // 2, cap, width), bf16)
    keep, send = call(
        teacher_kernel,
        "teacher_blocks",
        [half_blocks] * 2,
        [teacher_logits.transpose(1, 0, 2)],
        [fast],
        [fast] * 2,
        flops=10**10,
    )
    held = jnp.concatenate([keep, swap(send, seq_masks[0])], axis=1)
    behind = len(masks) - len(seq_masks)
    for step, mask in enumerate(masks[:-1]):
        arrived = swap(gathered, mask)
        bit = step - behind + 1
        if 1 <= bit < len(seq_masks):
            pairs = held.reshape((held.shape[0] // 2, 2) + held.shape[1:])
            held = jnp.concatenate([pairs[:, 0], swap(pairs[:, 1], seq_masks[bit])], axis=1)
        if step < len(masks) - 2:
            gathered = jnp.concatenate([gathered, arrived], axis=0)
    (gathered,) = call(
        join_kernel, "join", [shape((rows // 2, depth), bf16)], [gathered, arrived], [fast] * 2, [fast]
    )
    low, held = lax.optimization_barrier((gathered, held))
    high = swap(low, masks[-1])

    def with_masks(kernel, *more):
        return lambda *refs: kernel(masks, own, *more, *refs)

    logits, teacher, stats = call(
        with_masks(logits_kernel, cap),
        "logits",
        [shape((rows, width), f32), shape((rows, width), bf16), shape((4, 2 * rows), f32)],
        [low, high, head_weight, held[0], teacher_slot[None]],
        [fast] * 5,
        [fast] * 3,
        flops=2 * rows * depth * width,
    )
    keep, send = call(
        with_masks(products_kernel),
        "products",
        [shape((rows, depth), f32), shape((rows, depth), bf16)],
        [logits, teacher, stats, swap(stats, masks[-1]), head_weight],
        [fast] * 5,
        [fast] * 2,
        flops=4 * rows * depth * width,
    )
    def join(value, mask, *after):
        (joined,) = call(
            join_kernel,
            "join_statistics",
            [shape((2 * value.shape[0], 4, 2 * rows), f32)],
            [value, swap(value, mask), *after],
            [fast] * 2 + [far] * len(after),
            [fast],
            light=True,
        )
        return joined

    stats = join(stats[None], masks[0], send)
    stats, send = lax.optimization_barrier((stats, send))
    (share,) = call(
        with_masks(share_kernel),
        "share",
        [shape((chips, 4 * own, columns), bf16)],
        [keep, swap(send, masks[-1])],
        [fast] * 2,
        [far],
        [pltpu.VMEM((chips, 4 * own, columns), bf16), sems(chips)],
    )
    for step, mask in enumerate(masks[1:-1]):
        if step == 0:
            stats, share = lax.optimization_barrier((join(stats, mask, share), share))
        else:
            stats = join(stats, mask)
    other_stats = swap(stats, masks[-1])
    shares = lax.all_to_all(share, ("row", "seq"), split_axis=0, concat_axis=0, tiled=True)
    terms, factors = call(
        with_masks(terms_kernel),
        "terms",
        [shape((rows, 128), f32), shape((chips, 4 * own, 128), f32)],
        [stats, other_stats, valid_tokens[None]],
        [fast] * 3,
        [fast] * 2,
        light=True,
    )
    (grad_head,) = call(
        head_kernel,
        "grad_head",
        [shape(head_weight.shape, bf16)],
        [low, high, logits, teacher, terms],
        [fast] * 5,
        [far],
        [pltpu.VMEM((depth, width), bf16), sems(5)],
        light=True,
    )
    (grad_hidden,) = call(
        finish_kernel,
        "finish",
        [shape((own, depth), bf16)],
        [hidden, gain, shares, factors],
        [fast] * 4,
        [fast],
    )
    return (grad_hidden, grad_head)


def solution(mesh):
    n_seq, n_vocab = mesh.shape["seq"], mesh.shape["vocab"]
    finer = jax.sharding.Mesh(mesh.devices.reshape(n_seq, n_vocab // 2, 2), axes)
    placed = (
        P(axes, None),
        P(),
        P(None, axes),
        P("seq", None, ("row", "core")),
        P(),
        P(),
    )
    return jax.shard_map(
        shards,
        mesh=finer,
        in_specs=placed,
        out_specs=(P(axes, None), P(None, axes)),
        check_vma=False,
    )
```

```python
import math

import jax
import jax.numpy as jnp
from jax import lax
from jax.experimental import pallas as pl
from jax.experimental.pallas import tpu as pltpu
from jax.sharding import PartitionSpec as P

epsilon = 1e-06
axes = ("seq", "row", "core")
fast, far = pltpu.VMEM, pl.ANY
shape = jax.ShapeDtypeStruct
f32, bf16 = jnp.float32, jnp.bfloat16


def call(kernel, name, out_shape, inputs, spaces, out_spaces, scratch=(), flops=0, light=False):
    def size(leaf):
        return leaf.size * leaf.dtype.itemsize

    near = [x for x, s in zip(inputs, spaces) if s == fast]
    near += [x for x, s in zip(out_shape, out_spaces) if s == fast]
    held = sum(x.dtype.itemsize * math.prod(x.shape) for x in scratch if x.memory_space == fast)
    return pl.pallas_call(
        kernel,
        out_shape=list(out_shape),
        in_specs=[pl.BlockSpec(memory_space=s) for s in spaces],
        out_specs=[pl.BlockSpec(memory_space=s) for s in out_spaces],
        scratch_shapes=list(scratch),
        compiler_params=pltpu.CompilerParams(
            vmem_limit_bytes=2 * sum(map(size, near)) + held + (8 << 20)
        ),
        cost_estimate=pl.CostEstimate(
            flops=flops,
            bytes_accessed=0 if light else sum(map(size, list(inputs) + list(out_shape))),
            transcendentals=0,
        ),
        name=name,
    )(*inputs)


def split_evenly(total, unit):
    parts = max(p for p in (1, 2, 4, 5) if total % (p * unit) == 0)
    return parts, total // parts


def my_index():
    return (lax.axis_index("seq") * lax.axis_size("row") + lax.axis_index("row")) * 2 + lax.axis_index("core")


def partner(me, masks, place):
    for bit, mask in enumerate(masks):
        if place >> bit & 1:
            me = me ^ mask
    return me


def by_core(masks, core):
    steps = list(masks[:-1])
    if len(steps) > 1:
        steps[-2:] = [jnp.where(core != 0, b, a) for a, b in (steps[-2:], steps[:-3:-1])]
    return steps


def place_match(rows, masks, own, me):
    place = lax.broadcasted_iota(jnp.int32, (rows, rows), 0)
    block, inner = lax.div(place, own), lax.rem(place, own)
    swapped = (block >> (len(masks) - 1)) & 1
    device = me ^ swapped
    for bit, mask in enumerate(by_core(masks, device & 1)):
        device = device ^ (((block >> bit) & 1) * mask)
    return device * own + inner == lax.broadcasted_iota(jnp.int32, (rows, rows), 1)


def to_column(match, row_values):
    return jnp.sum(jnp.where(match, row_values, 0.0), axis=1, keepdims=True)


def to_row(match, column):
    return jnp.sum(jnp.where(match, column, 0.0), axis=0, keepdims=True)


def merge(first, second):
    top = jnp.maximum(first[0:1], second[0:1])
    near, far_off = jnp.exp(first[0:1] - top), jnp.exp(second[0:1] - top)
    return top, first[1:2] * near + second[1:2] * far_off, first[2:3] * near + second[2:3] * far_off


def first_kernel(out_ref):
    out_ref[...] = jnp.zeros_like(out_ref)


def features_kernel(hidden_ref, gain_ref, first_ref, features_ref):
    widened = hidden_ref[...].astype(f32)
    inv_rms = lax.rsqrt(jnp.mean(widened * widened, axis=1, keepdims=True) + epsilon)
    features_ref[...] = (widened * inv_rms * gain_ref[...]).astype(bf16)


def teacher_kernel(blocks_ref, keep_ref, send_ref):
    my_seq = lax.axis_index("seq")
    for k in range(keep_ref.shape[0]):
        keep_ref[k] = blocks_ref[my_seq ^ (2 * k)]
        send_ref[k] = blocks_ref[my_seq ^ (2 * k + 1)]


def join_kernel(first_ref, second_ref, *rest):
    out_ref = rest[-1]
    length = first_ref.shape[0]
    out_ref[:length] = first_ref[...]
    out_ref[length:] = second_ref[...]


def logits_kernel(masks, own, cap, low_ref, high_ref, weight_ref, table_ref, slots_ref, logits_ref, teacher_ref, stats_ref):
    my_seq = lax.axis_index("seq")
    rows = logits_ref.shape[0]
    parts, size = split_evenly(weight_ref.shape[0], 256)
    match = place_match(rows, masks, own, my_index())
    slots = to_column(match, slots_ref[...].astype(f32)).astype(jnp.int32)
    place = (lax.div(slots, cap) ^ my_seq) * cap + lax.rem(slots, cap)
    pick = (place == lax.broadcasted_iota(jnp.int32, (rows, table_ref.shape[0]), 1)).astype(bf16)
    teacher = jnp.dot(pick, table_ref[...], preferred_element_type=f32)
    teacher_ref[...] = teacher.astype(bf16)
    teacher_top = jnp.max(teacher, axis=1, keepdims=True)
    teacher_total = jnp.sum(jnp.exp(teacher - teacher_top), axis=1, keepdims=True)
    logits = jnp.zeros(logits_ref.shape, f32)
    for p in range(parts):
        block = slice(p * size, (p + 1) * size)
        features = jnp.concatenate([low_ref[:, block], high_ref[:, block]], axis=0)
        logits += jnp.dot(features, weight_ref[block, :], preferred_element_type=f32)
    logits_ref[...] = logits
    student_top = jnp.max(logits, axis=1, keepdims=True)
    shifted = jnp.exp(logits - student_top)
    student_total = jnp.sum(shifted, axis=1, keepdims=True)
    cross_sum = jnp.sum(shifted * (logits - teacher), axis=1, keepdims=True)
    nothing = jnp.zeros((1, rows), f32)
    pairs = [
        (to_row(match, student_top), to_row(match, teacher_top)),
        (to_row(match, student_total), to_row(match, teacher_total)),
        (to_row(match, cross_sum), nothing),
        (nothing, nothing),
    ]
    stats_ref[...] = jnp.concatenate([jnp.concatenate(p, axis=1) for p in pairs], axis=0)


def products_kernel(masks, own, logits_ref, teacher_ref, mine_ref, theirs_ref, weight_ref, keep_ref, send_ref):
    parts, size = split_evenly(weight_ref.shape[0], 256)
    logits = logits_ref[...]
    rows = logits.shape[0]
    half = rows // 2
    match = place_match(rows, masks, own, my_index())
    top, total, cross = merge(mine_ref[...], theirs_ref[...])
    center = to_column(match, cross[:, :rows] / total[:, :rows])
    shifted = jnp.exp(logits - to_column(match, top[:, :rows]))
    gaps = shifted * (logits - teacher_ref[...].astype(f32) - center)
    pieces = []
    for at in range(0, rows, own):
        pieces += [gaps[at : at + own], shifted[at : at + own]]
    left = jnp.concatenate(pieces, axis=0).astype(bf16)
    for p in range(parts):
        block = slice(p * size, (p + 1) * size)
        product = lax.dot_general(
            left, weight_ref[block, :], (((1,), (1,)), ((), ())), preferred_element_type=f32
        )
        keep_ref[:, block] = product[: 2 * half]
        send_ref[:, block] = product[2 * half :].astype(bf16)


def share_kernel(masks, own, keep_ref, arrived_ref, share_ref, held, sems):
    me = my_index()
    chips, length, columns = share_ref.shape
    length //= 2
    copies = []
    for p in range(chips):
        block = slice(p * length, (p + 1) * length)
        halves = [
            keep_ref[block, at : at + columns] + arrived_ref[block, at : at + columns].astype(f32)
            for at in (0, columns)
        ]
        held[p] = jnp.concatenate(halves, axis=0).astype(bf16)
        copies.append(
            pltpu.make_async_copy(held.at[p], share_ref.at[partner(me, by_core(masks, me & 1), p) >> 1], sems.at[p])
        )
        copies[-1].start()
    for copy in copies:
        copy.wait()


def terms_kernel(masks, own, mine_ref, theirs_ref, valid_ref, terms_ref, factors_ref):
    me = my_index()
    rows = valid_ref.shape[1]
    chips = factors_ref.shape[0]
    mine, theirs = mine_ref[...], theirs_ref[...]
    tops = jnp.maximum(mine[:, 0, :], theirs[:, 0, :])
    near, other = jnp.exp(mine[:, 0, :] - tops), jnp.exp(theirs[:, 0, :] - tops)
    totals = mine[:, 1, :] * near + theirs[:, 1, :] * other
    crosses = mine[:, 2, :] * near + theirs[:, 2, :] * other
    top = jnp.max(tops, axis=0, keepdims=True)
    scale = jnp.exp(tops - top)
    total = jnp.sum(totals * scale, axis=0, keepdims=True)
    cross = jnp.sum(crosses * scale, axis=0, keepdims=True)[:, :rows]
    lse = top + jnp.log(total)
    student_lse, teacher_lse = lse[:, :rows], lse[:, rows:]
    divergence = cross / total[:, :rows] - student_lse + teacher_lse
    row_weight = valid_ref[...].astype(f32)
    match = place_match(rows, masks, own, me)
    lane = lax.broadcasted_iota(jnp.int32, (rows, 128), 1)
    terms = to_column(match, row_weight)
    for at, values in enumerate((student_lse, teacher_lse, divergence)):
        terms = jnp.where(lane == at, to_column(match, values), terms)
    terms_ref[...] = terms
    scale = row_weight * jnp.exp(tops[:, :rows] - student_lse)
    offset = scale * (crosses[:, :rows] / totals[:, :rows] + (teacher_lse - student_lse - divergence))
    pick = lax.rem(lax.broadcasted_iota(jnp.int32, (4 * own, rows), 0), 2 * own)
    mine = lax.broadcasted_iota(jnp.int32, (4 * own, rows), 1) == me * own + lax.rem(pick, own)
    for p in range(chips):
        both = jnp.where(pick < own, scale[p : p + 1], offset[p : p + 1])
        column = jnp.sum(jnp.where(mine, both, 0.0), axis=1, keepdims=True)
        factors_ref[partner(me, masks, p) >> 1] = jnp.broadcast_to(column, factors_ref.shape[1:])


def head_kernel(low_ref, high_ref, logits_ref, teacher_ref, terms_ref, out_ref, held, sems):
    parts, size = split_evenly(out_ref.shape[0], 256)
    student_lse, teacher_lse = terms_ref[:, 0:1], terms_ref[:, 1:2]
    log_prob = logits_ref[...] - student_lse
    log_gap = log_prob - (teacher_ref[...].astype(f32) - teacher_lse)
    grad = (terms_ref[:, 3:4] * jnp.exp(log_prob) * (log_gap - terms_ref[:, 2:3])).astype(bf16)
    copies = []
    for p in range(parts):
        block = slice(p * size, (p + 1) * size)
        features = jnp.concatenate([low_ref[:, block], high_ref[:, block]], axis=0)
        held[block, :] = lax.dot_general(
            features, grad, (((0,), (0,)), ((), ())), preferred_element_type=f32
        ).astype(bf16)
        rows = pl.ds(p * size, size)
        copies.append(pltpu.make_async_copy(held.at[rows], out_ref.at[rows], sems.at[p]))
        copies[-1].start()
    for copy in copies:
        copy.wait()


def finish_kernel(hidden_ref, gain_ref, shares_ref, factors_ref, out_ref):
    own = hidden_ref.shape[0]
    widened = hidden_ref[...].astype(f32)
    inv_rms = lax.rsqrt(jnp.mean(widened * widened, axis=1, keepdims=True) + epsilon)
    normed = widened * inv_rms
    both = shares_ref[0].astype(f32) * factors_ref[0][:, 0:1]
    for p in range(1, shares_ref.shape[0]):
        both += shares_ref[p].astype(f32) * factors_ref[p][:, 0:1]
    sums = [both[at : at + own] + both[at + own : at + 2 * own] for at in (0, 2 * own)]
    norm_grad = jnp.concatenate(sums, axis=1) * gain_ref[...]
    mean = jnp.mean(norm_grad * normed, axis=1, keepdims=True)
    out_ref[...] = (inv_rms * (norm_grad - normed * mean)).astype(bf16)


def shards(hidden, norm_gain, head_weight, teacher_logits, teacher_slot, valid_tokens):
    n_seq, n_row = lax.axis_size("seq"), lax.axis_size("row")
    chips = n_seq * n_row
    count = chips * 2
    own, depth = hidden.shape
    width = head_weight.shape[1]
    rows = own * count
    cap = teacher_logits.shape[0]
    columns = depth // 2
    gain = norm_gain[None]
    masks = [1 << b for b in reversed(range(count.bit_length() - 1))]
    seq_masks = [m for m in reversed(masks) if m >= n_row * 2]

    def swap(value, mask, other=None):
        pairs = [(i, i ^ (mask if i & 1 == 0 or other is None else other)) for i in range(count)]
        return lax.ppermute(value, axes, pairs)

    def sems(number):
        return pltpu.SemaphoreType.DMA((number,))

    (first,) = call(first_kernel, "first", [shape((8, 128), f32)], [], [], [fast], flops=10**10)
    (gathered,) = call(
        features_kernel,
        "features",
        [shape((own, depth), bf16)],
        [hidden, gain, first],
        [fast] * 3,
        [fast],
    )
    half_blocks = shape((n_seq // 2, cap, width), bf16)
    keep, send = call(
        teacher_kernel,
        "teacher_blocks",
        [half_blocks] * 2,
        [teacher_logits.transpose(1, 0, 2)],
        [fast],
        [fast] * 2,
        flops=10**10,
    )
    held = jnp.concatenate([keep, swap(send, seq_masks[0])], axis=1)
    behind = len(masks) - len(seq_masks)
    for step, mask in enumerate(masks[:-1]):
        last = len(masks) - 2
        other = masks[2 * last - 1 - step] if step >= last - 1 >= 0 else None
        arrived = swap(gathered, mask, other)
        bit = step - behind + 1
        if 1 <= bit < len(seq_masks):
            pairs = held.reshape((held.shape[0] // 2, 2) + held.shape[1:])
            held = jnp.concatenate([pairs[:, 0], swap(pairs[:, 1], seq_masks[bit])], axis=1)
        if step < len(masks) - 2:
            gathered = jnp.concatenate([gathered, arrived], axis=0)
    (gathered,) = call(
        join_kernel, "join", [shape((rows // 2, depth), bf16)], [gathered, arrived], [fast] * 2, [fast]
    )
    low, held = lax.optimization_barrier((gathered, held))
    high = swap(low, masks[-1])

    def with_masks(kernel, *more):
        return lambda *refs: kernel(masks, own, *more, *refs)

    logits, teacher, stats = call(
        with_masks(logits_kernel, cap),
        "logits",
        [shape((rows, width), f32), shape((rows, width), bf16), shape((4, 2 * rows), f32)],
        [low, high, head_weight, held[0], teacher_slot[None]],
        [fast] * 5,
        [fast] * 3,
        flops=2 * rows * depth * width,
    )
    keep, send = call(
        with_masks(products_kernel),
        "products",
        [shape((rows, depth), f32), shape((rows, depth), bf16)],
        [logits, teacher, stats, swap(stats, masks[-1]), head_weight],
        [fast] * 5,
        [fast] * 2,
        flops=4 * rows * depth * width,
    )
    def join(value, mask, *after):
        (joined,) = call(
            join_kernel,
            "join_statistics",
            [shape((2 * value.shape[0], 4, 2 * rows), f32)],
            [value, swap(value, mask), *after],
            [fast] * 2 + [far] * len(after),
            [fast],
            light=True,
        )
        return joined

    stats = join(stats[None], masks[0], send)
    stats, send = lax.optimization_barrier((stats, send))
    (share,) = call(
        with_masks(share_kernel),
        "share",
        [shape((chips, 4 * own, columns), bf16)],
        [keep, swap(send, masks[-1])],
        [fast] * 2,
        [far],
        [pltpu.VMEM((chips, 4 * own, columns), bf16), sems(chips)],
    )
    for step, mask in enumerate(masks[1:-1]):
        if step == 0:
            stats, share = lax.optimization_barrier((join(stats, mask, share), share))
        else:
            stats = join(stats, mask)
    other_stats = swap(stats, masks[-1])
    shares = lax.all_to_all(share, ("seq", "row"), split_axis=0, concat_axis=0, tiled=True)
    terms, factors = call(
        with_masks(terms_kernel),
        "terms",
        [shape((rows, 128), f32), shape((chips, 4 * own, 128), f32)],
        [stats, other_stats, valid_tokens[None]],
        [fast] * 3,
        [fast] * 2,
        light=True,
    )
    (grad_head,) = call(
        head_kernel,
        "grad_head",
        [shape(head_weight.shape, bf16)],
        [low, high, logits, teacher, terms],
        [fast] * 5,
        [far],
        [pltpu.VMEM((depth, width), bf16), sems(5)],
        light=True,
    )
    (grad_hidden,) = call(
        finish_kernel,
        "finish",
        [shape((own, depth), bf16)],
        [hidden, gain, shares, factors],
        [fast] * 4,
        [fast],
    )
    return (grad_hidden, grad_head)


def solution(mesh):
    n_seq, n_vocab = mesh.shape["seq"], mesh.shape["vocab"]
    finer = jax.sharding.Mesh(mesh.devices.reshape(n_seq, n_vocab // 2, 2), axes)
    placed = (
        P(axes, None),
        P(),
        P(None, axes),
        P("seq", None, ("row", "core")),
        P(),
        P(),
    )
    return jax.shard_map(
        shards,
        mesh=finer,
        in_specs=placed,
        out_specs=(P(axes, None), P(None, axes)),
        check_vma=False,
    )
```

```python
import math

import jax
import jax.numpy as jnp
from jax import lax
from jax.experimental import pallas as pl
from jax.experimental.pallas import tpu as pltpu
from jax.sharding import PartitionSpec as P

epsilon = 1e-06
axes = ("seq", "row", "core")
fast, far = pltpu.VMEM, pl.ANY
shape = jax.ShapeDtypeStruct
f32, bf16 = jnp.float32, jnp.bfloat16


def call(kernel, name, out_shape, inputs, spaces, out_spaces, scratch=(), flops=0, light=False):
    def size(leaf):
        return leaf.size * leaf.dtype.itemsize

    near = [x for x, s in zip(inputs, spaces) if s == fast]
    near += [x for x, s in zip(out_shape, out_spaces) if s == fast]
    held = sum(x.dtype.itemsize * math.prod(x.shape) for x in scratch if x.memory_space == fast)
    return pl.pallas_call(
        kernel,
        out_shape=list(out_shape),
        in_specs=[pl.BlockSpec(memory_space=s) for s in spaces],
        out_specs=[pl.BlockSpec(memory_space=s) for s in out_spaces],
        scratch_shapes=list(scratch),
        compiler_params=pltpu.CompilerParams(
            vmem_limit_bytes=2 * sum(map(size, near)) + held + (8 << 20)
        ),
        cost_estimate=pl.CostEstimate(
            flops=flops,
            bytes_accessed=0 if light else sum(map(size, list(inputs) + list(out_shape))),
            transcendentals=0,
        ),
        name=name,
    )(*inputs)


def split_evenly(total, unit):
    parts = max(p for p in (1, 2, 4, 5) if total % (p * unit) == 0)
    return parts, total // parts


def my_index():
    return (lax.axis_index("seq") * lax.axis_size("row") + lax.axis_index("row")) * 2 + lax.axis_index("core")


def partner(me, masks, place):
    for bit, mask in enumerate(masks):
        if place >> bit & 1:
            me = me ^ mask
    return me


def place_match(rows, masks, own, me):
    place = lax.broadcasted_iota(jnp.int32, (rows, rows), 0)
    block, inner = lax.div(place, own), lax.rem(place, own)
    device = jnp.full((rows, rows), me, jnp.int32)
    for bit, mask in enumerate(masks):
        device = device ^ (((block >> bit) & 1) * mask)
    return device * own + inner == lax.broadcasted_iota(jnp.int32, (rows, rows), 1)


def to_column(match, row_values):
    return jnp.sum(jnp.where(match, row_values, 0.0), axis=1, keepdims=True)


def to_row(match, column):
    return jnp.sum(jnp.where(match, column, 0.0), axis=0, keepdims=True)


def merge(first, second):
    top = jnp.maximum(first[0:1], second[0:1])
    near, far_off = jnp.exp(first[0:1] - top), jnp.exp(second[0:1] - top)
    return top, first[1:2] * near + second[1:2] * far_off, first[2:3] * near + second[2:3] * far_off


def first_kernel(out_ref):
    out_ref[...] = jnp.zeros_like(out_ref)


def features_kernel(hidden_ref, gain_ref, first_ref, features_ref):
    widened = hidden_ref[...].astype(f32)
    inv_rms = lax.rsqrt(jnp.mean(widened * widened, axis=1, keepdims=True) + epsilon)
    features_ref[...] = (widened * inv_rms * gain_ref[...]).astype(bf16)


def teacher_kernel(blocks_ref, keep_ref, send_ref):
    my_seq = lax.axis_index("seq")
    for k in range(keep_ref.shape[0]):
        keep_ref[k] = blocks_ref[my_seq ^ (2 * k)]
        send_ref[k] = blocks_ref[my_seq ^ (2 * k + 1)]


def join_kernel(first_ref, second_ref, *rest):
    out_ref = rest[-1]
    length = first_ref.shape[0]
    out_ref[:length] = first_ref[...]
    out_ref[length:] = second_ref[...]


def logits_kernel(masks, own, cap, low_ref, high_ref, weight_ref, table_ref, slots_ref, logits_ref, teacher_ref, stats_ref):
    my_seq = lax.axis_index("seq")
    rows = logits_ref.shape[0]
    parts, size = split_evenly(weight_ref.shape[0], 256)
    match = place_match(rows, masks, own, my_index())
    slots = to_column(match, slots_ref[...].astype(f32)).astype(jnp.int32)
    place = (lax.div(slots, cap) ^ my_seq) * cap + lax.rem(slots, cap)
    pick = (place == lax.broadcasted_iota(jnp.int32, (rows, table_ref.shape[0]), 1)).astype(bf16)
    teacher = jnp.dot(pick, table_ref[...], preferred_element_type=f32)
    teacher_ref[...] = teacher.astype(bf16)
    teacher_top = jnp.max(teacher, axis=1, keepdims=True)
    teacher_total = jnp.sum(jnp.exp(teacher - teacher_top), axis=1, keepdims=True)
    logits = jnp.zeros(logits_ref.shape, f32)
    for p in range(parts):
        block = slice(p * size, (p + 1) * size)
        features = jnp.concatenate([low_ref[:, block], high_ref[:, block]], axis=0)
        logits += jnp.dot(features, weight_ref[block, :], preferred_element_type=f32)
    logits_ref[...] = logits
    student_top = jnp.max(logits, axis=1, keepdims=True)
    shifted = jnp.exp(logits - student_top)
    student_total = jnp.sum(shifted, axis=1, keepdims=True)
    cross_sum = jnp.sum(shifted * (logits - teacher), axis=1, keepdims=True)
    nothing = jnp.zeros((1, rows), f32)
    pairs = [
        (to_row(match, student_top), to_row(match, teacher_top)),
        (to_row(match, student_total), to_row(match, teacher_total)),
        (to_row(match, cross_sum), nothing),
        (nothing, nothing),
    ]
    stats_ref[...] = jnp.concatenate([jnp.concatenate(p, axis=1) for p in pairs], axis=0)


def products_kernel(masks, own, logits_ref, teacher_ref, mine_ref, theirs_ref, weight_ref, keep_ref, send_ref):
    parts, size = split_evenly(weight_ref.shape[0], 256)
    logits = logits_ref[...]
    rows = logits.shape[0]
    half = rows // 2
    match = place_match(rows, masks, own, my_index())
    top, total, cross = merge(mine_ref[...], theirs_ref[...])
    center = to_column(match, cross[:, :rows] / total[:, :rows])
    shifted = jnp.exp(logits - to_column(match, top[:, :rows]))
    gaps = shifted * (logits - teacher_ref[...].astype(f32) - center)
    pieces = []
    for at in range(0, rows, own):
        pieces += [gaps[at : at + own], shifted[at : at + own]]
    left = jnp.concatenate(pieces, axis=0).astype(bf16)
    for p in range(parts):
        block = slice(p * size, (p + 1) * size)
        product = lax.dot_general(
            left, weight_ref[block, :], (((1,), (1,)), ((), ())), preferred_element_type=f32
        )
        keep_ref[:, block] = product[: 2 * half]
        send_ref[:, block] = product[2 * half :].astype(bf16)


def share_kernel(masks, own, keep_ref, arrived_ref, share_ref, held, sems):
    me = my_index()
    chips, length, columns = share_ref.shape
    length //= 4
    group = 16 // length
    copies = []
    for first in range(0, chips, group):
        rows = slice(first * length, (first + group) * length)
        total = keep_ref[rows, :] + arrived_ref[rows, :].astype(f32)
        for p in range(first, first + group):
            mine = total[(p - first) * length : (p - first + 1) * length]
            quarters = [mine[:, at : at + columns] for at in range(0, 4 * columns, columns)]
            held[p] = jnp.concatenate(quarters, axis=0).astype(bf16)
            copies.append(
                pltpu.make_async_copy(held.at[p], share_ref.at[partner(me, masks, p) >> 1], sems.at[p])
            )
            copies[-1].start()
    for copy in copies:
        copy.wait()


def terms_kernel(masks, own, mine_ref, theirs_ref, valid_ref, terms_ref, factors_ref):
    me = my_index()
    rows = valid_ref.shape[1]
    chips = factors_ref.shape[0]
    mine, theirs = mine_ref[...], theirs_ref[...]
    tops = jnp.maximum(mine[:, 0, :], theirs[:, 0, :])
    near, other = jnp.exp(mine[:, 0, :] - tops), jnp.exp(theirs[:, 0, :] - tops)
    totals = mine[:, 1, :] * near + theirs[:, 1, :] * other
    crosses = mine[:, 2, :] * near + theirs[:, 2, :] * other
    top = jnp.max(tops, axis=0, keepdims=True)
    scale = jnp.exp(tops - top)
    total = jnp.sum(totals * scale, axis=0, keepdims=True)
    cross = jnp.sum(crosses * scale, axis=0, keepdims=True)[:, :rows]
    lse = top + jnp.log(total)
    student_lse, teacher_lse = lse[:, :rows], lse[:, rows:]
    divergence = cross / total[:, :rows] - student_lse + teacher_lse
    row_weight = valid_ref[...].astype(f32)
    match = place_match(rows, masks, own, me)
    lane = lax.broadcasted_iota(jnp.int32, (rows, 128), 1)
    terms = to_column(match, row_weight)
    for at, values in enumerate((student_lse, teacher_lse, divergence)):
        terms = jnp.where(lane == at, to_column(match, values), terms)
    terms_ref[...] = terms
    scale = row_weight * jnp.exp(tops[:, :rows] - student_lse)
    offset = scale * (crosses[:, :rows] / totals[:, :rows] + (teacher_lse - student_lse - divergence))
    pick = lax.rem(lax.broadcasted_iota(jnp.int32, (8 * own, rows), 0), 2 * own)
    mine = lax.broadcasted_iota(jnp.int32, (8 * own, rows), 1) == me * own + lax.rem(pick, own)
    for p in range(chips):
        both = jnp.where(pick < own, scale[p : p + 1], offset[p : p + 1])
        column = jnp.sum(jnp.where(mine, both, 0.0), axis=1, keepdims=True)
        factors_ref[partner(me, masks, p) >> 1] = jnp.broadcast_to(column, factors_ref.shape[1:])


def head_kernel(low_ref, high_ref, logits_ref, teacher_ref, terms_ref, out_ref, held, sems):
    parts, size = split_evenly(out_ref.shape[0], 256)
    student_lse, teacher_lse = terms_ref[:, 0:1], terms_ref[:, 1:2]
    log_prob = logits_ref[...] - student_lse
    log_gap = log_prob - (teacher_ref[...].astype(f32) - teacher_lse)
    grad = (terms_ref[:, 3:4] * jnp.exp(log_prob) * (log_gap - terms_ref[:, 2:3])).astype(bf16)
    copies = []
    for p in range(parts):
        block = slice(p * size, (p + 1) * size)
        features = jnp.concatenate([low_ref[:, block], high_ref[:, block]], axis=0)
        held[block, :] = lax.dot_general(
            features, grad, (((0,), (0,)), ((), ())), preferred_element_type=f32
        ).astype(bf16)
        rows = pl.ds(p * size, size)
        copies.append(pltpu.make_async_copy(held.at[rows], out_ref.at[rows], sems.at[p]))
        copies[-1].start()
    for copy in copies:
        copy.wait()


def finish_kernel(hidden_ref, gain_ref, shares_ref, factors_ref, out_ref):
    own = hidden_ref.shape[0]
    widened = hidden_ref[...].astype(f32)
    inv_rms = lax.rsqrt(jnp.mean(widened * widened, axis=1, keepdims=True) + epsilon)
    normed = widened * inv_rms
    both = shares_ref[0].astype(f32) * factors_ref[0][:, 0:1]
    for p in range(1, shares_ref.shape[0]):
        both += shares_ref[p].astype(f32) * factors_ref[p][:, 0:1]
    sums = [both[at : at + own] + both[at + own : at + 2 * own] for at in range(0, 8 * own, 2 * own)]
    norm_grad = jnp.concatenate(sums, axis=1) * gain_ref[...]
    mean = jnp.mean(norm_grad * normed, axis=1, keepdims=True)
    out_ref[...] = (inv_rms * (norm_grad - normed * mean)).astype(bf16)


def shards(hidden, norm_gain, head_weight, teacher_logits, teacher_slot, valid_tokens):
    n_seq, n_row = lax.axis_size("seq"), lax.axis_size("row")
    chips = n_seq * n_row
    count = chips * 2
    own, depth = hidden.shape
    width = head_weight.shape[1]
    rows = own * count
    cap = teacher_logits.shape[0]
    columns = depth // 4
    gain = norm_gain[None]
    masks = [1 << b for b in reversed(range(count.bit_length() - 1))]
    seq_masks = [m for m in reversed(masks) if m >= n_row * 2]

    def swap(value, mask):
        return lax.ppermute(value, axes, [(i, i ^ mask) for i in range(count)])

    def sems(number):
        return pltpu.SemaphoreType.DMA((number,))

    (first,) = call(first_kernel, "first", [shape((8, 128), f32)], [], [], [fast], flops=10**10)
    (gathered,) = call(
        features_kernel,
        "features",
        [shape((own, depth), bf16)],
        [hidden, gain, first],
        [fast] * 3,
        [fast],
    )
    half_blocks = shape((n_seq // 2, cap, width), bf16)
    keep, send = call(
        teacher_kernel,
        "teacher_blocks",
        [half_blocks] * 2,
        [teacher_logits.transpose(1, 0, 2)],
        [fast],
        [fast] * 2,
        flops=10**10,
    )
    held = jnp.concatenate([keep, swap(send, seq_masks[0])], axis=1)
    behind = len(masks) - len(seq_masks)
    for step, mask in enumerate(masks[:-1]):
        arrived = swap(gathered, mask)
        bit = step - behind + 1
        if 1 <= bit < len(seq_masks):
            pairs = held.reshape((held.shape[0] // 2, 2) + held.shape[1:])
            held = jnp.concatenate([pairs[:, 0], swap(pairs[:, 1], seq_masks[bit])], axis=1)
        if step < len(masks) - 2:
            gathered = jnp.concatenate([gathered, arrived], axis=0)
    (gathered,) = call(
        join_kernel, "join", [shape((rows // 2, depth), bf16)], [gathered, arrived], [fast] * 2, [fast]
    )
    low, held = lax.optimization_barrier((gathered, held))
    high = swap(low, masks[-1])

    def with_masks(kernel, *more):
        return lambda *refs: kernel(masks, own, *more, *refs)

    logits, teacher, stats = call(
        with_masks(logits_kernel, cap),
        "logits",
        [shape((rows, width), f32), shape((rows, width), bf16), shape((4, 2 * rows), f32)],
        [low, high, head_weight, held[0], teacher_slot[None]],
        [fast] * 5,
        [fast] * 3,
        flops=2 * rows * depth * width,
    )
    keep, send = call(
        with_masks(products_kernel),
        "products",
        [shape((rows, depth), f32), shape((rows, depth), bf16)],
        [logits, teacher, stats, swap(stats, masks[-1]), head_weight],
        [fast] * 5,
        [fast] * 2,
        flops=4 * rows * depth * width,
    )
    def join(value, mask, *after):
        (joined,) = call(
            join_kernel,
            "join_statistics",
            [shape((2 * value.shape[0], 4, 2 * rows), f32)],
            [value, swap(value, mask), *after],
            [fast] * 2 + [far] * len(after),
            [fast],
            light=True,
        )
        return joined

    stats = join(stats[None], masks[0], send)
    stats, send = lax.optimization_barrier((stats, send))
    (share,) = call(
        with_masks(share_kernel),
        "share",
        [shape((chips, 8 * own, columns), bf16)],
        [keep, swap(send, masks[-1])],
        [fast] * 2,
        [far],
        [pltpu.VMEM((chips, 8 * own, columns), bf16), sems(chips)],
    )
    for step, mask in enumerate(masks[1:-1]):
        if step == 0:
            stats, share = lax.optimization_barrier((join(stats, mask, share), share))
        else:
            stats = join(stats, mask)
    other_stats = swap(stats, masks[-1])
    shares = lax.all_to_all(share, ("seq", "row"), split_axis=0, concat_axis=0, tiled=True)
    terms, factors = call(
        with_masks(terms_kernel),
        "terms",
        [shape((rows, 128), f32), shape((chips, 8 * own, 128), f32)],
        [stats, other_stats, valid_tokens[None]],
        [fast] * 3,
        [fast] * 2,
        light=True,
    )
    (grad_head,) = call(
        head_kernel,
        "grad_head",
        [shape(head_weight.shape, bf16)],
        [low, high, logits, teacher, terms],
        [fast] * 5,
        [far],
        [pltpu.VMEM((depth, width), bf16), sems(5)],
        light=True,
    )
    (grad_hidden,) = call(
        finish_kernel,
        "finish",
        [shape((own, depth), bf16)],
        [hidden, gain, shares, factors],
        [fast] * 4,
        [fast],
    )
    return (grad_hidden, grad_head)


def solution(mesh):
    n_seq, n_vocab = mesh.shape["seq"], mesh.shape["vocab"]
    finer = jax.sharding.Mesh(mesh.devices.reshape(n_seq, n_vocab // 2, 2), axes)
    placed = (
        P(axes, None),
        P(),
        P(None, axes),
        P("seq", None, ("row", "core")),
        P(),
        P(),
    )
    return jax.shard_map(
        shards,
        mesh=finer,
        in_specs=placed,
        out_specs=(P(axes, None), P(None, axes)),
        check_vma=False,
    )
```

```python
import math

import jax
import jax.numpy as jnp
from jax import lax
from jax.experimental import pallas as pl
from jax.experimental.pallas import tpu as pltpu
from jax.sharding import PartitionSpec as P

epsilon = 1e-06
axes = ("seq", "row", "core")
fast, far = pltpu.VMEM, pl.ANY
shape = jax.ShapeDtypeStruct
f32, bf16 = jnp.float32, jnp.bfloat16


def call(kernel, name, out_shape, inputs, spaces, out_spaces, scratch=(), flops=0, light=False):
    def size(leaf):
        return leaf.size * leaf.dtype.itemsize

    near = [x for x, s in zip(inputs, spaces) if s == fast]
    near += [x for x, s in zip(out_shape, out_spaces) if s == fast]
    held = sum(x.dtype.itemsize * math.prod(x.shape) for x in scratch if x.memory_space == fast)
    return pl.pallas_call(
        kernel,
        out_shape=list(out_shape),
        in_specs=[pl.BlockSpec(memory_space=s) for s in spaces],
        out_specs=[pl.BlockSpec(memory_space=s) for s in out_spaces],
        scratch_shapes=list(scratch),
        compiler_params=pltpu.CompilerParams(
            vmem_limit_bytes=2 * sum(map(size, near)) + held + (8 << 20)
        ),
        cost_estimate=pl.CostEstimate(
            flops=flops,
            bytes_accessed=0 if light else sum(map(size, list(inputs) + list(out_shape))),
            transcendentals=0,
        ),
        name=name,
    )(*inputs)


def split_evenly(total, unit):
    parts = max(p for p in (1, 2, 4, 5) if total % (p * unit) == 0)
    return parts, total // parts


def my_index():
    return (lax.axis_index("seq") * lax.axis_size("row") + lax.axis_index("row")) * 2 + lax.axis_index("core")


def partner(me, masks, place):
    for bit, mask in enumerate(masks):
        if place >> bit & 1:
            me = me ^ mask
    return me


def place_match(rows, masks, own, me):
    place = lax.broadcasted_iota(jnp.int32, (rows, rows), 0)
    block, inner = lax.div(place, own), lax.rem(place, own)
    device = jnp.full((rows, rows), me, jnp.int32)
    for bit, mask in enumerate(masks):
        device = device ^ (((block >> bit) & 1) * mask)
    return device * own + inner == lax.broadcasted_iota(jnp.int32, (rows, rows), 1)


def to_column(match, row_values):
    return jnp.sum(jnp.where(match, row_values, 0.0), axis=1, keepdims=True)


def to_row(match, column):
    return jnp.sum(jnp.where(match, column, 0.0), axis=0, keepdims=True)


def merge(first, second):
    top = jnp.maximum(first[0:1], second[0:1])
    near, far_off = jnp.exp(first[0:1] - top), jnp.exp(second[0:1] - top)
    return top, first[1:2] * near + second[1:2] * far_off, first[2:3] * near + second[2:3] * far_off


def first_kernel(out_ref):
    out_ref[...] = jnp.zeros_like(out_ref)


def features_kernel(hidden_ref, gain_ref, first_ref, features_ref):
    widened = hidden_ref[...].astype(f32)
    inv_rms = lax.rsqrt(jnp.mean(widened * widened, axis=1, keepdims=True) + epsilon)
    features_ref[...] = (widened * inv_rms * gain_ref[...]).astype(bf16)


def teacher_kernel(blocks_ref, keep_ref, send_ref):
    my_seq = lax.axis_index("seq")
    for k in range(keep_ref.shape[0]):
        keep_ref[k] = blocks_ref[my_seq ^ (2 * k)]
        send_ref[k] = blocks_ref[my_seq ^ (2 * k + 1)]


def join_kernel(first_ref, second_ref, *rest):
    out_ref = rest[-1]
    length = first_ref.shape[0]
    out_ref[:length] = first_ref[...]
    out_ref[length:] = second_ref[...]


def logits_kernel(masks, own, cap, low_ref, high_ref, weight_ref, table_ref, slots_ref, logits_ref, teacher_ref, stats_ref):
    my_seq = lax.axis_index("seq")
    rows = logits_ref.shape[0]
    parts, size = split_evenly(weight_ref.shape[0], 256)
    match = place_match(rows, masks, own, my_index())
    slots = to_column(match, slots_ref[...].astype(f32)).astype(jnp.int32)
    place = (lax.div(slots, cap) ^ my_seq) * cap + lax.rem(slots, cap)
    pick = (place == lax.broadcasted_iota(jnp.int32, (rows, table_ref.shape[0]), 1)).astype(bf16)
    teacher = jnp.dot(pick, table_ref[...], preferred_element_type=f32)
    teacher_ref[...] = teacher.astype(bf16)
    teacher_top = jnp.max(teacher, axis=1, keepdims=True)
    teacher_total = jnp.sum(jnp.exp(teacher - teacher_top), axis=1, keepdims=True)
    logits = jnp.zeros(logits_ref.shape, f32)
    for p in range(parts):
        block = slice(p * size, (p + 1) * size)
        features = jnp.concatenate([low_ref[:, block], high_ref[:, block]], axis=0)
        logits += jnp.dot(features, weight_ref[block, :], preferred_element_type=f32)
    logits_ref[...] = logits
    student_top = jnp.max(logits, axis=1, keepdims=True)
    shifted = jnp.exp(logits - student_top)
    student_total = jnp.sum(shifted, axis=1, keepdims=True)
    cross_sum = jnp.sum(shifted * (logits - teacher), axis=1, keepdims=True)
    nothing = jnp.zeros((1, rows), f32)
    pairs = [
        (to_row(match, student_top), to_row(match, teacher_top)),
        (to_row(match, student_total), to_row(match, teacher_total)),
        (to_row(match, cross_sum), nothing),
        (nothing, nothing),
    ]
    stats_ref[...] = jnp.concatenate([jnp.concatenate(p, axis=1) for p in pairs], axis=0)


def products_kernel(masks, own, logits_ref, teacher_ref, mine_ref, theirs_ref, weight_ref, keep_ref, send_ref):
    parts, size = split_evenly(weight_ref.shape[0], 256)
    logits = logits_ref[...]
    rows = logits.shape[0]
    half = rows // 2
    match = place_match(rows, masks, own, my_index())
    top, total, cross = merge(mine_ref[...], theirs_ref[...])
    center = to_column(match, cross[:, :rows] / total[:, :rows])
    shifted = jnp.exp(logits - to_column(match, top[:, :rows]))
    gaps = shifted * (logits - teacher_ref[...].astype(f32) - center)
    pieces = []
    for at in range(0, rows, own):
        pieces += [gaps[at : at + own], shifted[at : at + own]]
    left = jnp.concatenate(pieces, axis=0).astype(bf16)
    for p in range(parts):
        block = slice(p * size, (p + 1) * size)
        product = lax.dot_general(
            left, weight_ref[block, :], (((1,), (1,)), ((), ())), preferred_element_type=f32
        )
        keep_ref[:, block] = product[: 2 * half]
        send_ref[:, block] = product[2 * half :].astype(bf16)


def share_kernel(masks, own, keep_ref, arrived_ref, share_ref, held, sems):
    me = my_index()
    chips, length, columns = share_ref.shape
    length //= 4
    group = 16 // length
    copies = []
    for first in range(0, chips, group):
        rows = slice(first * length, (first + group) * length)
        total = keep_ref[rows, :] + arrived_ref[rows, :].astype(f32)
        for p in range(first, first + group):
            mine = total[(p - first) * length : (p - first + 1) * length]
            quarters = [mine[:, at : at + columns] for at in range(0, 4 * columns, columns)]
            held[p] = jnp.concatenate(quarters, axis=0).astype(bf16)
            copies.append(
                pltpu.make_async_copy(held.at[p], share_ref.at[partner(me, masks, p) >> 1], sems.at[p])
            )
            copies[-1].start()
    for copy in copies:
        copy.wait()


def terms_kernel(masks, own, mine_ref, theirs_ref, valid_ref, terms_ref, factors_ref, held):
    me = my_index()
    rows = valid_ref.shape[1]
    chips = held.shape[0]
    mine, theirs = mine_ref[...], theirs_ref[...]
    tops = jnp.maximum(mine[:, 0, :], theirs[:, 0, :])
    near, other = jnp.exp(mine[:, 0, :] - tops), jnp.exp(theirs[:, 0, :] - tops)
    totals = mine[:, 1, :] * near + theirs[:, 1, :] * other
    crosses = mine[:, 2, :] * near + theirs[:, 2, :] * other
    top = jnp.max(tops, axis=0, keepdims=True)
    scale = jnp.exp(tops - top)
    total = jnp.sum(totals * scale, axis=0, keepdims=True)
    cross = jnp.sum(crosses * scale, axis=0, keepdims=True)[:, :rows]
    lse = top + jnp.log(total)
    student_lse, teacher_lse = lse[:, :rows], lse[:, rows:]
    divergence = cross / total[:, :rows] - student_lse + teacher_lse
    row_weight = valid_ref[...].astype(f32)
    match = place_match(rows, masks, own, me)
    lane = lax.broadcasted_iota(jnp.int32, (rows, 128), 1)
    terms = to_column(match, row_weight)
    for at, values in enumerate((student_lse, teacher_lse, divergence)):
        terms = jnp.where(lane == at, to_column(match, values), terms)
    terms_ref[...] = terms
    scale = row_weight * jnp.exp(tops[:, :rows] - student_lse)
    offset = scale * (crosses[:, :rows] / totals[:, :rows] + (teacher_lse - student_lse - divergence))
    pick = lax.rem(lax.broadcasted_iota(jnp.int32, (8 * own, rows), 0), 2 * own)
    mine = lax.broadcasted_iota(jnp.int32, (8 * own, rows), 1) == me * own + lax.rem(pick, own)
    for p in range(chips):
        both = jnp.where(pick < own, scale[p : p + 1], offset[p : p + 1])
        column = jnp.sum(jnp.where(mine, both, 0.0), axis=1, keepdims=True)
        held[partner(me, masks, p) >> 1] = jnp.broadcast_to(column, held.shape[1:])
    across = held[...].reshape(chips * 8 * own, 128).T[: 4 * own]
    target = lax.broadcasted_iota(jnp.int32, across.shape, 0)
    source = lax.rem(lax.broadcasted_iota(jnp.int32, across.shape, 1), 8 * own)
    same = lax.div(target, own) == lax.div(source, 2 * own)
    same = jnp.logical_and(same, lax.rem(target, own) == lax.rem(source, own))
    rest = jnp.where(same, across, 0.0)
    split = []
    for _ in range(3):
        split.append(rest.astype(bf16).astype(f32))
        rest = rest - split[-1]
    factors_ref[...] = jnp.concatenate(split, axis=0).astype(bf16)


def head_kernel(low_ref, high_ref, logits_ref, teacher_ref, terms_ref, out_ref, held, sems):
    parts, size = split_evenly(out_ref.shape[0], 256)
    student_lse, teacher_lse = terms_ref[:, 0:1], terms_ref[:, 1:2]
    log_prob = logits_ref[...] - student_lse
    log_gap = log_prob - (teacher_ref[...].astype(f32) - teacher_lse)
    grad = (terms_ref[:, 3:4] * jnp.exp(log_prob) * (log_gap - terms_ref[:, 2:3])).astype(bf16)
    copies = []
    for p in range(parts):
        block = slice(p * size, (p + 1) * size)
        features = jnp.concatenate([low_ref[:, block], high_ref[:, block]], axis=0)
        held[block, :] = lax.dot_general(
            features, grad, (((0,), (0,)), ((), ())), preferred_element_type=f32
        ).astype(bf16)
        rows = pl.ds(p * size, size)
        copies.append(pltpu.make_async_copy(held.at[rows], out_ref.at[rows], sems.at[p]))
        copies[-1].start()
    for copy in copies:
        copy.wait()


def finish_kernel(hidden_ref, gain_ref, shares_ref, factors_ref, out_ref):
    own = hidden_ref.shape[0]
    widened = hidden_ref[...].astype(f32)
    inv_rms = lax.rsqrt(jnp.mean(widened * widened, axis=1, keepdims=True) + epsilon)
    normed = widened * inv_rms
    chips, length, columns = shares_ref.shape
    shares = shares_ref[...].reshape(chips * length, columns)
    parts = jnp.dot(factors_ref[...], shares, preferred_element_type=f32)
    total = parts[: 4 * own] + parts[4 * own : 8 * own] + parts[8 * own :]
    norm_grad = jnp.concatenate([total[at : at + own] for at in range(0, 4 * own, own)], axis=1) * gain_ref[...]
    mean = jnp.mean(norm_grad * normed, axis=1, keepdims=True)
    out_ref[...] = (inv_rms * (norm_grad - normed * mean)).astype(bf16)


def shards(hidden, norm_gain, head_weight, teacher_logits, teacher_slot, valid_tokens):
    n_seq, n_row = lax.axis_size("seq"), lax.axis_size("row")
    chips = n_seq * n_row
    count = chips * 2
    own, depth = hidden.shape
    width = head_weight.shape[1]
    rows = own * count
    cap = teacher_logits.shape[0]
    columns = depth // 4
    gain = norm_gain[None]
    masks = [1 << b for b in reversed(range(count.bit_length() - 1))]
    seq_masks = [m for m in reversed(masks) if m >= n_row * 2]

    def swap(value, mask):
        return lax.ppermute(value, axes, [(i, i ^ mask) for i in range(count)])

    def sems(number):
        return pltpu.SemaphoreType.DMA((number,))

    (first,) = call(first_kernel, "first", [shape((8, 128), f32)], [], [], [fast], flops=10**10)
    (gathered,) = call(
        features_kernel,
        "features",
        [shape((own, depth), bf16)],
        [hidden, gain, first],
        [fast] * 3,
        [fast],
    )
    half_blocks = shape((n_seq // 2, cap, width), bf16)
    keep, send = call(
        teacher_kernel,
        "teacher_blocks",
        [half_blocks] * 2,
        [teacher_logits.transpose(1, 0, 2)],
        [fast],
        [fast] * 2,
        flops=10**10,
    )
    held = jnp.concatenate([keep, swap(send, seq_masks[0])], axis=1)
    behind = len(masks) - len(seq_masks)
    for step, mask in enumerate(masks[:-1]):
        arrived = swap(gathered, mask)
        bit = step - behind + 1
        if 1 <= bit < len(seq_masks):
            pairs = held.reshape((held.shape[0] // 2, 2) + held.shape[1:])
            held = jnp.concatenate([pairs[:, 0], swap(pairs[:, 1], seq_masks[bit])], axis=1)
        if step < len(masks) - 2:
            gathered = jnp.concatenate([gathered, arrived], axis=0)
    (gathered,) = call(
        join_kernel, "join", [shape((rows // 2, depth), bf16)], [gathered, arrived], [fast] * 2, [fast]
    )
    low, held = lax.optimization_barrier((gathered, held))
    high = swap(low, masks[-1])

    def with_masks(kernel, *more):
        return lambda *refs: kernel(masks, own, *more, *refs)

    logits, teacher, stats = call(
        with_masks(logits_kernel, cap),
        "logits",
        [shape((rows, width), f32), shape((rows, width), bf16), shape((4, 2 * rows), f32)],
        [low, high, head_weight, held[0], teacher_slot[None]],
        [fast] * 5,
        [fast] * 3,
        flops=2 * rows * depth * width,
    )
    keep, send = call(
        with_masks(products_kernel),
        "products",
        [shape((rows, depth), f32), shape((rows, depth), bf16)],
        [logits, teacher, stats, swap(stats, masks[-1]), head_weight],
        [fast] * 5,
        [fast] * 2,
        flops=4 * rows * depth * width,
    )
    def join(value, mask, *after):
        (joined,) = call(
            join_kernel,
            "join_statistics",
            [shape((2 * value.shape[0], 4, 2 * rows), f32)],
            [value, swap(value, mask), *after],
            [fast] * 2 + [far] * len(after),
            [fast],
            light=True,
        )
        return joined

    stats = join(stats[None], masks[0], send)
    stats, send = lax.optimization_barrier((stats, send))
    (share,) = call(
        with_masks(share_kernel),
        "share",
        [shape((chips, 8 * own, columns), bf16)],
        [keep, swap(send, masks[-1])],
        [fast] * 2,
        [far],
        [pltpu.VMEM((chips, 8 * own, columns), bf16), sems(chips)],
    )
    for step, mask in enumerate(masks[1:-1]):
        if step == 0:
            stats, share = lax.optimization_barrier((join(stats, mask, share), share))
        else:
            stats = join(stats, mask)
    other_stats = swap(stats, masks[-1])
    shares = lax.all_to_all(share, ("seq", "row"), split_axis=0, concat_axis=0, tiled=True)
    terms, factors = call(
        with_masks(terms_kernel),
        "terms",
        [shape((rows, 128), f32), shape((12 * own, chips * 8 * own), bf16)],
        [stats, other_stats, valid_tokens[None]],
        [fast] * 3,
        [fast] * 2,
        [pltpu.VMEM((chips, 8 * own, 128), f32)],
        light=True,
    )
    (grad_head,) = call(
        head_kernel,
        "grad_head",
        [shape(head_weight.shape, bf16)],
        [low, high, logits, teacher, terms],
        [fast] * 5,
        [far],
        [pltpu.VMEM((depth, width), bf16), sems(5)],
        light=True,
    )
    (grad_hidden,) = call(
        finish_kernel,
        "finish",
        [shape((own, depth), bf16)],
        [hidden, gain, shares, factors],
        [fast] * 4,
        [fast],
    )
    return (grad_hidden, grad_head)


def solution(mesh):
    n_seq, n_vocab = mesh.shape["seq"], mesh.shape["vocab"]
    finer = jax.sharding.Mesh(mesh.devices.reshape(n_seq, n_vocab // 2, 2), axes)
    placed = (
        P(axes, None),
        P(),
        P(None, axes),
        P("seq", None, ("row", "core")),
        P(),
        P(),
    )
    return jax.shard_map(
        shards,
        mesh=finer,
        in_specs=placed,
        out_specs=(P(axes, None), P(None, axes)),
        check_vma=False,
    )
```

```python
import math

import jax
import jax.numpy as jnp
from jax import lax
from jax.experimental import pallas as pl
from jax.experimental.pallas import tpu as pltpu
from jax.sharding import PartitionSpec as P

epsilon = 1e-06
axes = ("seq", "row", "core")
fast, far = pltpu.VMEM, pl.ANY
shape = jax.ShapeDtypeStruct
f32, bf16 = jnp.float32, jnp.bfloat16


def call(kernel, name, out_shape, inputs, spaces, out_spaces, scratch=(), flops=0, light=False):
    def size(leaf):
        return leaf.size * leaf.dtype.itemsize

    near = [x for x, s in zip(inputs, spaces) if s == fast]
    near += [x for x, s in zip(out_shape, out_spaces) if s == fast]
    held = sum(x.dtype.itemsize * math.prod(x.shape) for x in scratch if x.memory_space == fast)
    return pl.pallas_call(
        kernel,
        out_shape=list(out_shape),
        in_specs=[pl.BlockSpec(memory_space=s) for s in spaces],
        out_specs=[pl.BlockSpec(memory_space=s) for s in out_spaces],
        scratch_shapes=list(scratch),
        compiler_params=pltpu.CompilerParams(
            vmem_limit_bytes=2 * sum(map(size, near)) + held + (8 << 20)
        ),
        cost_estimate=pl.CostEstimate(
            flops=flops,
            bytes_accessed=0 if light else sum(map(size, list(inputs) + list(out_shape))),
            transcendentals=0,
        ),
        name=name,
    )(*inputs)


def split_evenly(total, unit):
    parts = max(p for p in (1, 2, 4, 5) if total % (p * unit) == 0)
    return parts, total // parts


def my_index():
    return (lax.axis_index("seq") * lax.axis_size("row") + lax.axis_index("row")) * 2 + lax.axis_index("core")


def partner(me, masks, place):
    for bit, mask in enumerate(masks):
        if place >> bit & 1:
            me = me ^ mask
    return me


def near_first(masks):
    return [masks[1], masks[0], *masks[2:]] if len(masks) > 2 else masks


def place_match(rows, masks, own, me):
    place = lax.broadcasted_iota(jnp.int32, (rows, rows), 0)
    block, inner = lax.div(place, own), lax.rem(place, own)
    device = jnp.full((rows, rows), me, jnp.int32)
    for bit, mask in enumerate(masks):
        device = device ^ (((block >> bit) & 1) * mask)
    return device * own + inner == lax.broadcasted_iota(jnp.int32, (rows, rows), 1)


def to_column(match, row_values):
    return jnp.sum(jnp.where(match, row_values, 0.0), axis=1, keepdims=True)


def to_row(match, column):
    return jnp.sum(jnp.where(match, column, 0.0), axis=0, keepdims=True)


def merge(first, second):
    top = jnp.maximum(first[0:1], second[0:1])
    near, far_off = jnp.exp(first[0:1] - top), jnp.exp(second[0:1] - top)
    return top, first[1:2] * near + second[1:2] * far_off, first[2:3] * near + second[2:3] * far_off


def first_kernel(out_ref):
    out_ref[...] = jnp.zeros_like(out_ref)


def features_kernel(hidden_ref, gain_ref, first_ref, features_ref):
    widened = hidden_ref[...].astype(f32)
    inv_rms = lax.rsqrt(jnp.mean(widened * widened, axis=1, keepdims=True) + epsilon)
    features_ref[...] = (widened * inv_rms * gain_ref[...]).astype(bf16)


def teacher_kernel(blocks_ref, keep_ref, send_ref):
    my_seq = lax.axis_index("seq")
    for k in range(keep_ref.shape[0]):
        keep_ref[k] = blocks_ref[my_seq ^ (2 * k)]
        send_ref[k] = blocks_ref[my_seq ^ (2 * k + 1)]


def join_kernel(first_ref, second_ref, *rest):
    out_ref = rest[-1]
    length = first_ref.shape[0]
    out_ref[:length] = first_ref[...]
    out_ref[length:] = second_ref[...]


def logits_kernel(masks, own, cap, low_ref, high_ref, weight_ref, table_ref, slots_ref, logits_ref, teacher_ref, stats_ref):
    my_seq = lax.axis_index("seq")
    rows = logits_ref.shape[0]
    parts, size = split_evenly(weight_ref.shape[0], 256)
    match = place_match(rows, masks, own, my_index())
    slots = to_column(match, slots_ref[...].astype(f32)).astype(jnp.int32)
    place = (lax.div(slots, cap) ^ my_seq) * cap + lax.rem(slots, cap)
    pick = (place == lax.broadcasted_iota(jnp.int32, (rows, table_ref.shape[0]), 1)).astype(bf16)
    teacher = jnp.dot(pick, table_ref[...], preferred_element_type=f32)
    teacher_ref[...] = teacher.astype(bf16)
    teacher_top = jnp.max(teacher, axis=1, keepdims=True)
    teacher_total = jnp.sum(jnp.exp(teacher - teacher_top), axis=1, keepdims=True)
    logits = jnp.zeros(logits_ref.shape, f32)
    for p in range(parts):
        block = slice(p * size, (p + 1) * size)
        features = jnp.concatenate([low_ref[:, block], high_ref[:, block]], axis=0)
        logits += jnp.dot(features, weight_ref[block, :], preferred_element_type=f32)
    logits_ref[...] = logits
    student_top = jnp.max(logits, axis=1, keepdims=True)
    shifted = jnp.exp(logits - student_top)
    student_total = jnp.sum(shifted, axis=1, keepdims=True)
    cross_sum = jnp.sum(shifted * (logits - teacher), axis=1, keepdims=True)
    nothing = jnp.zeros((1, rows), f32)
    pairs = [
        (to_row(match, student_top), to_row(match, teacher_top)),
        (to_row(match, student_total), to_row(match, teacher_total)),
        (to_row(match, cross_sum), nothing),
        (nothing, nothing),
    ]
    stats_ref[...] = jnp.concatenate([jnp.concatenate(p, axis=1) for p in pairs], axis=0)


def products_kernel(masks, own, logits_ref, teacher_ref, mine_ref, theirs_ref, weight_ref, keep_ref, send_ref):
    parts, size = split_evenly(weight_ref.shape[0], 256)
    logits = logits_ref[...]
    rows = logits.shape[0]
    half = rows // 2
    match = place_match(rows, masks, own, my_index())
    top, total, cross = merge(mine_ref[...], theirs_ref[...])
    center = to_column(match, cross[:, :rows] / total[:, :rows])
    shifted = jnp.exp(logits - to_column(match, top[:, :rows]))
    gaps = shifted * (logits - teacher_ref[...].astype(f32) - center)
    pieces = []
    for at in range(0, rows, own):
        pieces += [gaps[at : at + own], shifted[at : at + own]]
    left = jnp.concatenate(pieces, axis=0).astype(bf16)
    for p in range(parts):
        block = slice(p * size, (p + 1) * size)
        product = lax.dot_general(
            left, weight_ref[block, :], (((1,), (1,)), ((), ())), preferred_element_type=f32
        )
        keep_ref[:, block] = product[: 2 * half]
        send_ref[:, block] = product[2 * half :].astype(bf16)


def share_kernel(masks, own, keep_ref, arrived_ref, share_ref, held, sems):
    me = my_index()
    chips, length, columns = share_ref.shape
    length //= 4
    group = 16 // length
    copies = []
    for first in range(0, chips, group):
        rows = slice(first * length, (first + group) * length)
        total = keep_ref[rows, :] + arrived_ref[rows, :].astype(f32)
        for p in range(first, first + group):
            mine = total[(p - first) * length : (p - first + 1) * length]
            quarters = [mine[:, at : at + columns] for at in range(0, 4 * columns, columns)]
            held[p] = jnp.concatenate(quarters, axis=0).astype(bf16)
            copies.append(
                pltpu.make_async_copy(held.at[p], share_ref.at[partner(me, masks, p) >> 1], sems.at[p])
            )
            copies[-1].start()
    for copy in copies:
        copy.wait()


def terms_kernel(masks, own, mine_ref, theirs_ref, valid_ref, terms_ref, factors_ref):
    me = my_index()
    rows = valid_ref.shape[1]
    chips = factors_ref.shape[0]
    mine, theirs = mine_ref[...], theirs_ref[...]
    tops = jnp.maximum(mine[:, 0, :], theirs[:, 0, :])
    near, other = jnp.exp(mine[:, 0, :] - tops), jnp.exp(theirs[:, 0, :] - tops)
    totals = mine[:, 1, :] * near + theirs[:, 1, :] * other
    crosses = mine[:, 2, :] * near + theirs[:, 2, :] * other
    top = jnp.max(tops, axis=0, keepdims=True)
    scale = jnp.exp(tops - top)
    total = jnp.sum(totals * scale, axis=0, keepdims=True)
    cross = jnp.sum(crosses * scale, axis=0, keepdims=True)[:, :rows]
    lse = top + jnp.log(total)
    student_lse, teacher_lse = lse[:, :rows], lse[:, rows:]
    divergence = cross / total[:, :rows] - student_lse + teacher_lse
    row_weight = valid_ref[...].astype(f32)
    match = place_match(rows, masks, own, me)
    lane = lax.broadcasted_iota(jnp.int32, (rows, 128), 1)
    terms = to_column(match, row_weight)
    for at, values in enumerate((student_lse, teacher_lse, divergence)):
        terms = jnp.where(lane == at, to_column(match, values), terms)
    terms_ref[...] = terms
    scale = row_weight * jnp.exp(tops[:, :rows] - student_lse)
    offset = scale * (crosses[:, :rows] / totals[:, :rows] + (teacher_lse - student_lse - divergence))
    pick = lax.rem(lax.broadcasted_iota(jnp.int32, (8 * own, rows), 0), 2 * own)
    mine = lax.broadcasted_iota(jnp.int32, (8 * own, rows), 1) == me * own + lax.rem(pick, own)
    for p in range(chips):
        both = jnp.where(pick < own, scale[p : p + 1], offset[p : p + 1])
        column = jnp.sum(jnp.where(mine, both, 0.0), axis=1, keepdims=True)
        factors_ref[partner(me, near_first(masks), p) >> 1] = jnp.broadcast_to(column, factors_ref.shape[1:])


def head_kernel(low_ref, high_ref, logits_ref, teacher_ref, terms_ref, out_ref, held, sems):
    parts, size = split_evenly(out_ref.shape[0], 256)
    student_lse, teacher_lse = terms_ref[:, 0:1], terms_ref[:, 1:2]
    log_prob = logits_ref[...] - student_lse
    log_gap = log_prob - (teacher_ref[...].astype(f32) - teacher_lse)
    grad = (terms_ref[:, 3:4] * jnp.exp(log_prob) * (log_gap - terms_ref[:, 2:3])).astype(bf16)
    copies = []
    for p in range(parts):
        block = slice(p * size, (p + 1) * size)
        features = jnp.concatenate([low_ref[:, block], high_ref[:, block]], axis=0)
        held[block, :] = lax.dot_general(
            features, grad, (((0,), (0,)), ((), ())), preferred_element_type=f32
        ).astype(bf16)
        rows = pl.ds(p * size, size)
        copies.append(pltpu.make_async_copy(held.at[rows], out_ref.at[rows], sems.at[p]))
        copies[-1].start()
    for copy in copies:
        copy.wait()


def finish_kernel(hidden_ref, gain_ref, shares_ref, factors_ref, out_ref):
    own = hidden_ref.shape[0]
    widened = hidden_ref[...].astype(f32)
    inv_rms = lax.rsqrt(jnp.mean(widened * widened, axis=1, keepdims=True) + epsilon)
    normed = widened * inv_rms
    both = shares_ref[0].astype(f32) * factors_ref[0][:, 0:1]
    for p in range(1, shares_ref.shape[0]):
        both += shares_ref[p].astype(f32) * factors_ref[p][:, 0:1]
    sums = [both[at : at + own] + both[at + own : at + 2 * own] for at in range(0, 8 * own, 2 * own)]
    norm_grad = jnp.concatenate(sums, axis=1) * gain_ref[...]
    mean = jnp.mean(norm_grad * normed, axis=1, keepdims=True)
    out_ref[...] = (inv_rms * (norm_grad - normed * mean)).astype(bf16)


def shards(hidden, norm_gain, head_weight, teacher_logits, teacher_slot, valid_tokens):
    n_seq, n_row = lax.axis_size("seq"), lax.axis_size("row")
    chips = n_seq * n_row
    count = chips * 2
    own, depth = hidden.shape
    width = head_weight.shape[1]
    rows = own * count
    cap = teacher_logits.shape[0]
    columns = depth // 4
    gain = norm_gain[None]
    masks = [1 << b for b in reversed(range(count.bit_length() - 1))]
    seq_masks = [m for m in reversed(masks) if m >= n_row * 2]

    def swap(value, mask):
        return lax.ppermute(value, axes, [(i, i ^ mask) for i in range(count)])

    def sems(number):
        return pltpu.SemaphoreType.DMA((number,))

    (first,) = call(first_kernel, "first", [shape((8, 128), f32)], [], [], [fast], flops=10**10)
    (gathered,) = call(
        features_kernel,
        "features",
        [shape((own, depth), bf16)],
        [hidden, gain, first],
        [fast] * 3,
        [fast],
    )
    half_blocks = shape((n_seq // 2, cap, width), bf16)
    keep, send = call(
        teacher_kernel,
        "teacher_blocks",
        [half_blocks] * 2,
        [teacher_logits.transpose(1, 0, 2)],
        [fast],
        [fast] * 2,
        flops=10**10,
    )
    held = jnp.concatenate([keep, swap(send, seq_masks[0])], axis=1)
    behind = len(masks) - len(seq_masks)
    for step, mask in enumerate(masks[:-1]):
        arrived = swap(gathered, mask)
        bit = step - behind + 1
        if 1 <= bit < len(seq_masks):
            pairs = held.reshape((held.shape[0] // 2, 2) + held.shape[1:])
            held = jnp.concatenate([pairs[:, 0], swap(pairs[:, 1], seq_masks[bit])], axis=1)
        if step < len(masks) - 2:
            gathered = jnp.concatenate([gathered, arrived], axis=0)
    (gathered,) = call(
        join_kernel, "join", [shape((rows // 2, depth), bf16)], [gathered, arrived], [fast] * 2, [fast]
    )
    low, held = lax.optimization_barrier((gathered, held))
    high = swap(low, masks[-1])

    def with_masks(kernel, *more):
        return lambda *refs: kernel(masks, own, *more, *refs)

    logits, teacher, stats = call(
        with_masks(logits_kernel, cap),
        "logits",
        [shape((rows, width), f32), shape((rows, width), bf16), shape((4, 2 * rows), f32)],
        [low, high, head_weight, held[0], teacher_slot[None]],
        [fast] * 5,
        [fast] * 3,
        flops=2 * rows * depth * width,
    )
    keep, send = call(
        with_masks(products_kernel),
        "products",
        [shape((rows, depth), f32), shape((rows, depth), bf16)],
        [logits, teacher, stats, swap(stats, masks[-1]), head_weight],
        [fast] * 5,
        [fast] * 2,
        flops=4 * rows * depth * width,
    )
    def join(value, mask, *after):
        (joined,) = call(
            join_kernel,
            "join_statistics",
            [shape((2 * value.shape[0], 4, 2 * rows), f32)],
            [value, swap(value, mask), *after],
            [fast] * 2 + [far] * len(after),
            [fast],
            light=True,
        )
        return joined

    steps = near_first(masks)
    stats = join(stats[None], steps[0], send)
    stats, send = lax.optimization_barrier((stats, send))
    (share,) = call(
        with_masks(share_kernel),
        "share",
        [shape((chips, 8 * own, columns), bf16)],
        [keep, swap(send, masks[-1])],
        [fast] * 2,
        [far],
        [pltpu.VMEM((chips, 8 * own, columns), bf16), sems(chips)],
    )
    for step, mask in enumerate(steps[1:-1]):
        if step == 0:
            stats, share = lax.optimization_barrier((join(stats, mask, share), share))
        else:
            stats = join(stats, mask)
    other_stats = swap(stats, masks[-1])
    shares = lax.all_to_all(share, ("seq", "row"), split_axis=0, concat_axis=0, tiled=True)
    terms, factors = call(
        with_masks(terms_kernel),
        "terms",
        [shape((rows, 128), f32), shape((chips, 8 * own, 128), f32)],
        [stats, other_stats, valid_tokens[None]],
        [fast] * 3,
        [fast] * 2,
        light=True,
    )
    (grad_head,) = call(
        head_kernel,
        "grad_head",
        [shape(head_weight.shape, bf16)],
        [low, high, logits, teacher, terms],
        [fast] * 5,
        [far],
        [pltpu.VMEM((depth, width), bf16), sems(5)],
        light=True,
    )
    (grad_hidden,) = call(
        finish_kernel,
        "finish",
        [shape((own, depth), bf16)],
        [hidden, gain, shares, factors],
        [fast] * 4,
        [fast],
    )
    return (grad_hidden, grad_head)


def solution(mesh):
    n_seq, n_vocab = mesh.shape["seq"], mesh.shape["vocab"]
    finer = jax.sharding.Mesh(mesh.devices.reshape(n_seq, n_vocab // 2, 2), axes)
    placed = (
        P(axes, None),
        P(),
        P(None, axes),
        P("seq", None, ("row", "core")),
        P(),
        P(),
    )
    return jax.shard_map(
        shards,
        mesh=finer,
        in_specs=placed,
        out_specs=(P(axes, None), P(None, axes)),
        check_vma=False,
    )
```

```python
import math

import jax
import jax.numpy as jnp
from jax import lax
from jax.experimental import pallas as pl
from jax.experimental.pallas import tpu as pltpu
from jax.sharding import PartitionSpec as P

epsilon = 1e-06
axes = ("seq", "row", "core")
fast, far = pltpu.VMEM, pl.ANY
shape = jax.ShapeDtypeStruct
f32, bf16 = jnp.float32, jnp.bfloat16


def call(kernel, name, out_shape, inputs, spaces, out_spaces, scratch=(), flops=0, light=False):
    def size(leaf):
        return leaf.size * leaf.dtype.itemsize

    near = [x for x, s in zip(inputs, spaces) if s == fast]
    near += [x for x, s in zip(out_shape, out_spaces) if s == fast]
    held = sum(x.dtype.itemsize * math.prod(x.shape) for x in scratch if x.memory_space == fast)
    return pl.pallas_call(
        kernel,
        out_shape=list(out_shape),
        in_specs=[pl.BlockSpec(memory_space=s) for s in spaces],
        out_specs=[pl.BlockSpec(memory_space=s) for s in out_spaces],
        scratch_shapes=list(scratch),
        compiler_params=pltpu.CompilerParams(
            vmem_limit_bytes=2 * sum(map(size, near)) + held + (8 << 20)
        ),
        cost_estimate=pl.CostEstimate(
            flops=flops,
            bytes_accessed=0 if light else sum(map(size, list(inputs) + list(out_shape))),
            transcendentals=0,
        ),
        name=name,
    )(*inputs)


def split_evenly(total, unit):
    parts = max(p for p in (1, 2, 4, 5) if total % (p * unit) == 0)
    return parts, total // parts


def my_index():
    return (lax.axis_index("seq") * lax.axis_size("row") + lax.axis_index("row")) * 2 + lax.axis_index("core")


def partner(me, masks, place):
    for bit, mask in enumerate(masks):
        if place >> bit & 1:
            me = me ^ mask
    return me


def near_first(masks):
    return [masks[1], masks[0], *masks[2:]] if len(masks) > 2 else masks


def place_match(rows, masks, own, me):
    place = lax.broadcasted_iota(jnp.int32, (rows, rows), 0)
    block, inner = lax.div(place, own), lax.rem(place, own)
    device = jnp.full((rows, rows), me, jnp.int32)
    for bit, mask in enumerate(masks):
        device = device ^ (((block >> bit) & 1) * mask)
    return device * own + inner == lax.broadcasted_iota(jnp.int32, (rows, rows), 1)


def to_column(match, row_values):
    return jnp.sum(jnp.where(match, row_values, 0.0), axis=1, keepdims=True)


def to_row(match, column):
    return jnp.sum(jnp.where(match, column, 0.0), axis=0, keepdims=True)


def merge(first, second):
    top = jnp.maximum(first[0:1], second[0:1])
    near, far_off = jnp.exp(first[0:1] - top), jnp.exp(second[0:1] - top)
    return top, first[1:2] * near + second[1:2] * far_off, first[2:3] * near + second[2:3] * far_off


def first_kernel(out_ref):
    out_ref[...] = jnp.zeros_like(out_ref)


def features_kernel(hidden_ref, gain_ref, first_ref, features_ref):
    widened = hidden_ref[...].astype(f32)
    inv_rms = lax.rsqrt(jnp.mean(widened * widened, axis=1, keepdims=True) + epsilon)
    features_ref[...] = (widened * inv_rms * gain_ref[...]).astype(bf16)


def teacher_kernel(blocks_ref, keep_ref, send_ref):
    my_seq = lax.axis_index("seq")
    for k in range(keep_ref.shape[0]):
        keep_ref[k] = blocks_ref[my_seq ^ (2 * k)]
        send_ref[k] = blocks_ref[my_seq ^ (2 * k + 1)]


def join_kernel(first_ref, second_ref, *rest):
    out_ref = rest[-1]
    length = first_ref.shape[0]
    out_ref[:length] = first_ref[...]
    out_ref[length:] = second_ref[...]


def logits_kernel(masks, own, cap, low_ref, high_ref, weight_ref, table_ref, slots_ref, logits_ref, teacher_ref, stats_ref):
    my_seq = lax.axis_index("seq")
    rows = logits_ref.shape[0]
    parts, size = split_evenly(weight_ref.shape[0], 256)
    match = place_match(rows, masks, own, my_index())
    slots = to_column(match, slots_ref[...].astype(f32)).astype(jnp.int32)
    place = (lax.div(slots, cap) ^ my_seq) * cap + lax.rem(slots, cap)
    pick = (place == lax.broadcasted_iota(jnp.int32, (rows, table_ref.shape[0]), 1)).astype(bf16)
    teacher = jnp.dot(pick, table_ref[...], preferred_element_type=f32)
    teacher_ref[...] = teacher.astype(bf16)
    teacher_top = jnp.max(teacher, axis=1, keepdims=True)
    teacher_total = jnp.sum(jnp.exp(teacher - teacher_top), axis=1, keepdims=True)
    logits = jnp.zeros(logits_ref.shape, f32)
    for p in range(parts):
        block = slice(p * size, (p + 1) * size)
        features = jnp.concatenate([low_ref[:, block], high_ref[:, block]], axis=0)
        logits += jnp.dot(features, weight_ref[block, :], preferred_element_type=f32)
    logits_ref[...] = logits
    student_top = jnp.max(logits, axis=1, keepdims=True)
    shifted = jnp.exp(logits - student_top)
    student_total = jnp.sum(shifted, axis=1, keepdims=True)
    cross_sum = jnp.sum(shifted * (logits - teacher), axis=1, keepdims=True)
    nothing = jnp.zeros((1, rows), f32)
    pairs = [
        (to_row(match, student_top), to_row(match, teacher_top)),
        (to_row(match, student_total), to_row(match, teacher_total)),
        (to_row(match, cross_sum), nothing),
        (nothing, nothing),
    ]
    stats_ref[...] = jnp.concatenate([jnp.concatenate(p, axis=1) for p in pairs], axis=0)


def products_kernel(masks, own, logits_ref, teacher_ref, mine_ref, theirs_ref, weight_ref, keep_ref, send_ref):
    parts, size = split_evenly(weight_ref.shape[0], 256)
    logits = logits_ref[...]
    rows = logits.shape[0]
    half = rows // 2
    match = place_match(rows, masks, own, my_index())
    top, total, cross = merge(mine_ref[...], theirs_ref[...])
    center = to_column(match, cross[:, :rows] / total[:, :rows])
    shifted = jnp.exp(logits - to_column(match, top[:, :rows]))
    gaps = shifted * (logits - teacher_ref[...].astype(f32) - center)
    pieces = []
    for at in range(0, rows, own):
        pieces += [gaps[at : at + own], shifted[at : at + own]]
    left = jnp.concatenate(pieces, axis=0).astype(bf16)
    for p in range(parts):
        block = slice(p * size, (p + 1) * size)
        product = lax.dot_general(
            left, weight_ref[block, :], (((1,), (1,)), ((), ())), preferred_element_type=f32
        )
        keep_ref[:, block] = product[: 2 * half]
        send_ref[:, block] = product[2 * half :].astype(bf16)


def share_kernel(masks, own, keep_ref, arrived_ref, share_ref, held, sems):
    me = my_index()
    chips, length, columns = share_ref.shape
    length //= 4
    group = 16 // length
    copies = []
    for first in range(0, chips, group):
        rows = slice(first * length, (first + group) * length)
        total = keep_ref[rows, :] + arrived_ref[rows, :].astype(f32)
        for p in range(first, first + group):
            mine = total[(p - first) * length : (p - first + 1) * length]
            quarters = [mine[:, at : at + columns] for at in range(0, 4 * columns, columns)]
            held[p] = jnp.concatenate(quarters, axis=0).astype(bf16)
            copies.append(
                pltpu.make_async_copy(held.at[p], share_ref.at[partner(me, masks, p) >> 1], sems.at[p])
            )
            copies[-1].start()
    for copy in copies:
        copy.wait()


def terms_kernel(masks, own, mine_ref, theirs_ref, valid_ref, terms_ref, factors_ref):
    me = my_index()
    rows = valid_ref.shape[1]
    chips = factors_ref.shape[0]
    mine, theirs = mine_ref[...], theirs_ref[...]
    tops = jnp.maximum(mine[:, 0, :], theirs[:, 0, :])
    near, other = jnp.exp(mine[:, 0, :] - tops), jnp.exp(theirs[:, 0, :] - tops)
    totals = mine[:, 1, :] * near + theirs[:, 1, :] * other
    crosses = mine[:, 2, :] * near + theirs[:, 2, :] * other
    top = jnp.max(tops, axis=0, keepdims=True)
    scale = jnp.exp(tops - top)
    total = jnp.sum(totals * scale, axis=0, keepdims=True)
    cross = jnp.sum(crosses * scale, axis=0, keepdims=True)[:, :rows]
    lse = top + jnp.log(total)
    student_lse, teacher_lse = lse[:, :rows], lse[:, rows:]
    divergence = cross / total[:, :rows] - student_lse + teacher_lse
    row_weight = valid_ref[...].astype(f32)
    match = place_match(rows, masks, own, me)
    lane = lax.broadcasted_iota(jnp.int32, (rows, 128), 1)
    terms = to_column(match, row_weight)
    for at, values in enumerate((student_lse, teacher_lse, divergence)):
        terms = jnp.where(lane == at, to_column(match, values), terms)
    terms_ref[...] = terms
    scale = row_weight * jnp.exp(tops[:, :rows] - student_lse)
    offset = scale * (crosses[:, :rows] / totals[:, :rows] + (teacher_lse - student_lse - divergence))
    pick = lax.rem(lax.broadcasted_iota(jnp.int32, (8 * own, rows), 0), 2 * own)
    mine = lax.broadcasted_iota(jnp.int32, (8 * own, rows), 1) == me * own + lax.rem(pick, own)
    for p in range(chips):
        both = jnp.where(pick < own, scale[p : p + 1], offset[p : p + 1])
        column = jnp.sum(jnp.where(mine, both, 0.0), axis=1, keepdims=True)
        factors_ref[partner(me, masks, p) >> 1] = jnp.broadcast_to(column, factors_ref.shape[1:])


def head_kernel(low_ref, high_ref, logits_ref, teacher_ref, terms_ref, out_ref, held, sems):
    parts, size = split_evenly(out_ref.shape[0], 256)
    student_lse, teacher_lse = terms_ref[:, 0:1], terms_ref[:, 1:2]
    log_prob = logits_ref[...] - student_lse
    log_gap = log_prob - (teacher_ref[...].astype(f32) - teacher_lse)
    grad = (terms_ref[:, 3:4] * jnp.exp(log_prob) * (log_gap - terms_ref[:, 2:3])).astype(bf16)
    copies = []
    for p in range(parts):
        block = slice(p * size, (p + 1) * size)
        features = jnp.concatenate([low_ref[:, block], high_ref[:, block]], axis=0)
        held[block, :] = lax.dot_general(
            features, grad, (((0,), (0,)), ((), ())), preferred_element_type=f32
        ).astype(bf16)
        rows = pl.ds(p * size, size)
        copies.append(pltpu.make_async_copy(held.at[rows], out_ref.at[rows], sems.at[p]))
        copies[-1].start()
    for copy in copies:
        copy.wait()


def finish_kernel(hidden_ref, gain_ref, shares_ref, factors_ref, out_ref):
    own = hidden_ref.shape[0]
    widened = hidden_ref[...].astype(f32)
    inv_rms = lax.rsqrt(jnp.mean(widened * widened, axis=1, keepdims=True) + epsilon)
    normed = widened * inv_rms
    both = shares_ref[0].astype(f32) * factors_ref[0][:, 0:1]
    for p in range(1, shares_ref.shape[0]):
        both += shares_ref[p].astype(f32) * factors_ref[p][:, 0:1]
    sums = [both[at : at + own] + both[at + own : at + 2 * own] for at in range(0, 8 * own, 2 * own)]
    norm_grad = jnp.concatenate(sums, axis=1) * gain_ref[...]
    mean = jnp.mean(norm_grad * normed, axis=1, keepdims=True)
    out_ref[...] = (inv_rms * (norm_grad - normed * mean)).astype(bf16)


def shards(hidden, norm_gain, head_weight, teacher_logits, teacher_slot, valid_tokens):
    n_seq, n_row = lax.axis_size("seq"), lax.axis_size("row")
    chips = n_seq * n_row
    count = chips * 2
    own, depth = hidden.shape
    width = head_weight.shape[1]
    rows = own * count
    cap = teacher_logits.shape[0]
    columns = depth // 4
    gain = norm_gain[None]
    masks = near_first([1 << b for b in reversed(range(count.bit_length() - 1))])
    seq_masks = sorted(m for m in masks if m >= n_row * 2)

    def swap(value, mask):
        return lax.ppermute(value, axes, [(i, i ^ mask) for i in range(count)])

    def sems(number):
        return pltpu.SemaphoreType.DMA((number,))

    (first,) = call(first_kernel, "first", [shape((8, 128), f32)], [], [], [fast], flops=10**10)
    (gathered,) = call(
        features_kernel,
        "features",
        [shape((own, depth), bf16)],
        [hidden, gain, first],
        [fast] * 3,
        [fast],
    )
    half_blocks = shape((n_seq // 2, cap, width), bf16)
    keep, send = call(
        teacher_kernel,
        "teacher_blocks",
        [half_blocks] * 2,
        [teacher_logits.transpose(1, 0, 2)],
        [fast],
        [fast] * 2,
        flops=10**10,
    )
    held = jnp.concatenate([keep, swap(send, seq_masks[0])], axis=1)
    behind = len(masks) - len(seq_masks)
    for step, mask in enumerate(masks[:-1]):
        arrived = swap(gathered, mask)
        bit = step - behind + 1
        if 1 <= bit < len(seq_masks):
            pairs = held.reshape((held.shape[0] // 2, 2) + held.shape[1:])
            held = jnp.concatenate([pairs[:, 0], swap(pairs[:, 1], seq_masks[bit])], axis=1)
        if step < len(masks) - 2:
            gathered = jnp.concatenate([gathered, arrived], axis=0)
    (gathered,) = call(
        join_kernel, "join", [shape((rows // 2, depth), bf16)], [gathered, arrived], [fast] * 2, [fast]
    )
    low, held = lax.optimization_barrier((gathered, held))
    high = swap(low, masks[-1])

    def with_masks(kernel, *more):
        return lambda *refs: kernel(masks, own, *more, *refs)

    logits, teacher, stats = call(
        with_masks(logits_kernel, cap),
        "logits",
        [shape((rows, width), f32), shape((rows, width), bf16), shape((4, 2 * rows), f32)],
        [low, high, head_weight, held[0], teacher_slot[None]],
        [fast] * 5,
        [fast] * 3,
        flops=2 * rows * depth * width,
    )
    keep, send = call(
        with_masks(products_kernel),
        "products",
        [shape((rows, depth), f32), shape((rows, depth), bf16)],
        [logits, teacher, stats, swap(stats, masks[-1]), head_weight],
        [fast] * 5,
        [fast] * 2,
        flops=4 * rows * depth * width,
    )
    def join(value, mask, *after):
        (joined,) = call(
            join_kernel,
            "join_statistics",
            [shape((2 * value.shape[0], 4, 2 * rows), f32)],
            [value, swap(value, mask), *after],
            [fast] * 2 + [far] * len(after),
            [fast],
            light=True,
        )
        return joined

    steps = masks
    stats = join(stats[None], steps[0], send)
    stats, send = lax.optimization_barrier((stats, send))
    (share,) = call(
        with_masks(share_kernel),
        "share",
        [shape((chips, 8 * own, columns), bf16)],
        [keep, swap(send, masks[-1])],
        [fast] * 2,
        [far],
        [pltpu.VMEM((chips, 8 * own, columns), bf16), sems(chips)],
    )
    for step, mask in enumerate(steps[1:-1]):
        if step == 0:
            stats, share = lax.optimization_barrier((join(stats, mask, share), share))
        else:
            stats = join(stats, mask)
    other_stats = swap(stats, masks[-1])
    shares = lax.all_to_all(share, ("seq", "row"), split_axis=0, concat_axis=0, tiled=True)
    terms, factors = call(
        with_masks(terms_kernel),
        "terms",
        [shape((rows, 128), f32), shape((chips, 8 * own, 128), f32)],
        [stats, other_stats, valid_tokens[None]],
        [fast] * 3,
        [fast] * 2,
        light=True,
    )
    (grad_head,) = call(
        head_kernel,
        "grad_head",
        [shape(head_weight.shape, bf16)],
        [low, high, logits, teacher, terms],
        [fast] * 5,
        [far],
        [pltpu.VMEM((depth, width), bf16), sems(5)],
        light=True,
    )
    (grad_hidden,) = call(
        finish_kernel,
        "finish",
        [shape((own, depth), bf16)],
        [hidden, gain, shares, factors],
        [fast] * 4,
        [fast],
    )
    return (grad_hidden, grad_head)


def solution(mesh):
    n_seq, n_vocab = mesh.shape["seq"], mesh.shape["vocab"]
    finer = jax.sharding.Mesh(mesh.devices.reshape(n_seq, n_vocab // 2, 2), axes)
    placed = (
        P(axes, None),
        P(),
        P(None, axes),
        P("seq", None, ("row", "core")),
        P(),
        P(),
    )
    return jax.shard_map(
        shards,
        mesh=finer,
        in_specs=placed,
        out_specs=(P(axes, None), P(None, axes)),
        check_vma=False,
    )
```
